32 devices in a mesh: dp: 4 (over y, x), seq: 8 (over z, core).
Axes of the slice: x: 2, y: 2, z: 4, core: 2. Of those that a mesh axis runs over, the one named last changes fastest.
Arguments:
- block_input: bfloat16 [2, 4, 1024, 576], P(None, 'dp', 'seq'), may hold values from -6 to 6
- out_grad: bfloat16 [2, 4, 1024, 576], P(None, 'dp', 'seq'), may hold values from -6 to 6
- doc_lengths: int32 [2, 4, 6], P(None, 'dp'), may hold values from 200 to 1000, as said below
- attention_weights: float32 [884736], P(('dp', 'seq'))
- feedforward_weights: float32 [2654208], P(('dp', 'seq'))
- norm_gains: float32 [2, 576], replicated, may hold values from 0.5 to 1.5
- attention_moment: float32 [884736], P(('dp', 'seq'))
- attention_square: float32 [884736], P(('dp', 'seq')), as said below
- feedforward_moment: float32 [2654208], P(('dp', 'seq'))
- feedforward_square: float32 [2654208], P(('dp', 'seq')), as said below
- gain_moment: float32 [2, 576], replicated, may hold values from -64 to 64
- gain_square: float32 [2, 576], replicated, may hold values from 212.992 to 3440.64
Outputs:
- block_output: bfloat16 [2, 4, 1024, 576], P(None, 'dp', 'seq')
- input_grad: float32 [2, 4, 1024, 576], P(None, 'dp', 'seq')
- new_attention: float32 [884736], P(('dp', 'seq'))
- new_attention_moment: float32 [884736], P(('dp', 'seq'))
- new_attention_square: float32 [884736], P(('dp', 'seq'))
- new_feedforward: float32 [2654208], P(('dp', 'seq'))
- new_feedforward_moment: float32 [2654208], P(('dp', 'seq'))
- new_feedforward_square: float32 [2654208], P(('dp', 'seq'))
- new_gains: float32 [2, 576], replicated
- new_gain_moment: float32 [2, 576], replicated
- new_gain_square: float32 [2, 576], replicated
The draws below stay inside these ranges and needn't reach their ends.
Inputs may be any that keep to these rules, and one draw needn't show every extreme that they name: `doc_lengths`: documents lie end to end from each sequence's first token in the given order; those starting at or after 1024 are unused and the last used one is cut at 1024. The first or the second document of every sequence has exactly 1000 tokens. `attention_square`: positive. `feedforward_square`: positive.
All inputs are finite; a program needn't handle non-finite values.
Results may differ from the reference program's by a relative error of at most 0.014.
Values may be sent and summed in bfloat16 or wider, within the bound.
No kernel may reach another device: no remote copies, remote signals or barrier semaphores. Data moves between devices by JAX's collectives and lax.ppermute only.
A program may use at most 128 MiB of HBM per device.

```python
import math
import jax
import jax.numpy as jnp
from jax import lax

D = 576
QUERY_HEADS = 9
KEY_VALUE_HEADS = 3
HEAD_SIZE = 64
FF = 1536
MICRO = 2
DOC_MIN = 200
DOC_MAX = 1000
STEP = 10
PACKED_LENGTH = 1024
BATCH = 4
DOCS = 6
TOKENS = 8192
QKV_WIDTH = 960
OUT_FAN = 14
PA = 884736
PM = 2654208


def region_scale(entries, boundary, first_scale, second_scale):
    flat_place = jnp.arange(entries, dtype=jnp.int32)
    return jnp.where(flat_place < boundary, jnp.float32(first_scale), jnp.float32(second_scale))


def attention_grad_sizes():
    root_tokens = math.sqrt(TOKENS)
    inner_size = 7.6 * math.sqrt(D / OUT_FAN) / math.sqrt(DOC_MAX) * root_tokens
    outer_size = 5.4 / math.sqrt(DOC_MAX) * root_tokens
    return (inner_size, outer_size)


def feedforward_grad_sizes():
    root_tokens = math.sqrt(TOKENS)
    return (0.35 * root_tokens, 0.6 * root_tokens)


def moment_draw(key, entries, boundary, grad_sizes):
    normal_base = jax.random.truncated_normal(key, -4.0, 4.0, (entries,), jnp.float32)
    return normal_base * region_scale(entries, boundary, grad_sizes[0] / 9.0, grad_sizes[1] / 9.0)


def square_draw(key, entries, boundary, grad_sizes):
    spread = jnp.exp(jax.random.uniform(key, (entries,), jnp.float32, math.log(0.5), math.log(8.0)))
    return spread * region_scale(entries, boundary, grad_sizes[0] ** 2 / 19.0, grad_sizes[1] ** 2 / 19.0)


def draw_doc_lengths(key, part):
    key = jax.random.fold_in(key, 3)
    length_key, which_key = jax.random.split(key)
    lengths = jax.random.randint(length_key, (MICRO, BATCH, DOCS), DOC_MIN, DOC_MAX + 1, jnp.int32)
    longest = jax.random.randint(which_key, (MICRO, BATCH, 1), 0, 2, jnp.int32)
    doc_slot = jnp.arange(DOCS, dtype=jnp.int32)[None, None, :]
    return jnp.where(doc_slot == longest, DOC_MAX, lengths).astype(jnp.int32)


def draw_attention_weights(key, part):
    key = jax.random.fold_in(key, 11)
    normal_base = jax.random.truncated_normal(key, -4.0, 4.0, (PA,), jnp.float32)
    return normal_base * region_scale(PA, D * QKV_WIDTH, D ** (-0.5), OUT_FAN ** (-0.5))


def draw_feedforward_weights(key, part):
    key = jax.random.fold_in(key, 13)
    normal_base = jax.random.truncated_normal(key, -4.0, 4.0, (PM,), jnp.float32)
    return normal_base * region_scale(PM, 2 * D * FF, D ** (-0.5), FF ** (-0.5))


def draw_attention_moment(key, part):
    key = jax.random.fold_in(key, 17)
    return moment_draw(key, PA, D * QKV_WIDTH, attention_grad_sizes())


def draw_attention_square(key, part):
    key = jax.random.fold_in(key, 19)
    return square_draw(key, PA, D * QKV_WIDTH, attention_grad_sizes())


def draw_feedforward_moment(key, part):
    key = jax.random.fold_in(key, 23)
    return moment_draw(key, PM, 2 * D * FF, feedforward_grad_sizes())


def draw_feedforward_square(key, part):
    key = jax.random.fold_in(key, 29)
    return square_draw(key, PM, 2 * D * FF, feedforward_grad_sizes())


def block_scale(key, extent, cuts, least, top_value):
    level, own = 1.0, jax.random.fold_in(key, 6)
    for dim, parts in cuts:
        heights = jnp.exp(jax.random.uniform(jax.random.fold_in(own, dim), (parts,), jnp.float32, least / len(cuts), top_value / len(cuts)))
        level = level * jnp.repeat(heights, extent[dim] // parts).reshape([-1 if axis == dim else 1 for axis in range(len(extent))])
    return level


def gaussian(own_key, dims, scale, reach, cuts=(), held_as=jnp.bfloat16):
    result = jax.random.normal(own_key, dims, jnp.float32) * scale
    if len(cuts) > 0:
        result = block_scale(own_key, dims, cuts, -0.22, 0.18) * result
    return jnp.clip(result, min=-reach, max=reach).astype(held_as)


def setup_inputs(seed: int = 0) -> dict:
    key_list = jax.random.split(jax.random.key(seed), 13)
    block_input = gaussian(key_list[0], (MICRO, BATCH, PACKED_LENGTH, D), 1.0, 6.0, ((1, 4), (2, 8)))
    out_grad = gaussian(key_list[1], (MICRO, BATCH, PACKED_LENGTH, D), 1.0, 6.0, ((1, 4), (2, 8)))
    doc_lengths = draw_doc_lengths(jax.random.fold_in(key_list[12], 71), 0)
    attention_weights = draw_attention_weights(jax.random.fold_in(key_list[12], 71), 0)
    feedforward_weights = draw_feedforward_weights(jax.random.fold_in(key_list[12], 71), 0)
    norm_gains = jnp.clip(1.0 + 0.1 * jax.random.normal(key_list[5], (2, D), jnp.float32), 0.5, 1.5)
    attention_moment = draw_attention_moment(jax.random.fold_in(key_list[12], 71), 0)
    attention_square = draw_attention_square(jax.random.fold_in(key_list[12], 71), 0)
    feedforward_moment = draw_feedforward_moment(jax.random.fold_in(key_list[12], 71), 0)
    feedforward_square = draw_feedforward_square(jax.random.fold_in(key_list[12], 71), 0)
    gain_moment = gaussian(key_list[10], (2, D), (0.111 * TOKENS ** 0.5), 64.0, (), jnp.float32)
    gain_square = jnp.clip(jnp.exp(jax.random.uniform(key_list[11], (2, D), jnp.float32, math.log(212.992), math.log(3440.64))), 212.992, 3440.64)
    return {"block_input": block_input, "out_grad": out_grad, "doc_lengths": doc_lengths, "attention_weights": attention_weights, "feedforward_weights": feedforward_weights, "norm_gains": norm_gains, "attention_moment": attention_moment, "attention_square": attention_square, "feedforward_moment": feedforward_moment, "feedforward_square": feedforward_square, "gain_moment": gain_moment, "gain_square": gain_square}


NORM_EPSILON = 1e-05
THETA = 100000.0
BETA_ONE = 0.9
BETA_TWO = 0.95
ADAM_EPSILON = 1e-08
MATRIX_DECAY = 0.1
RATE_FACTOR = 1.5
GAIN_RATE = 0.2

@jax.custom_vjp
def reduced_precision(v):
    return lax.optimization_barrier(v.astype(jnp.bfloat16)).astype(jnp.float32)

@jax.custom_vjp
def reduced_backward(v):
    return v

def low_keep(v):
    return (reduced_precision(v), None)

def low_pass(kept, grad):
    return (grad,)

def back_keep(v):
    return (v, None)

def back_low(kept, grad):
    return (reduced_precision(grad),)
reduced_precision.defvjp(low_keep, low_pass)
reduced_backward.defvjp(back_keep, back_low)

def highest(left, right):
    return jnp.dot(left, right, precision=lax.Precision.HIGHEST)

def rope_tables(position):
    half_width = HEAD_SIZE // 2
    inverse = THETA ** (-(jnp.arange(half_width, dtype=jnp.float32) * 2.0) / HEAD_SIZE)
    angles = position.astype(jnp.float32)[:, None] * inverse[None, :]
    return (jnp.cos(angles)[:, None, :], jnp.sin(angles)[:, None, :])

def apply_rotary(value_rows, cosine_table, sine_lookup):
    half_width = HEAD_SIZE // 2
    first_half = value_rows[..., :half_width]
    second_half = value_rows[..., half_width:]
    return jnp.concatenate([first_half * cosine_table - second_half * sine_lookup, second_half * cosine_table + first_half * sine_lookup], -1)

def rms_norm(inputs, gain_row):
    inverse_rms = lax.rsqrt(lax.optimization_barrier(jnp.mean(inputs * inputs, axis=-1, keepdims=True)) + NORM_EPSILON)
    return inputs * inverse_rms * gain_row

def attention(query_matrix, key_rows, value_rows, first_index):
    block_rows = min(512, PACKED_LENGTH)
    backward_extent = DOC_MAX
    key_rows_padded = jnp.concatenate([jnp.zeros((backward_extent, KEY_VALUE_HEADS, HEAD_SIZE), jnp.float32), key_rows], 0)
    value_rows_padded = jnp.concatenate([jnp.zeros((backward_extent, KEY_VALUE_HEADS, HEAD_SIZE), jnp.float32), value_rows], 0)

    def one_block(start):
        query_rows = lax.dynamic_slice_in_dim(query_matrix, start, block_rows, 0)
        rows_first = lax.dynamic_slice_in_dim(first_index, start, block_rows, 0)
        near_keys = lax.dynamic_slice_in_dim(key_rows_padded, start, backward_extent + block_rows, 0)
        near_values = lax.dynamic_slice_in_dim(value_rows_padded, start, backward_extent + block_rows, 0)
        key_index = start - backward_extent + jnp.arange(backward_extent + block_rows, dtype=jnp.int32)
        query_index = start + jnp.arange(block_rows, dtype=jnp.int32)
        scores = jnp.einsum('thgd,khd->hgtk', query_rows, near_keys, precision=lax.Precision.HIGHEST) * HEAD_SIZE ** (-0.5)
        scores = reduced_backward(scores)
        allowed = (key_index[None, :] >= rows_first[:, None]) & (key_index[None, :] <= query_index[:, None])
        scores = jnp.where(allowed[None, None], scores, -jnp.inf)
        probability = reduced_precision(jax.nn.softmax(scores, axis=-1))
        return jnp.einsum('hgtk,khd->thgd', probability, near_values, precision=lax.Precision.HIGHEST)
    block_starts = jnp.arange(PACKED_LENGTH // block_rows, dtype=jnp.int32) * block_rows
    return lax.map(jax.checkpoint(one_block), block_starts).reshape(PACKED_LENGTH, QUERY_HEADS * HEAD_SIZE)

def layer_forward(attention_part, feedforward_part, gains_part, sequence, lengths):
    attention_low = reduced_precision(attention_part)
    feedforward_low = reduced_precision(feedforward_part)
    split_one = D * QKV_WIDTH
    w_project = attention_low[:split_one].reshape(D, QKV_WIDTH)
    w_output = attention_low[split_one:].reshape(QUERY_HEADS * HEAD_SIZE, D)
    split_two = 2 * D * FF
    w_gate_up = feedforward_low[:split_two].reshape(D, 2 * FF)
    w_down = feedforward_low[split_two:].reshape(FF, D)
    token_index = jnp.arange(PACKED_LENGTH, dtype=jnp.int32)
    doc_ends = jnp.cumsum(lengths).astype(jnp.int32)
    starts = (doc_ends - lengths).astype(jnp.int32)
    first_index = lax.optimization_barrier(jnp.max(jnp.where(starts[None, :] <= token_index[:, None], starts[None, :], 0), axis=1)).astype(jnp.int32)
    cosine_table, sine_lookup = rope_tables(token_index - first_index)
    normed_one = reduced_precision(rms_norm(sequence, gains_part[0]))
    projection_output = highest(normed_one, w_project)
    query_matrix = reduced_precision(apply_rotary(reduced_backward(projection_output[:, :QUERY_HEADS * HEAD_SIZE]).reshape(PACKED_LENGTH, QUERY_HEADS, HEAD_SIZE), cosine_table, sine_lookup))
    query_matrix = query_matrix.reshape(PACKED_LENGTH, KEY_VALUE_HEADS, QUERY_HEADS // KEY_VALUE_HEADS, HEAD_SIZE)
    rotated_key_rows = reduced_precision(apply_rotary(reduced_backward(projection_output[:, QUERY_HEADS * HEAD_SIZE:(QUERY_HEADS + KEY_VALUE_HEADS) * HEAD_SIZE]).reshape(PACKED_LENGTH, KEY_VALUE_HEADS, HEAD_SIZE), cosine_table, sine_lookup))
    value_rows = reduced_precision(reduced_backward(projection_output[:, (QUERY_HEADS + KEY_VALUE_HEADS) * HEAD_SIZE:])).reshape(PACKED_LENGTH, KEY_VALUE_HEADS, HEAD_SIZE)
    mixed = reduced_precision(reduced_backward(attention(query_matrix, rotated_key_rows, value_rows, first_index)))
    residual = sequence + reduced_backward(highest(mixed, w_output))
    normed_two = reduced_precision(rms_norm(residual, gains_part[1]))
    gate_up = highest(normed_two, w_gate_up)
    gate_value = reduced_backward(gate_up[:, :FF])
    up_part = reduced_backward(gate_up[:, FF:])
    hidden = reduced_precision(jax.nn.silu(gate_value) * up_part)
    return residual + reduced_backward(highest(hidden, w_down))

def adam_update(weights, moment, square, grad, rate, decay):
    new_moment = BETA_ONE * moment + (1.0 - BETA_ONE) * grad
    new_square = BETA_TWO * square + (1.0 - BETA_TWO) * grad * grad
    mean_hat = new_moment / (1.0 - BETA_ONE ** STEP)
    square_hat = new_square / (1.0 - BETA_TWO ** STEP)
    new_weights = weights - rate * (mean_hat / (jnp.sqrt(square_hat) + ADAM_EPSILON) + decay * weights)
    return (new_weights, new_moment, new_square)

def reference(block_input, out_grad, doc_lengths, attention_weights, feedforward_weights, norm_gains, attention_moment, attention_square, feedforward_moment, feedforward_square, gain_moment, gain_square):
    sequence_count = MICRO * BATCH
    inputs = block_input.astype(jnp.float32).reshape(sequence_count, PACKED_LENGTH, D)
    cotangents = out_grad.astype(jnp.float32).reshape(sequence_count, PACKED_LENGTH, D)
    all_lengths = doc_lengths.reshape(sequence_count, DOCS)

    def per_sequence(totals, scan_item):
        sequence, cotangent, lengths = scan_item

        def forward(attention_part, feedforward_part, gains_part, sequence_part):
            return layer_forward(attention_part, feedforward_part, gains_part, sequence_part, lengths)
        output, pullback = jax.vjp(forward, attention_weights, feedforward_weights, norm_gains, sequence)
        grads = pullback(cotangent)
        new_totals = (totals[0] + grads[0], totals[1] + grads[1], totals[2] + grads[2])
        return (new_totals, (output.astype(jnp.bfloat16), grads[3]))
    zero_totals = (jnp.zeros((PA,), jnp.float32), jnp.zeros((PM,), jnp.float32), jnp.zeros((2, D), jnp.float32))
    totals, (outputs, input_grads) = lax.scan(per_sequence, zero_totals, (inputs, cotangents, all_lengths))
    attention_place = jnp.arange(PA, dtype=jnp.int32)
    attention_rate = jnp.where(attention_place < D * QKV_WIDTH, RATE_FACTOR * D ** (-0.5), RATE_FACTOR * OUT_FAN ** (-0.5))
    feedforward_place = jnp.arange(PM, dtype=jnp.int32)
    feedforward_rate = jnp.where(feedforward_place < 2 * D * FF, RATE_FACTOR * D ** (-0.5), RATE_FACTOR * FF ** (-0.5))
    new_attention, new_attention_moment, new_attention_square = adam_update(attention_weights, attention_moment, attention_square, totals[0], attention_rate, MATRIX_DECAY)
    new_feedforward, new_feedforward_moment, new_feedforward_square = adam_update(feedforward_weights, feedforward_moment, feedforward_square, totals[1], feedforward_rate, MATRIX_DECAY)
    new_gains, new_gain_moment, new_gain_square = adam_update(norm_gains, gain_moment, gain_square, totals[2], GAIN_RATE, 0.0)
    return (outputs.reshape(MICRO, BATCH, PACKED_LENGTH, D), input_grads.reshape(MICRO, BATCH, PACKED_LENGTH, D), new_attention, new_attention_moment, new_attention_square, new_feedforward, new_feedforward_moment, new_feedforward_square, new_gains, new_gain_moment, new_gain_square)
```

```python
import functools

import jax
import jax.numpy as jnp
from jax import lax
from jax.experimental import pallas as pl
from jax.experimental.pallas import tpu as pltpu
from jax.sharding import PartitionSpec as P

D = 576
QUERY_HEADS = 9
KEY_VALUE_HEADS = 3
GROUP = QUERY_HEADS // KEY_VALUE_HEADS
HEAD_SIZE = 64
FF = 1536
DEVICE_TOKENS = 128
MICRO = 2
DOC_MAX = 1000
STEP = 10
QKV_WIDTH = 960
QUERY_WIDTH = QUERY_HEADS * HEAD_SIZE
KV_WIDTH = KEY_VALUE_HEADS * HEAD_SIZE
OUT_FAN = 14
LANES = 128

NORM_EPSILON = 1e-05
THETA = 100000.0
BETA_ONE = 0.9
BETA_TWO = 0.95
ADAM_EPSILON = 1e-08
MATRIX_DECAY = 0.1
RATE_FACTOR = 1.5
GAIN_RATE = 0.2
SCALE = HEAD_SIZE ** (-0.5)
BF16 = jnp.bfloat16
F32 = jnp.float32


def is_power_of_two(count):
    return count & (count - 1) == 0


def exchange(value, axis, bit):
    count = lax.axis_size(axis)
    return lax.ppermute(value, axis, [(place, place ^ bit) for place in range(count)])


def gather_stages():
    seq, dp = lax.axis_size("seq"), lax.axis_size("dp")
    stages = []
    bit = seq // 2
    while bit > 1:
        stages.append(("seq", bit, bit))
        bit //= 2
    bit = dp // 2
    while bit >= 1:
        stages.append(("dp", bit, bit * seq))
        bit //= 2
    if seq > 1:
        stages.append(("seq", 1, 1))
    return stages


def block_order(stages):
    order = [0]
    for unused_axis, unused_bit, flat_bit in stages:
        order = order + [place ^ flat_bit for place in order]
    return order


def doubled(block, stages):
    for axis, bit, unused_flat in stages:
        block = jnp.concatenate([block, exchange(block, axis, bit)], 0)
    return block


def halved(blocks, stages):
    for axis, bit, unused_flat in reversed(stages):
        half = blocks.shape[0] // 2
        received = exchange(blocks[half:], axis, bit)
        blocks = (blocks[:half].astype(F32) + received.astype(F32)).astype(BF16)
    return blocks


def reorder(blocks, places):
    count = blocks.shape[0]

    def body(places_ref, in_ref, out_ref, sems):
        for index in range(count):
            pltpu.make_async_copy(
                in_ref.at[places_ref[index]], out_ref.at[index], sems.at[index]
            ).start()
        for index in range(count):
            pltpu.make_async_copy(
                in_ref.at[places_ref[index]], out_ref.at[index], sems.at[index]
            ).wait()

    return pl.pallas_call(
        body,
        out_shape=jax.ShapeDtypeStruct(blocks.shape, blocks.dtype),
        in_specs=[pl.BlockSpec(memory_space=pltpu.SMEM), pl.BlockSpec(memory_space=pl.ANY)],
        out_specs=pl.BlockSpec(memory_space=pl.ANY),
        scratch_shapes=[pltpu.SemaphoreType.DMA((count,))],
    )(places, blocks)


def inverse_places(order, place):
    by_relative = [0] * len(order)
    for position, relative in enumerate(order):
        by_relative[relative] = position
    count = len(order)
    return jnp.array(by_relative, jnp.int32)[jnp.arange(count, dtype=jnp.int32) ^ place]


def rope_tables(position):
    half_width = HEAD_SIZE // 2
    inverse = THETA ** (-(jnp.arange(half_width, dtype=F32) * 2.0) / HEAD_SIZE)
    angles = position.astype(F32)[..., None] * inverse
    return (jnp.cos(angles)[..., None, :], jnp.sin(angles)[..., None, :])


def apply_rotary(rows, cosine, sine):
    half_width = HEAD_SIZE // 2
    first, second = rows[..., :half_width], rows[..., half_width:]
    return jnp.concatenate([first * cosine - second * sine, second * cosine + first * sine], -1)


def rotate_back(rows, cosine, sine):
    return apply_rotary(rows, cosine, -sine)


def unit_norm(inputs):
    inverse_rms = lax.rsqrt(jnp.mean(inputs * inputs, axis=-1, keepdims=True) + NORM_EPSILON)
    return (inputs * inverse_rms, inverse_rms)


def norm_backward(d_normed, unit_rows, inverse_rms, gain_row):
    scaled = d_normed * gain_row
    return inverse_rms * (
        scaled - unit_rows * jnp.mean(scaled * unit_rows, axis=-1, keepdims=True)
    )


def matmul(equation, left, right):
    return jnp.einsum(equation, left, right, preferred_element_type=F32)


def adam_update(weights, moment, square, grad, rate, decay):
    new_moment = BETA_ONE * moment + (1.0 - BETA_ONE) * grad
    new_square = BETA_TWO * square + (1.0 - BETA_TWO) * grad * grad
    mean_hat = new_moment / (1.0 - BETA_ONE**STEP)
    square_hat = new_square / (1.0 - BETA_TWO**STEP)
    new_weights = weights - rate * (
        mean_hat / (jnp.sqrt(square_hat) + ADAM_EPSILON) + decay * weights
    )
    return (new_weights, new_moment, new_square)


def first_of(lengths, index):
    starts = jnp.cumsum(lengths, axis=-1) - lengths
    return jnp.max(
        jnp.where(starts[:, None, :] <= index[None, :, None], starts[:, None, :], 0), axis=-1
    )


def on_device(
    block_input,
    out_grad,
    doc_lengths,
    attention_weights,
    feedforward_weights,
    norm_gains,
    attention_moment,
    attention_square,
    feedforward_moment,
    feedforward_square,
    gain_moment,
    gain_square,
):
    both = ("dp", "seq")
    seq_count = lax.axis_size("seq")
    owner_count = lax.axis_size(both)
    seq_place = lax.axis_index("seq")
    owner_place = lax.axis_index(both)
    attention_length = attention_weights.shape[0]
    feedforward_length = feedforward_weights.shape[0]
    reach = min((DOC_MAX + DEVICE_TOKENS - 2) // DEVICE_TOKENS, seq_count - 1)
    paired = is_power_of_two(seq_count) and reach == seq_count - 1
    butterfly = is_power_of_two(owner_count) and attention_length % (8 * LANES) == 0
    stages = gather_stages()
    order = block_order(stages)
    seq_stages = [stage for stage in stages if stage[0] == "seq"]

    attention_low = attention_weights.astype(BF16)
    feedforward_low = feedforward_weights.astype(BF16)
    own_inputs = block_input[:, 0]
    if butterfly:
        gathered = doubled(attention_low.reshape(1, attention_length // LANES, LANES), stages)
        attention_full = reorder(gathered, inverse_places(order, owner_place)).reshape(-1)
    else:
        attention_full = lax.all_gather(attention_low, both, axis=0, tiled=True)
    if paired:
        window_inputs = doubled(own_inputs[None], seq_stages)
        window_blocks = seq_place ^ jnp.array(block_order(seq_stages), jnp.int32)
    else:
        window_inputs = jnp.stack(
            [own_inputs]
            + [
                lax.ppermute(
                    own_inputs, "seq", [(p, p + step) for p in range(seq_count - step)]
                )
                for step in range(1, reach + 1)
            ],
            0,
        )
        window_blocks = seq_place - jnp.arange(reach + 1, dtype=jnp.int32)
    if feedforward_length % (8 * LANES) == 0:
        feedforward_full = lax.all_gather(
            feedforward_low.reshape(-1, LANES), both, axis=0, tiled=True
        ).reshape(-1)
    else:
        feedforward_full = lax.all_gather(feedforward_low, both, axis=0, tiled=True)

    w_project = attention_full[: D * QKV_WIDTH].reshape(D, QKV_WIDTH)
    w_output = attention_full[D * QKV_WIDTH :].reshape(QUERY_WIDTH, D)
    w_gate_up = feedforward_full[: 2 * D * FF].reshape(D, 2 * FF)
    w_down = feedforward_full[2 * D * FF :].reshape(FF, D)

    window = (reach + 1) * DEVICE_TOKENS
    token = jnp.arange(DEVICE_TOKENS, dtype=jnp.int32)
    query_index = seq_place * DEVICE_TOKENS + token
    key_index = (window_blocks[:, None] * DEVICE_TOKENS + token[None, :]).reshape(-1)
    lengths = doc_lengths[:, 0]
    first_query = first_of(lengths, query_index)
    first_key = first_of(lengths, key_index)
    cosine_query, sine_query = rope_tables(query_index[None] - first_query)
    cosine_key, sine_key = rope_tables(key_index[None] - first_key)
    allowed = (key_index[None, None, :] >= first_query[:, :, None]) & (
        key_index[None, None, :] <= query_index[None, :, None]
    )

    inputs = own_inputs.astype(F32)
    unit_one, inverse_one = unit_norm(inputs)
    normed_one = (unit_one * norm_gains[0]).astype(BF16)
    window_rows = window_inputs.transpose(1, 0, 2, 3).reshape(MICRO, window, D)
    window_normed = (unit_norm(window_rows.astype(F32))[0] * norm_gains[0]).astype(BF16)
    query = apply_rotary(
        matmul("mtd,de->mte", normed_one, w_project[:, :QUERY_WIDTH]).reshape(
            MICRO, DEVICE_TOKENS, QUERY_HEADS, HEAD_SIZE
        ),
        cosine_query,
        sine_query,
    ).astype(BF16)
    query = query.reshape(MICRO, DEVICE_TOKENS, KEY_VALUE_HEADS, GROUP, HEAD_SIZE)
    projected = matmul("mkd,de->mke", window_normed, w_project[:, QUERY_WIDTH:])
    keys = apply_rotary(
        projected[..., :KV_WIDTH].reshape(MICRO, window, KEY_VALUE_HEADS, HEAD_SIZE),
        cosine_key,
        sine_key,
    ).astype(BF16)
    values = (
        projected[..., KV_WIDTH:].astype(BF16).reshape(MICRO, window, KEY_VALUE_HEADS, HEAD_SIZE)
    )
    scores = matmul("mthgd,mkhd->mhgtk", query, keys) * SCALE
    scores = jnp.where(allowed[:, None, None], scores, -jnp.inf)
    row_max = jnp.max(scores, axis=-1, keepdims=True)
    weights = jnp.exp(scores - row_max)
    row_sum = jnp.sum(weights, axis=-1, keepdims=True)
    probability = weights / row_sum
    probability_low = probability.astype(BF16)
    mixed = matmul("mhgtk,mkhd->mthgd", probability_low, values)
    mixed_low = mixed.astype(BF16).reshape(MICRO, DEVICE_TOKENS, QUERY_WIDTH)
    residual = inputs + matmul("mte,ed->mtd", mixed_low, w_output)
    unit_two, inverse_two = unit_norm(residual)
    normed_two = (unit_two * norm_gains[1]).astype(BF16)
    gate_up = matmul("mtd,de->mte", normed_two, w_gate_up)
    gate, up = gate_up[..., :FF], gate_up[..., FF:]
    gate_sigmoid = jax.nn.sigmoid(gate)
    activated = gate * gate_sigmoid
    hidden_low = (activated * up).astype(BF16)
    block_output = (residual + matmul("mtf,fd->mtd", hidden_low, w_down)).astype(BF16)

    cotangent_low = out_grad[:, 0]
    d_hidden = matmul("mtd,fd->mtf", cotangent_low, w_down)
    d_gate = d_hidden * up * gate_sigmoid * (1.0 + gate * (1.0 - gate_sigmoid))
    d_up = d_hidden * activated
    d_gate_up = jnp.concatenate([d_gate, d_up], -1).astype(BF16)
    grad_down = matmul("mtf,mtd->fd", hidden_low, cotangent_low)
    grad_gate_up = matmul("mtd,mte->de", normed_two, d_gate_up)
    gain_two = jnp.sum(grad_gate_up * w_gate_up.astype(F32), axis=1) / norm_gains[1]
    feedforward_rows = jnp.concatenate(
        [
            grad_gate_up.astype(BF16).reshape(-1, LANES),
            grad_down.astype(BF16).reshape(-1, LANES),
        ],
        0,
    )
    if feedforward_length % (8 * LANES) == 0:
        feedforward_owned = lax.psum_scatter(
            feedforward_rows, both, scatter_dimension=0, tiled=True
        ).reshape(-1)
    else:
        feedforward_owned = lax.psum_scatter(
            feedforward_rows.reshape(-1), both, scatter_dimension=0, tiled=True
        )
    d_normed_two = matmul("mte,de->mtd", d_gate_up, w_gate_up)
    d_residual = cotangent_low.astype(F32) + norm_backward(
        d_normed_two, unit_two, inverse_two, norm_gains[1]
    )
    d_branch = d_residual.astype(BF16)

    d_mixed = matmul("mtd,ed->mte", d_branch, w_output).astype(BF16)
    d_mixed = d_mixed.reshape(MICRO, DEVICE_TOKENS, KEY_VALUE_HEADS, GROUP, HEAD_SIZE)
    row_delta = jnp.einsum("mthgd,mthgd->mhgt", d_mixed.astype(F32), mixed)
    d_probs = matmul("mthgd,mkhd->mhgtk", d_mixed, values)
    d_scores = (probability * (d_probs - row_delta[..., None])).astype(BF16)
    d_query = matmul("mhgtk,mkhd->mthgd", d_scores, keys) * SCALE
    d_keys = matmul("mhgtk,mthgd->mkhd", d_scores, query) * SCALE
    d_values = matmul("mhgtk,mthgd->mkhd", probability_low, d_mixed)
    d_query_low = (
        rotate_back(
            d_query.reshape(MICRO, DEVICE_TOKENS, QUERY_HEADS, HEAD_SIZE), cosine_query, sine_query
        )
        .reshape(MICRO, DEVICE_TOKENS, QUERY_WIDTH)
        .astype(BF16)
    )
    d_window = jnp.concatenate(
        [
            rotate_back(d_keys, cosine_key, sine_key).reshape(MICRO, window, KV_WIDTH),
            d_values.reshape(MICRO, window, KV_WIDTH),
        ],
        -1,
    ).astype(BF16)
    grad_output = matmul("mte,mtd->ed", mixed_low, d_branch)
    grad_project = jnp.concatenate(
        [
            matmul("mtd,mte->de", normed_one, d_query_low),
            matmul("mkd,mke->de", window_normed, d_window),
        ],
        1,
    )
    gain_one = jnp.sum(grad_project * w_project.astype(F32), axis=1) / norm_gains[0]
    attention_rows = jnp.concatenate(
        [
            grad_project.astype(BF16).reshape(-1, LANES),
            grad_output.astype(BF16).reshape(-1, LANES),
        ],
        0,
    )
    if butterfly:
        attention_blocks = reorder(
            attention_rows.reshape(owner_count, attention_length // LANES, LANES),
            jnp.array(order, jnp.int32) ^ owner_place,
        )
        attention_owned = halved(attention_blocks, stages).reshape(-1)
    else:
        attention_owned = lax.psum_scatter(
            attention_rows.reshape(-1), both, scatter_dimension=0, tiled=True
        )
    blocks = d_window.reshape(MICRO, reach + 1, DEVICE_TOKENS, 2 * KV_WIDTH).transpose(1, 0, 2, 3)
    if paired:
        d_own = halved(blocks, seq_stages)[0]
    else:
        d_own = blocks[0].astype(F32)
        for step in range(1, reach + 1):
            d_own = d_own + lax.ppermute(
                blocks[step], "seq", [(p, p - step) for p in range(step, seq_count)]
            ).astype(F32)
        d_own = d_own.astype(BF16)
    d_normed_one = matmul(
        "mte,de->mtd", jnp.concatenate([d_query_low, d_own], -1), w_project
    )
    input_grad = d_residual + norm_backward(d_normed_one, unit_one, inverse_one, norm_gains[0])

    gains_total = jnp.stack([gain_one, gain_two], 0)
    if butterfly:
        for axis, bit, unused_flat in stages:
            gains_total = gains_total + exchange(gains_total, axis, bit)
    else:
        gains_total = lax.psum(gains_total, both)

    attention_place = owner_place * attention_length + jnp.arange(attention_length, dtype=jnp.int32)
    attention_rate = jnp.where(
        attention_place < D * QKV_WIDTH, RATE_FACTOR * D ** (-0.5), RATE_FACTOR * OUT_FAN ** (-0.5)
    )
    feedforward_place = owner_place * feedforward_length + jnp.arange(
        feedforward_length, dtype=jnp.int32
    )
    feedforward_rate = jnp.where(
        feedforward_place < 2 * D * FF, RATE_FACTOR * D ** (-0.5), RATE_FACTOR * FF ** (-0.5)
    )
    new_attention = adam_update(
        attention_weights,
        attention_moment,
        attention_square,
        attention_owned.astype(F32),
        attention_rate,
        MATRIX_DECAY,
    )
    new_feedforward = adam_update(
        feedforward_weights,
        feedforward_moment,
        feedforward_square,
        feedforward_owned.astype(F32),
        feedforward_rate,
        MATRIX_DECAY,
    )
    new_gains = adam_update(norm_gains, gain_moment, gain_square, gains_total, GAIN_RATE, 0.0)
    return (
        block_output[:, None],
        input_grad[:, None],
        *new_attention,
        *new_feedforward,
        *new_gains,
    )


def solution(mesh):
    tokens = P(None, "dp", "seq", None)
    flat = P(("dp", "seq"))
    return jax.shard_map(
        on_device,
        mesh=mesh,
        in_specs=(
            tokens,
            tokens,
            P(None, "dp", None),
            flat,
            flat,
            P(),
            flat,
            flat,
            flat,
            flat,
            P(),
            P(),
        ),
        out_specs=(tokens, tokens, flat, flat, flat, flat, flat, flat, P(), P(), P()),
        check_vma=False,
    )
```

```python
import jax
import jax.numpy as jnp
from jax import lax
from jax.experimental import pallas as pl
from jax.experimental.pallas import tpu as pltpu
from jax.sharding import PartitionSpec as P

D = 576
QUERY_HEADS = 9
KEY_VALUE_HEADS = 3
GROUP = QUERY_HEADS // KEY_VALUE_HEADS
HEAD_SIZE = 64
FF = 1536
DEVICE_TOKENS = 128
MICRO = 2
DOC_MAX = 1000
STEP = 10
QKV_WIDTH = 960
QUERY_WIDTH = QUERY_HEADS * HEAD_SIZE
KV_WIDTH = KEY_VALUE_HEADS * HEAD_SIZE
OUT_FAN = 14
LANES = 128
HALF = LANES // 2
BLOCKS = 32
VMEM_LIMIT = 52 * 2**20

NORM_EPSILON = 1e-05
THETA = 100000.0
BETA_ONE = 0.9
BETA_TWO = 0.95
ADAM_EPSILON = 1e-08
MATRIX_DECAY = 0.1
RATE_FACTOR = 1.5
GAIN_RATE = 0.2
SCALE = HEAD_SIZE ** (-0.5)
BF16 = jnp.bfloat16
F32 = jnp.float32


def is_power_of_two(count):
    return count & (count - 1) == 0


def exchange(value, axis, bit):
    count = lax.axis_size(axis)
    return lax.ppermute(value, axis, [(place, place ^ bit) for place in range(count)])


def gather_stages():
    seq, dp = lax.axis_size("seq"), lax.axis_size("dp")
    stages = []
    bit = seq // 2
    while bit > 1:
        stages.append(("seq", bit, bit))
        bit //= 2
    bit = dp // 2
    while bit >= 1:
        stages.append(("dp", bit, bit * seq))
        bit //= 2
    if seq > 1:
        stages.append(("seq", 1, 1))
    return stages


def block_order(stages):
    order = [0]
    for unused_axis, unused_bit, flat_bit in stages:
        order = order + [place ^ flat_bit for place in order]
    return order


def doubled(block, stages):
    for axis, bit, unused_flat in stages:
        block = jnp.concatenate([block, exchange(block, axis, bit)], 0)
    return block


def halved(blocks, stages):
    for axis, bit, unused_flat in reversed(stages):
        half = blocks.shape[0] // 2
        received = exchange(blocks[half:], axis, bit)
        blocks = (blocks[:half].astype(F32) + received.astype(F32)).astype(BF16)
    return blocks


def inverse_places(order, place):
    by_relative = [0] * len(order)
    for position, relative in enumerate(order):
        by_relative[relative] = position
    count = len(order)
    return jnp.array(by_relative, jnp.int32)[jnp.arange(count, dtype=jnp.int32) ^ place]


def unit_norm(inputs):
    inverse_rms = lax.rsqrt(jnp.mean(inputs * inputs, axis=-1, keepdims=True) + NORM_EPSILON)
    return (inputs * inverse_rms, inverse_rms)


def norm_backward(d_normed, unit_rows, inverse_rms, gain_row):
    scaled = d_normed * gain_row
    return inverse_rms * (
        scaled - unit_rows * jnp.mean(scaled * unit_rows, axis=-1, keepdims=True)
    )


def matmul(equation, left, right):
    return jnp.einsum(equation, left, right, preferred_element_type=F32)


def params():
    return pltpu.CompilerParams(vmem_limit_bytes=VMEM_LIMIT)


def vmem(count):
    return [pl.BlockSpec(memory_space=pltpu.VMEM)] * count


def smem():
    return pl.BlockSpec(memory_space=pltpu.SMEM)


def dot(left, right):
    return jnp.dot(left, right, preferred_element_type=F32)


def dot_nt(left, right):
    return lax.dot_general(left, right, (((1,), (1,)), ((), ())), preferred_element_type=F32)


def dot_tn(left, right):
    return lax.dot_general(left, right, (((0,), (0,)), ((), ())), preferred_element_type=F32)


def shift_half(low, high):
    lane = lax.broadcasted_iota(jnp.int32, low.shape, 1)
    return pltpu.roll(jnp.where(lane < HALF, low, high), HALF, 1)


def unflatten_odd(flat, base, pairs, whole, planes):
    step = 2 * whole + 1

    def piece(k):
        return flat[pl.ds(base + k, pairs, stride=step), :]

    for j in range(whole + 1):
        planes[j, pl.ds(0, pairs, stride=2), :] = piece(j)
        planes[j, pl.ds(1, pairs, stride=2), :] = shift_half(
            piece(min(whole + 1 + j, 2 * whole)), piece(whole + j)
        )


def flatten_odd(planes, pairs, whole, flat, base):
    step = 2 * whole + 1

    def even(j):
        return planes[j, pl.ds(0, pairs, stride=2), :]

    def odd(j):
        return planes[j, pl.ds(1, pairs, stride=2), :]

    for k in range(step):
        if k < whole:
            rows = even(k)
        elif k == whole:
            first = odd(0)
            lane = lax.broadcasted_iota(jnp.int32, first.shape, 1)
            rows = jnp.where(lane < HALF, even(whole), pltpu.roll(first, HALF, 1))
        else:
            rows = shift_half(odd(k - whole), odd(k - whole - 1))
        flat[pl.ds(base + k, pairs, stride=step), :] = rows


def load_blocks(places, blocks, flat):
    count, rows, unused = blocks.shape
    for index in range(count):
        flat[index * rows : (index + 1) * rows, :] = blocks[places[index]].astype(F32)


def store_blocks(order, flat, blocks):
    count, rows, unused = blocks.shape
    for index in range(count):
        start = pl.multiple_of(order[index] * rows, 8)
        blocks[index] = flat[pl.ds(start, rows), :].astype(BF16)


def planes_to_matrix(planes, whole, matrix):
    for j in range(whole):
        matrix[:, j * LANES : (j + 1) * LANES] = planes[j].astype(BF16)
    matrix[:, whole * LANES : whole * LANES + HALF] = planes[whole, :, :HALF].astype(BF16)


def rotated(rows, cosine, sine):
    half_width = HEAD_SIZE // 2
    first, second = rows[:half_width], rows[half_width:]
    return jnp.concatenate([first * cosine - second * sine, second * cosine + first * sine], 0)


def attention_forward_kernel(
    places,
    weight_blocks,
    window_inputs,
    cosines,
    sines,
    bias,
    gains,
    w_project,
    w_output,
    normed,
    queries,
    keys_across,
    keys,
    values,
    log_totals,
    mixed_across,
    residual,
    flat,
    planes_one,
    planes_two,
    w_across,
    values_across,
):
    load_blocks(places, weight_blocks, flat)
    unflatten_odd(flat, 0, D // 2, 7, planes_one)
    planes_to_matrix(planes_one, 7, w_project)
    for j in range(7):
        w_across[j * LANES : (j + 1) * LANES, :] = jnp.transpose(planes_one[j]).astype(BF16)
    w_across[7 * LANES :, :] = jnp.transpose(planes_one[7])[:HALF].astype(BF16)
    unflatten_odd(flat, D * QKV_WIDTH // LANES, QUERY_WIDTH // 2, 4, planes_two)
    planes_to_matrix(planes_two, 4, w_output)
    blocks = window_inputs.shape[0]
    gain = gains[0:1, :]
    for micro in range(MICRO):
        for block in range(blocks):
            rows = window_inputs[block, micro].astype(F32)
            inverse = lax.rsqrt(jnp.mean(rows * rows, axis=-1, keepdims=True) + NORM_EPSILON)
            normed[micro, block * DEVICE_TOKENS : (block + 1) * DEVICE_TOKENS, :] = (
                rows * inverse * gain
            ).astype(BF16)
        cosine, sine = cosines[micro], sines[micro]
        own_cosine, own_sine = cosine[:, :DEVICE_TOKENS], sine[:, :DEVICE_TOKENS]
        query = dot_nt(w_across[:QUERY_WIDTH, :], normed[micro, :DEVICE_TOKENS, :])
        for head in range(QUERY_HEADS):
            rows = slice(head * HEAD_SIZE, (head + 1) * HEAD_SIZE)
            queries[micro, rows, :] = rotated(query[rows], own_cosine, own_sine).astype(BF16)
        other = dot_nt(w_across[QUERY_WIDTH:, :], normed[micro])
        for head in range(KEY_VALUE_HEADS):
            rows = slice(head * HEAD_SIZE, (head + 1) * HEAD_SIZE)
            key = rotated(other[rows], cosine, sine)
            keys_across[micro, rows, :] = key.astype(BF16)
            keys[micro, head] = jnp.transpose(key).astype(BF16)
            value = other[KV_WIDTH + head * HEAD_SIZE : KV_WIDTH + (head + 1) * HEAD_SIZE]
            values_across[rows, :] = value.astype(BF16)
            values[micro, head] = jnp.transpose(value).astype(BF16)
        for head in range(QUERY_HEADS):
            group = head // GROUP
            rows = slice(head * HEAD_SIZE, (head + 1) * HEAD_SIZE)
            group_rows = slice(group * HEAD_SIZE, (group + 1) * HEAD_SIZE)
            scores = dot(keys[micro, group], queries[micro, rows, :] * SCALE) + bias[micro]
            top = jnp.max(scores, axis=0, keepdims=True)
            weights = jnp.exp(scores - top)
            total = jnp.sum(weights, axis=0, keepdims=True)
            low = (weights * (1.0 / total)).astype(BF16)
            mixed_across[micro, rows, :] = dot(values_across[group_rows, :], low)
            log_totals[micro, head : head + 1, :] = top + jnp.log(total)
        mixed = jnp.transpose(mixed_across[micro]).astype(BF16)
        residual[micro] = window_inputs[0, micro].astype(F32) + dot(mixed, w_output[...])


def attention_forward(places, weight_blocks, window_inputs, cosines, sines, bias, gains):
    window = window_inputs.shape[0] * DEVICE_TOKENS
    shape = jax.ShapeDtypeStruct
    rows = weight_blocks.shape[0] * weight_blocks.shape[1]
    return pl.pallas_call(
        attention_forward_kernel,
        out_shape=(
            shape((D, QKV_WIDTH), BF16),
            shape((QUERY_WIDTH, D), BF16),
            shape((MICRO, window, D), BF16),
            shape((MICRO, QUERY_WIDTH, DEVICE_TOKENS), BF16),
            shape((MICRO, KV_WIDTH, window), BF16),
            shape((MICRO, KEY_VALUE_HEADS, window, HEAD_SIZE), BF16),
            shape((MICRO, KEY_VALUE_HEADS, window, HEAD_SIZE), BF16),
            shape((MICRO, QUERY_HEADS, DEVICE_TOKENS), F32),
            shape((MICRO, QUERY_WIDTH, DEVICE_TOKENS), F32),
            shape((MICRO, DEVICE_TOKENS, D), F32),
        ),
        in_specs=[smem()] + vmem(6),
        out_specs=tuple(vmem(10)),
        scratch_shapes=[
            pltpu.VMEM((rows, LANES), F32),
            pltpu.VMEM((8, D, LANES), F32),
            pltpu.VMEM((5, QUERY_WIDTH, LANES), F32),
            pltpu.VMEM((QKV_WIDTH, D), BF16),
            pltpu.VMEM((KV_WIDTH, window), BF16),
        ],
        compiler_params=params(),
    )(places, weight_blocks, window_inputs, cosines, sines, bias, gains)


def feedforward_kernel(
    places,
    order,
    weight_blocks,
    residual,
    cotangent,
    gains,
    block_output,
    d_residual,
    grad_blocks,
    gain_grad,
    flat,
    planes,
    w_gate_up,
    w_down,
    hidden,
    d_gate_up,
):
    columns = 2 * FF // LANES
    load_blocks(places, weight_blocks, flat)
    for j in range(columns):
        w_gate_up[:, j * LANES : (j + 1) * LANES] = flat[
            pl.ds(j, D, stride=columns), :
        ].astype(BF16)
    unflatten_odd(flat, D * columns, FF // 2, 4, planes)
    planes_to_matrix(planes, 4, w_down)
    gain = gains[1:2, :]
    rows = residual[...]
    inverse = lax.rsqrt(jnp.mean(rows * rows, axis=-1, keepdims=True) + NORM_EPSILON)
    unit = rows * inverse
    normed = (unit * gain).astype(BF16)
    cotangent_low = cotangent[...]
    part = 256
    for start in range(0, FF, part):
        gate = dot(normed, w_gate_up[:, start : start + part])
        up = dot(normed, w_gate_up[:, FF + start : FF + start + part])
        d_hidden = dot_nt(cotangent_low, w_down[start : start + part, :])
        sigmoid = 1.0 / (1.0 + jnp.exp(-gate))
        activated = gate * sigmoid
        hidden[:, start : start + part] = (activated * up).astype(BF16)
        d_gate_up[:, start : start + part] = (
            d_hidden * up * sigmoid * (1.0 + gate * (1.0 - sigmoid))
        ).astype(BF16)
        d_gate_up[:, FF + start : FF + start + part] = (d_hidden * activated).astype(BF16)
    block_output[...] = (rows + dot(hidden[...], w_down[...])).astype(BF16)
    d_normed = dot_nt(d_gate_up[...], w_gate_up[...])
    scaled = d_normed * gain
    d_residual[...] = cotangent_low.astype(F32) + inverse * (
        scaled - unit * jnp.mean(scaled * unit, axis=-1, keepdims=True)
    )
    normed_across = jnp.transpose(unit * gain).astype(BF16)
    total = jnp.zeros((D, LANES), F32)
    for start in range(0, 2 * FF, part):
        grad = dot(normed_across, d_gate_up[:, start : start + part])
        for offset in range(0, part, LANES):
            piece = grad[:, offset : offset + LANES]
            place = start + offset
            total = total + piece * w_gate_up[:, place : place + LANES].astype(F32)
            flat[pl.ds(place // LANES, D, stride=columns), :] = piece
    gain_grad[...] = jnp.sum(total, axis=1, keepdims=True)
    for start in range(0, FF, part):
        grad = dot_tn(hidden[:, start : start + part], cotangent_low)
        for j in range(4):
            planes[j, start : start + part, :] = grad[:, j * LANES : (j + 1) * LANES]
        planes[4, start : start + part, :HALF] = grad[:, 4 * LANES :]
    flatten_odd(planes, FF // 2, 4, flat, D * columns)
    store_blocks(order, flat, grad_blocks)


def feedforward(places, order, weight_blocks, residual, cotangent, gains):
    shape = jax.ShapeDtypeStruct
    tokens = residual.shape[0]
    rows = weight_blocks.shape[0] * weight_blocks.shape[1]
    return pl.pallas_call(
        feedforward_kernel,
        out_shape=(
            shape((tokens, D), BF16),
            shape((tokens, D), F32),
            shape(weight_blocks.shape, BF16),
            shape((D, 1), F32),
        ),
        in_specs=[smem(), smem()] + vmem(4),
        out_specs=tuple(vmem(4)),
        scratch_shapes=[
            pltpu.VMEM((rows, LANES), F32),
            pltpu.VMEM((5, FF, LANES), F32),
            pltpu.VMEM((D, 2 * FF), BF16),
            pltpu.VMEM((FF, D), BF16),
            pltpu.VMEM((tokens, FF), BF16),
            pltpu.VMEM((tokens, 2 * FF), BF16),
        ],
        compiler_params=params(),
    )(places, order, weight_blocks, residual, cotangent, gains)


def attention_backward_kernel(
    order,
    w_project,
    w_output,
    normed,
    queries,
    keys_across,
    keys,
    values,
    log_totals,
    mixed_across,
    d_residual,
    cosines,
    sines,
    bias,
    grad_blocks,
    d_queries,
    d_window,
    gain_grad,
    flat,
    planes,
    d_window_across,
    grad_across,
    grad_output,
):
    blocks = d_window.shape[0]
    for micro in range(MICRO):
        cosine, sine = cosines[micro], sines[micro]
        own_cosine, own_sine = cosine[:, :DEVICE_TOKENS], sine[:, :DEVICE_TOKENS]
        d_branch = d_residual[micro].astype(BF16)
        d_mixed = dot_nt(w_output[...], d_branch).astype(BF16)
        mixed = mixed_across[micro]
        for group in range(KEY_VALUE_HEADS):
            group_rows = slice(group * HEAD_SIZE, (group + 1) * HEAD_SIZE)
            d_key = None
            for head in range(group * GROUP, (group + 1) * GROUP):
                rows = slice(head * HEAD_SIZE, (head + 1) * HEAD_SIZE)
                query = queries[micro, rows, :] * SCALE
                d_mixed_head = d_mixed[rows]
                delta = jnp.sum(d_mixed_head.astype(F32) * mixed[rows], axis=0, keepdims=True)
                scores = dot(keys[micro, group], query) + bias[micro]
                probability = jnp.exp(scores - log_totals[micro, head : head + 1, :])
                d_probs = dot(values[micro, group], d_mixed_head)
                d_scores = (probability * (d_probs - delta)).astype(BF16)
                d_query = dot(keys_across[micro, group_rows, :], d_scores) * SCALE
                d_queries[micro, rows, :] = rotated(d_query, own_cosine, -own_sine).astype(BF16)
                key_part = dot_nt(query, d_scores)
                value_part = dot_nt(d_mixed_head, probability.astype(BF16))
                d_key = key_part if d_key is None else d_key + key_part
                if head == group * GROUP:
                    d_value = value_part
                else:
                    d_value = d_value + value_part
            d_window_across[group_rows, :] = rotated(d_key, cosine, -sine).astype(BF16)
            value_rows = slice(
                KV_WIDTH + group * HEAD_SIZE, KV_WIDTH + (group + 1) * HEAD_SIZE
            )
            d_window_across[value_rows, :] = d_value.astype(BF16)
        for block in range(blocks):
            d_window[block, micro] = d_window_across[
                :, block * DEVICE_TOKENS : (block + 1) * DEVICE_TOKENS
            ]
        query_grad = dot(d_queries[micro], normed[micro, :DEVICE_TOKENS, :])
        window_grad = dot(d_window_across[...], normed[micro])
        output_grad = dot(mixed.astype(BF16), d_branch)
        if micro == 0:
            grad_across[:QUERY_WIDTH, :] = query_grad
            grad_across[QUERY_WIDTH:, :] = window_grad
            grad_output[...] = output_grad
        else:
            grad_across[:QUERY_WIDTH, :] += query_grad
            grad_across[QUERY_WIDTH:, :] += window_grad
            grad_output[...] += output_grad
    total = jnp.zeros((D, LANES), F32)
    for j in range(7):
        piece = jnp.transpose(grad_across[j * LANES : (j + 1) * LANES, :])
        planes[j] = piece
        total = total + piece * w_project[:, j * LANES : (j + 1) * LANES].astype(F32)
    last = jnp.transpose(grad_across[QKV_WIDTH - LANES :, :])
    last = pltpu.roll(last, HALF, 1)
    planes[7] = last
    last_sum = last[:, :HALF] * w_project[:, 7 * LANES :].astype(F32)
    gain_grad[...] = jnp.sum(total, axis=1, keepdims=True) + jnp.sum(
        last_sum, axis=1, keepdims=True
    )
    flatten_odd(planes, D // 2, 7, flat, 0)
    for j in range(4):
        planes[j] = grad_output[:, j * LANES : (j + 1) * LANES]
    planes[4, :, :HALF] = grad_output[:, 4 * LANES :]
    flatten_odd(planes, QUERY_WIDTH // 2, 4, flat, D * QKV_WIDTH // LANES)
    store_blocks(order, flat, grad_blocks)


def attention_backward(order, rows, *operands):
    shape = jax.ShapeDtypeStruct
    window = operands[2].shape[1]
    count = order.shape[0]
    return pl.pallas_call(
        attention_backward_kernel,
        out_shape=(
            shape((count, rows, LANES), BF16),
            shape((MICRO, QUERY_WIDTH, DEVICE_TOKENS), BF16),
            shape((window // DEVICE_TOKENS, MICRO, 2 * KV_WIDTH, DEVICE_TOKENS), BF16),
            shape((D, 1), F32),
        ),
        in_specs=[smem()] + vmem(len(operands)),
        out_specs=tuple(vmem(4)),
        scratch_shapes=[
            pltpu.VMEM((count * rows, LANES), F32),
            pltpu.VMEM((8, D, LANES), F32),
            pltpu.VMEM((2 * KV_WIDTH, window), BF16),
            pltpu.VMEM((QKV_WIDTH, D), F32),
            pltpu.VMEM((QUERY_WIDTH, D), F32),
        ],
        compiler_params=params(),
    )(order, *operands)


def adam_update(weights, moment, square, grad, rate, decay):
    new_moment = BETA_ONE * moment + (1.0 - BETA_ONE) * grad
    new_square = BETA_TWO * square + (1.0 - BETA_TWO) * grad * grad
    mean_hat = new_moment / (1.0 - BETA_ONE**STEP)
    square_hat = new_square / (1.0 - BETA_TWO**STEP)
    new_weights = weights - rate * (
        mean_hat / (jnp.sqrt(square_hat) + ADAM_EPSILON) + decay * weights
    )
    return (new_weights, new_moment, new_square)


def first_of(lengths, index):
    starts = jnp.cumsum(lengths, axis=-1) - lengths
    return jnp.max(
        jnp.where(starts[:, None, :] <= index[None, :, None], starts[:, None, :], 0), axis=-1
    )


def on_device(
    block_input,
    out_grad,
    doc_lengths,
    attention_weights,
    feedforward_weights,
    norm_gains,
    attention_moment,
    attention_square,
    feedforward_moment,
    feedforward_square,
    gain_moment,
    gain_square,
):
    both = ("dp", "seq")
    seq_count = lax.axis_size("seq")
    owner_count = lax.axis_size(both)
    seq_place = lax.axis_index("seq")
    owner_place = lax.axis_index(both)
    attention_length = attention_weights.shape[0]
    feedforward_length = feedforward_weights.shape[0]
    reach = min((DOC_MAX + DEVICE_TOKENS - 2) // DEVICE_TOKENS, seq_count - 1)
    paired = is_power_of_two(seq_count) and reach == seq_count - 1
    butterfly = is_power_of_two(owner_count) and attention_length % (8 * LANES) == 0
    stages = gather_stages()
    order = block_order(stages)
    seq_stages = [stage for stage in stages if stage[0] == "seq"]

    attention_low = attention_weights.astype(BF16)
    feedforward_low = feedforward_weights.astype(BF16)
    own_inputs = block_input[:, 0]
    straight = jnp.arange(BLOCKS, dtype=jnp.int32)
    if butterfly:
        attention_blocks = doubled(
            attention_low.reshape(1, attention_length // LANES, LANES), stages
        )
        attention_places = inverse_places(order, owner_place)
        attention_order = jnp.array(order, jnp.int32) ^ owner_place
    else:
        attention_blocks = lax.all_gather(attention_low, both, axis=0, tiled=True)
        attention_blocks = attention_blocks.reshape(BLOCKS, -1, LANES)
        attention_places = attention_order = straight
    if paired:
        window_inputs = doubled(own_inputs[None], seq_stages)
        window_blocks = seq_place ^ jnp.array(block_order(seq_stages), jnp.int32)
    else:
        window_inputs = jnp.stack(
            [own_inputs]
            + [
                lax.ppermute(
                    own_inputs, "seq", [(p, p + step) for p in range(seq_count - step)]
                )
                for step in range(1, reach + 1)
            ],
            0,
        )
        window_blocks = seq_place - jnp.arange(reach + 1, dtype=jnp.int32)
    tiled_rows = feedforward_length % (8 * LANES) == 0
    if tiled_rows:
        feedforward_low = feedforward_low.reshape(-1, LANES)
    feedforward_blocks = lax.all_gather(feedforward_low, both, axis=0, tiled=True)
    feedforward_blocks = feedforward_blocks.reshape(BLOCKS, -1, LANES)

    token = jnp.arange(DEVICE_TOKENS, dtype=jnp.int32)
    query_index = seq_place * DEVICE_TOKENS + token
    key_index = (window_blocks[:, None] * DEVICE_TOKENS + token[None, :]).reshape(-1)
    lengths = doc_lengths[:, 0]
    first_query = first_of(lengths, query_index)
    first_key = first_of(lengths, key_index)
    half_width = HEAD_SIZE // 2
    inverse = THETA ** (-(jnp.arange(half_width, dtype=F32) * 2.0) / HEAD_SIZE)
    position = (key_index[None] - first_key).astype(F32)
    angles = position[:, None, :] * inverse[None, :, None]
    cosines, sines = jnp.cos(angles), jnp.sin(angles)
    allowed = (key_index[None, :, None] >= first_query[:, None, :]) & (
        key_index[None, :, None] <= query_index[None, None, :]
    )
    bias = jnp.where(allowed, 0.0, -jnp.inf).astype(F32)

    (
        w_project,
        w_output,
        normed_one,
        queries,
        keys_across,
        keys,
        values,
        log_totals,
        mixed_across,
        residual,
    ) = attention_forward(
        attention_places, attention_blocks, window_inputs, cosines, sines, bias, norm_gains
    )
    block_output, d_residual, feedforward_grads, gain_two = feedforward(
        straight,
        straight,
        feedforward_blocks,
        residual.reshape(-1, D),
        out_grad[:, 0].reshape(-1, D),
        norm_gains,
    )
    block_output = block_output.reshape(MICRO, DEVICE_TOKENS, D)
    d_residual = d_residual.reshape(MICRO, DEVICE_TOKENS, D)
    feedforward_grads = feedforward_grads.reshape(-1, LANES)
    if not tiled_rows:
        feedforward_grads = feedforward_grads.reshape(-1)
    feedforward_owned = lax.psum_scatter(
        feedforward_grads, both, scatter_dimension=0, tiled=True
    ).reshape(-1)
    attention_grads, d_queries, d_window, gain_one = attention_backward(
        attention_order,
        D * (QKV_WIDTH + QUERY_WIDTH) // (LANES * BLOCKS),
        w_project,
        w_output,
        normed_one,
        queries,
        keys_across,
        keys,
        values,
        log_totals,
        mixed_across,
        d_residual,
        cosines,
        sines,
        bias,
    )
    if butterfly:
        attention_owned = halved(attention_grads, stages).reshape(-1)
    else:
        attention_owned = lax.psum_scatter(
            attention_grads.reshape(-1), both, scatter_dimension=0, tiled=True
        )
    if paired:
        d_own = halved(d_window, seq_stages)[0]
    else:
        d_own = d_window[0].astype(F32)
        for step in range(1, reach + 1):
            d_own = d_own + lax.ppermute(
                d_window[step], "seq", [(p, p - step) for p in range(step, seq_count)]
            ).astype(F32)
        d_own = d_own.astype(BF16)
    d_normed_one = matmul("met,de->mtd", jnp.concatenate([d_queries, d_own], 1), w_project)
    unit_one, inverse_one = unit_norm(own_inputs.astype(F32))
    input_grad = d_residual + norm_backward(d_normed_one, unit_one, inverse_one, norm_gains[0])

    gains_total = jnp.stack([gain_one[:, 0], gain_two[:, 0]], 0) / norm_gains
    if butterfly:
        for axis, bit, unused_flat in stages:
            gains_total = gains_total + exchange(gains_total, axis, bit)
    else:
        gains_total = lax.psum(gains_total, both)

    attention_place = owner_place * attention_length + jnp.arange(attention_length, dtype=jnp.int32)
    attention_rate = jnp.where(
        attention_place < D * QKV_WIDTH, RATE_FACTOR * D ** (-0.5), RATE_FACTOR * OUT_FAN ** (-0.5)
    )
    feedforward_place = owner_place * feedforward_length + jnp.arange(
        feedforward_length, dtype=jnp.int32
    )
    feedforward_rate = jnp.where(
        feedforward_place < 2 * D * FF, RATE_FACTOR * D ** (-0.5), RATE_FACTOR * FF ** (-0.5)
    )
    new_attention = adam_update(
        attention_weights,
        attention_moment,
        attention_square,
        attention_owned.astype(F32),
        attention_rate,
        MATRIX_DECAY,
    )
    new_feedforward = adam_update(
        feedforward_weights,
        feedforward_moment,
        feedforward_square,
        feedforward_owned.astype(F32),
        feedforward_rate,
        MATRIX_DECAY,
    )
    new_gains = adam_update(norm_gains, gain_moment, gain_square, gains_total, GAIN_RATE, 0.0)
    return (
        block_output[:, None],
        input_grad[:, None],
        *new_attention,
        *new_feedforward,
        *new_gains,
    )


def solution(mesh):
    tokens = P(None, "dp", "seq", None)
    flat = P(("dp", "seq"))
    return jax.shard_map(
        on_device,
        mesh=mesh,
        in_specs=(
            tokens,
            tokens,
            P(None, "dp", None),
            flat,
            flat,
            P(),
            flat,
            flat,
            flat,
            flat,
            P(),
            P(),
        ),
        out_specs=(tokens, tokens, flat, flat, flat, flat, flat, flat, P(), P(), P()),
        check_vma=False,
    )
```

```python
import jax
import jax.numpy as jnp
from jax import lax
from jax.experimental import pallas as pl
from jax.experimental.pallas import tpu as pltpu
from jax.sharding import PartitionSpec as P

D = 576
QUERY_HEADS = 9
KEY_VALUE_HEADS = 3
GROUP = QUERY_HEADS // KEY_VALUE_HEADS
HEAD_SIZE = 64
FF = 1536
DEVICE_TOKENS = 128
MICRO = 2
DOC_MAX = 1000
STEP = 10
QKV_WIDTH = 960
QUERY_WIDTH = QUERY_HEADS * HEAD_SIZE
KV_WIDTH = KEY_VALUE_HEADS * HEAD_SIZE
OUT_FAN = 14
LANES = 128
HALF = LANES // 2
BLOCKS = 32
VMEM_LIMIT = 52 * 2**20

NORM_EPSILON = 1e-05
THETA = 100000.0
BETA_ONE = 0.9
BETA_TWO = 0.95
ADAM_EPSILON = 1e-08
MATRIX_DECAY = 0.1
RATE_FACTOR = 1.5
GAIN_RATE = 0.2
SCALE = HEAD_SIZE ** (-0.5)
BF16 = jnp.bfloat16
F32 = jnp.float32


def is_power_of_two(count):
    return count & (count - 1) == 0


def exchange(value, axis, bit):
    count = lax.axis_size(axis)
    return lax.ppermute(value, axis, [(place, place ^ bit) for place in range(count)])


def gather_stages():
    seq, dp = lax.axis_size("seq"), lax.axis_size("dp")
    stages = []
    bit = seq // 2
    while bit > 1:
        stages.append(("seq", bit, bit))
        bit //= 2
    bit = dp // 2
    while bit >= 1:
        stages.append(("dp", bit, bit * seq))
        bit //= 2
    if seq > 1:
        stages.append(("seq", 1, 1))
    return stages


def block_order(stages):
    order = [0]
    for unused_axis, unused_bit, flat_bit in stages:
        order = order + [place ^ flat_bit for place in order]
    return order


def swap_dp(stages):
    turned = iter([stage for stage in reversed(stages) if stage[0] == "dp"])
    return [next(turned) if stage[0] == "dp" else stage for stage in stages]


def halve_step(blocks, received):
    half = blocks.shape[0] // 2
    return (blocks[:half].astype(F32) + received.astype(F32)).astype(BF16)


def send_half(blocks, stage):
    axis, bit, unused_flat = stage
    return exchange(blocks[blocks.shape[0] // 2 :], axis, bit)


def together(*values):
    return lax.optimization_barrier(values)


def unit_norm(inputs):
    inverse_rms = lax.rsqrt(jnp.mean(inputs * inputs, axis=-1, keepdims=True) + NORM_EPSILON)
    return (inputs * inverse_rms, inverse_rms)


def norm_backward(d_normed, unit_rows, inverse_rms, gain_row):
    scaled = d_normed * gain_row
    return inverse_rms * (
        scaled - unit_rows * jnp.mean(scaled * unit_rows, axis=-1, keepdims=True)
    )


def matmul(equation, left, right):
    return jnp.einsum(equation, left, right, preferred_element_type=F32)


def params():
    return pltpu.CompilerParams(vmem_limit_bytes=VMEM_LIMIT)


def vmem(count):
    return [pl.BlockSpec(memory_space=pltpu.VMEM)] * count


def smem():
    return pl.BlockSpec(memory_space=pltpu.SMEM)


def dot(left, right):
    return jnp.dot(left, right, preferred_element_type=F32)


def dot_nt(left, right):
    return lax.dot_general(left, right, (((1,), (1,)), ((), ())), preferred_element_type=F32)


def dot_tn(left, right):
    return lax.dot_general(left, right, (((0,), (0,)), ((), ())), preferred_element_type=F32)


def shift_half(low, high):
    lane = lax.broadcasted_iota(jnp.int32, low.shape, 1)
    return pltpu.roll(jnp.where(lane < HALF, low, high), HALF, 1)


def unflatten_odd(flat, base, pairs, whole, planes):
    step = 2 * whole + 1

    def piece(k):
        return flat[pl.ds(base + k, pairs, stride=step), :]

    for j in range(whole + 1):
        planes[j, pl.ds(0, pairs, stride=2), :] = piece(j)
        planes[j, pl.ds(1, pairs, stride=2), :] = shift_half(
            piece(min(whole + 1 + j, 2 * whole)), piece(whole + j)
        )


def flatten_odd(planes, pairs, whole, flat, base):
    step = 2 * whole + 1

    def even(j):
        return planes[j, pl.ds(0, pairs, stride=2), :]

    def odd(j):
        return planes[j, pl.ds(1, pairs, stride=2), :]

    for k in range(step):
        if k < whole:
            rows = even(k)
        elif k == whole:
            first = odd(0)
            lane = lax.broadcasted_iota(jnp.int32, first.shape, 1)
            rows = jnp.where(lane < HALF, even(whole), pltpu.roll(first, HALF, 1))
        else:
            rows = shift_half(odd(k - whole), odd(k - whole - 1))
        flat[pl.ds(base + k, pairs, stride=step), :] = rows


def load_blocks(order, halves, flat):
    first = 0
    for blocks in halves:
        count, rows, unused = blocks.shape

        def move(place, unused, blocks=blocks, rows=rows, first=first):
            start = pl.multiple_of(order[first + place] * rows, 8)
            flat[pl.ds(start, rows), :] = blocks[place].astype(F32)
            return unused

        lax.fori_loop(0, count, move, 0)
        first += count


def store_blocks(order, flat, blocks, owner_rows, first_row):
    count, rows, unused = blocks.shape

    def move(index, unused):
        start = pl.multiple_of(order[index] * owner_rows + first_row, 8)
        blocks[index] = flat[pl.ds(start, rows), :].astype(BF16)
        return unused

    lax.fori_loop(0, count, move, 0)


def planes_to_matrix(planes, whole, matrix):
    for j in range(whole):
        matrix[:, j * LANES : (j + 1) * LANES] = planes[j].astype(BF16)
    matrix[:, whole * LANES : whole * LANES + HALF] = planes[whole, :, :HALF].astype(BF16)


def rotated(rows, cosine, sine):
    half_width = HEAD_SIZE // 2
    first, second = rows[:half_width], rows[half_width:]
    return jnp.concatenate([first * cosine - second * sine, second * cosine + first * sine], 0)


def attention_forward_kernel(
    order,
    weights_near,
    weights_far,
    inputs_near,
    inputs_far,
    cosines,
    sines,
    bias,
    gains,
    w_project,
    w_output,
    normed,
    queries,
    keys_across,
    keys,
    values,
    log_totals,
    mixed_across,
    residual,
    flat,
    planes_one,
    planes_two,
    w_across,
    values_across,
):
    load_blocks(order, (weights_near, weights_far), flat)
    unflatten_odd(flat, 0, D // 2, 7, planes_one)
    planes_to_matrix(planes_one, 7, w_project)
    for j in range(7):
        w_across[j * LANES : (j + 1) * LANES, :] = jnp.transpose(planes_one[j]).astype(BF16)
    w_across[7 * LANES :, :] = jnp.transpose(planes_one[7])[:HALF].astype(BF16)
    unflatten_odd(flat, D * QKV_WIDTH // LANES, QUERY_WIDTH // 2, 4, planes_two)
    planes_to_matrix(planes_two, 4, w_output)
    near_count = inputs_near.shape[0]
    blocks = near_count + inputs_far.shape[0]
    gain = gains[0:1, :]

    def one(micro, unused):
        for block in range(blocks):
            if block < near_count:
                rows = inputs_near[block, micro].astype(F32)
            else:
                rows = inputs_far[block - near_count, micro].astype(F32)
            inverse = lax.rsqrt(jnp.mean(rows * rows, axis=-1, keepdims=True) + NORM_EPSILON)
            normed[micro, block * DEVICE_TOKENS : (block + 1) * DEVICE_TOKENS, :] = (
                rows * inverse * gain
            ).astype(BF16)
        cosine, sine = cosines[micro], sines[micro]
        own_cosine, own_sine = cosine[:, :DEVICE_TOKENS], sine[:, :DEVICE_TOKENS]
        query = dot_nt(w_across[:QUERY_WIDTH, :], normed[micro, :DEVICE_TOKENS, :])
        for head in range(QUERY_HEADS):
            rows = slice(head * HEAD_SIZE, (head + 1) * HEAD_SIZE)
            queries[micro, rows, :] = rotated(query[rows], own_cosine, own_sine).astype(BF16)
        other = dot_nt(w_across[QUERY_WIDTH:, :], normed[micro])
        for head in range(KEY_VALUE_HEADS):
            rows = slice(head * HEAD_SIZE, (head + 1) * HEAD_SIZE)
            key = rotated(other[rows], cosine, sine)
            keys_across[micro, rows, :] = key.astype(BF16)
            keys[micro, head] = jnp.transpose(key).astype(BF16)
            value = other[KV_WIDTH + head * HEAD_SIZE : KV_WIDTH + (head + 1) * HEAD_SIZE]
            values_across[rows, :] = value.astype(BF16)
            values[micro, head] = jnp.transpose(value).astype(BF16)
        for head in range(QUERY_HEADS):
            group = head // GROUP
            rows = slice(head * HEAD_SIZE, (head + 1) * HEAD_SIZE)
            group_rows = slice(group * HEAD_SIZE, (group + 1) * HEAD_SIZE)
            scores = dot(keys[micro, group], queries[micro, rows, :] * SCALE) + bias[micro]
            top = jnp.max(scores, axis=0, keepdims=True)
            weights = jnp.exp(scores - top)
            total = jnp.sum(weights, axis=0, keepdims=True)
            low = (weights * (1.0 / total)).astype(BF16)
            mixed_across[micro, rows, :] = dot(values_across[group_rows, :], low)
            log_totals[micro, head : head + 1, :] = top + jnp.log(total)
        mixed = jnp.transpose(mixed_across[micro]).astype(BF16)
        residual[micro] = inputs_near[0, micro].astype(F32) + dot(mixed, w_output[...])
        return unused

    lax.fori_loop(0, MICRO, one, 0)


def attention_forward(order, weight_halves, input_halves, *tables):
    window = sum(half.shape[0] for half in input_halves) * DEVICE_TOKENS
    shape = jax.ShapeDtypeStruct
    rows = sum(half.shape[0] * half.shape[1] for half in weight_halves)
    return pl.pallas_call(
        attention_forward_kernel,
        out_shape=(
            shape((D, QKV_WIDTH), BF16),
            shape((QUERY_WIDTH, D), BF16),
            shape((MICRO, window, D), BF16),
            shape((MICRO, QUERY_WIDTH, DEVICE_TOKENS), BF16),
            shape((MICRO, KV_WIDTH, window), BF16),
            shape((MICRO, KEY_VALUE_HEADS, window, HEAD_SIZE), BF16),
            shape((MICRO, KEY_VALUE_HEADS, window, HEAD_SIZE), BF16),
            shape((MICRO, QUERY_HEADS, DEVICE_TOKENS), F32),
            shape((MICRO, QUERY_WIDTH, DEVICE_TOKENS), F32),
            shape((MICRO, DEVICE_TOKENS, D), F32),
        ),
        in_specs=[smem()] + vmem(4 + len(tables)),
        out_specs=tuple(vmem(10)),
        scratch_shapes=[
            pltpu.VMEM((rows, LANES), F32),
            pltpu.VMEM((8, D, LANES), F32),
            pltpu.VMEM((5, QUERY_WIDTH, LANES), F32),
            pltpu.VMEM((QKV_WIDTH, D), BF16),
            pltpu.VMEM((KV_WIDTH, window), BF16),
        ],
        compiler_params=params(),
    )(order, *weight_halves, *input_halves, *tables)


def feedforward_kernel(
    straight,
    order_two,
    order_three,
    weight_blocks,
    residual,
    cotangent,
    gains,
    block_output,
    d_residual,
    grads_one,
    grads_two,
    grads_three,
    gain_grad,
    flat,
    planes,
    w_gate_up,
    w_down,
    hidden,
    d_gate_up,
):
    columns = 2 * FF // LANES
    load_blocks(straight, (weight_blocks,), flat)
    for j in range(columns):
        w_gate_up[:, j * LANES : (j + 1) * LANES] = flat[
            pl.ds(j, D, stride=columns), :
        ].astype(BF16)
    unflatten_odd(flat, D * columns, FF // 2, 4, planes)
    planes_to_matrix(planes, 4, w_down)
    gain = gains[1:2, :]
    rows = residual[...]
    inverse = lax.rsqrt(jnp.mean(rows * rows, axis=-1, keepdims=True) + NORM_EPSILON)
    unit = rows * inverse
    normed = (unit * gain).astype(BF16)
    cotangent_low = cotangent[...]
    part = 256
    for start in range(0, FF, part):
        gate = dot(normed, w_gate_up[:, start : start + part])
        up = dot(normed, w_gate_up[:, FF + start : FF + start + part])
        d_hidden = dot_nt(cotangent_low, w_down[start : start + part, :])
        sigmoid = 1.0 / (1.0 + jnp.exp(-gate))
        activated = gate * sigmoid
        hidden[:, start : start + part] = (activated * up).astype(BF16)
        d_gate_up[:, start : start + part] = (
            d_hidden * up * sigmoid * (1.0 + gate * (1.0 - sigmoid))
        ).astype(BF16)
        d_gate_up[:, FF + start : FF + start + part] = (d_hidden * activated).astype(BF16)
    block_output[...] = (rows + dot(hidden[...], w_down[...])).astype(BF16)
    d_normed = dot_nt(d_gate_up[...], w_gate_up[...])
    scaled = d_normed * gain
    d_residual[...] = cotangent_low.astype(F32) + inverse * (
        scaled - unit * jnp.mean(scaled * unit, axis=-1, keepdims=True)
    )
    normed_across = jnp.transpose(unit * gain).astype(BF16)
    total = jnp.zeros((D, LANES), F32)
    for start in range(0, 2 * FF, part):
        grad = dot(normed_across, d_gate_up[:, start : start + part])
        for offset in range(0, part, LANES):
            piece = grad[:, offset : offset + LANES]
            place = start + offset
            total = total + piece * w_gate_up[:, place : place + LANES].astype(F32)
            flat[pl.ds(place // LANES, D, stride=columns), :] = piece
    gain_grad[...] = jnp.sum(total, axis=1, keepdims=True)
    for start in range(0, FF, part):
        grad = dot_tn(hidden[:, start : start + part], cotangent_low)
        for j in range(4):
            planes[j, start : start + part, :] = grad[:, j * LANES : (j + 1) * LANES]
        planes[4, start : start + part, :HALF] = grad[:, 4 * LANES :]
    flatten_odd(planes, FF // 2, 4, flat, D * columns)
    owner_rows = weight_blocks.shape[1]
    first_row = 0
    for order, blocks in (
        (straight, grads_one),
        (order_two, grads_two),
        (order_three, grads_three),
    ):
        store_blocks(order, flat, blocks, owner_rows, first_row)
        first_row += blocks.shape[1]


def feedforward(orders, weight_blocks, residual, cotangent, gains):
    shape = jax.ShapeDtypeStruct
    part = shape((weight_blocks.shape[0], weight_blocks.shape[1] // 3, LANES), BF16)
    tokens = residual.shape[0]
    rows = weight_blocks.shape[0] * weight_blocks.shape[1]
    return pl.pallas_call(
        feedforward_kernel,
        out_shape=(
            shape((tokens, D), BF16),
            shape((tokens, D), F32),
            part,
            part,
            part,
            shape((D, 1), F32),
        ),
        in_specs=[smem()] * 3 + vmem(4),
        out_specs=tuple(vmem(6)),
        scratch_shapes=[
            pltpu.VMEM((rows, LANES), F32),
            pltpu.VMEM((5, FF, LANES), F32),
            pltpu.VMEM((D, 2 * FF), BF16),
            pltpu.VMEM((FF, D), BF16),
            pltpu.VMEM((tokens, FF), BF16),
            pltpu.VMEM((tokens, 2 * FF), BF16),
        ],
        compiler_params=params(),
    )(*orders, weight_blocks, residual, cotangent, gains)


def attention_backward_body(
    w_output,
    normed,
    queries,
    keys_across,
    keys,
    values,
    log_totals,
    mixed_across,
    d_residual,
    cosines,
    sines,
    bias,
    d_queries,
    d_window,
    d_window_across,
    grad_across,
    grad_output,
    d_mixed,
):
    blocks = d_window.shape[0]
    cosine, sine = cosines[...], sines[...]
    own_cosine, own_sine = cosine[:, :DEVICE_TOKENS], sine[:, :DEVICE_TOKENS]
    d_branch = d_residual[...].astype(BF16)
    d_mixed[...] = dot_nt(w_output[...], d_branch).astype(BF16)

    def one(group, unused):
        group_rows = pl.ds(pl.multiple_of(group * HEAD_SIZE, HEAD_SIZE), HEAD_SIZE)
        value_rows = pl.ds(pl.multiple_of(KV_WIDTH + group * HEAD_SIZE, HEAD_SIZE), HEAD_SIZE)
        d_key = d_value = jnp.zeros((HEAD_SIZE, cosine.shape[1]), F32)
        for offset in range(GROUP):
            head = group * GROUP + offset
            rows = pl.ds(pl.multiple_of(head * HEAD_SIZE, HEAD_SIZE), HEAD_SIZE)
            query = queries[rows, :] * SCALE
            d_mixed_head = d_mixed[rows, :]
            delta = jnp.sum(
                d_mixed_head.astype(F32) * mixed_across[rows, :], axis=0, keepdims=True
            )
            scores = dot(keys[group], query) + bias[...]
            probability = jnp.exp(scores - log_totals[pl.ds(head, 1), :])
            d_probs = dot(values[group], d_mixed_head)
            d_scores = (probability * (d_probs - delta)).astype(BF16)
            d_query = dot(keys_across[group_rows, :], d_scores) * SCALE
            d_queries[rows, :] = rotated(d_query, own_cosine, -own_sine).astype(BF16)
            d_key = d_key + dot_nt(query, d_scores)
            d_value = d_value + dot_nt(d_mixed_head, probability.astype(BF16))
        d_window_across[group_rows, :] = rotated(d_key, cosine, -sine).astype(BF16)
        d_window_across[value_rows, :] = d_value.astype(BF16)
        return unused

    lax.fori_loop(0, KEY_VALUE_HEADS, one, 0)
    for block in range(blocks):
        d_window[block] = d_window_across[
            :, block * DEVICE_TOKENS : (block + 1) * DEVICE_TOKENS
        ]
    query_grad = dot(d_queries[...], normed[:DEVICE_TOKENS, :])
    window_grad = dot(d_window_across[...], normed[...])
    output_grad = dot(mixed_across[...].astype(BF16), d_branch)
    grad_across[:QUERY_WIDTH, :] = query_grad
    grad_across[QUERY_WIDTH:, :] = window_grad
    grad_output[...] = output_grad


def attention_backward_first(*refs):
    operands, (d_queries, d_window, grad_across, grad_output, across, d_mixed) = (
        refs[:12],
        refs[12:],
    )
    attention_backward_body(
        *operands, d_queries, d_window, across, grad_across, grad_output, d_mixed
    )


def attention_backward_second(order, w_project, first_across, first_output, *refs):
    operands, (grad_blocks, d_queries, d_window, gain_grad) = refs[:12], refs[12:16]
    flat, planes, across, d_mixed, grad_across, grad_output = refs[16:]
    attention_backward_body(
        *operands, d_queries, d_window, across, grad_across, grad_output, d_mixed
    )
    grad_across[...] += first_across[...]
    grad_output[...] += first_output[...]
    total = jnp.zeros((D, LANES), F32)
    for j in range(7):
        piece = jnp.transpose(grad_across[j * LANES : (j + 1) * LANES, :])
        planes[j] = piece
        total = total + piece * w_project[:, j * LANES : (j + 1) * LANES].astype(F32)
    last = jnp.transpose(grad_across[QKV_WIDTH - LANES :, :])
    last = pltpu.roll(last, HALF, 1)
    planes[7] = last
    last_sum = last[:, :HALF] * w_project[:, 7 * LANES :].astype(F32)
    gain_grad[...] = jnp.sum(total, axis=1, keepdims=True) + jnp.sum(
        last_sum, axis=1, keepdims=True
    )
    flatten_odd(planes, D // 2, 7, flat, 0)
    for j in range(4):
        planes[j] = grad_output[:, j * LANES : (j + 1) * LANES]
    planes[4, :, :HALF] = grad_output[:, 4 * LANES :]
    flatten_odd(planes, QUERY_WIDTH // 2, 4, flat, D * QKV_WIDTH // LANES)
    store_blocks(order, flat, grad_blocks, grad_blocks.shape[1], 0)


def attention_backward(operands, count, rows, final=()):
    shape = jax.ShapeDtypeStruct
    window = operands[1].shape[0]
    outputs = (
        shape((QUERY_WIDTH, DEVICE_TOKENS), BF16),
        shape((window // DEVICE_TOKENS, 2 * KV_WIDTH, DEVICE_TOKENS), BF16),
    )
    sums = [(QKV_WIDTH, D), (QUERY_WIDTH, D)]
    scratch = [
        pltpu.VMEM((2 * KV_WIDTH, window), BF16),
        pltpu.VMEM((QUERY_WIDTH, DEVICE_TOKENS), BF16),
    ]
    if final:
        kernel = attention_backward_second
        outputs = (shape((count, rows, LANES), BF16), *outputs, shape((D, 1), F32))
        scratch = [
            pltpu.VMEM((count * rows, LANES), F32),
            pltpu.VMEM((8, D, LANES), F32),
            *scratch,
            *[pltpu.VMEM(dims, F32) for dims in sums],
        ]
        in_specs = [smem()] + vmem(len(final) - 1 + len(operands))
    else:
        kernel = attention_backward_first
        outputs = (*outputs, *[shape(dims, F32) for dims in sums])
        in_specs = vmem(len(operands))
    return pl.pallas_call(
        kernel,
        out_shape=outputs,
        in_specs=in_specs,
        out_specs=tuple(vmem(len(outputs))),
        scratch_shapes=scratch,
        compiler_params=params(),
    )(*final, *operands)


def adam_update(weights, moment, square, grad, rate, decay):
    new_moment = BETA_ONE * moment + (1.0 - BETA_ONE) * grad
    new_square = BETA_TWO * square + (1.0 - BETA_TWO) * grad * grad
    mean_hat = new_moment / (1.0 - BETA_ONE**STEP)
    square_hat = new_square / (1.0 - BETA_TWO**STEP)
    new_weights = weights - rate * (
        mean_hat / (jnp.sqrt(square_hat) + ADAM_EPSILON) + decay * weights
    )
    return (new_weights, new_moment, new_square)


def first_of(lengths, index):
    starts = jnp.cumsum(lengths, axis=-1) - lengths
    return jnp.max(
        jnp.where(starts[:, None, :] <= index[None, :, None], starts[:, None, :], 0), axis=-1
    )


def on_device(
    block_input,
    out_grad,
    doc_lengths,
    attention_weights,
    feedforward_weights,
    norm_gains,
    attention_moment,
    attention_square,
    feedforward_moment,
    feedforward_square,
    gain_moment,
    gain_square,
):
    both = ("dp", "seq")
    seq_count = lax.axis_size("seq")
    owner_count = lax.axis_size(both)
    seq_place = lax.axis_index("seq")
    owner_place = lax.axis_index(both)
    attention_length = attention_weights.shape[0]
    feedforward_length = feedforward_weights.shape[0]
    reach = min((DOC_MAX + DEVICE_TOKENS - 2) // DEVICE_TOKENS, seq_count - 1)
    paired = is_power_of_two(seq_count) and reach == seq_count - 1
    butterfly = is_power_of_two(owner_count) and attention_length % (8 * LANES) == 0
    stages = gather_stages()
    order = block_order(stages)
    seq_stages = [stage for stage in stages if stage[0] == "seq"]

    own_inputs = block_input[:, 0]
    straight = jnp.arange(BLOCKS, dtype=jnp.int32)
    tiled_rows = feedforward_length % (8 * LANES) == 0
    feedforward_low = feedforward_weights.astype(BF16)
    if tiled_rows:
        feedforward_low = feedforward_low.reshape(-1, LANES)
    feedforward_blocks = lax.all_gather(feedforward_low, both, axis=0, tiled=True)
    feedforward_blocks = feedforward_blocks.reshape(BLOCKS, -1, LANES)

    if paired:
        window_blocks = seq_place ^ jnp.array(block_order(seq_stages), jnp.int32)
    else:
        window_blocks = seq_place - jnp.arange(reach + 1, dtype=jnp.int32)
    token = jnp.arange(DEVICE_TOKENS, dtype=jnp.int32)
    query_index = seq_place * DEVICE_TOKENS + token
    key_index = (window_blocks[:, None] * DEVICE_TOKENS + token[None, :]).reshape(-1)
    lengths = doc_lengths[:, 0]
    first_query = first_of(lengths, query_index)
    first_key = first_of(lengths, key_index)
    half_width = HEAD_SIZE // 2
    inverse = THETA ** (-(jnp.arange(half_width, dtype=F32) * 2.0) / HEAD_SIZE)
    position = (key_index[None] - first_key).astype(F32)
    angles = position[:, None, :] * inverse[None, :, None]
    cosines, sines = jnp.cos(angles), jnp.sin(angles)
    allowed = (key_index[None, :, None] >= first_query[:, None, :]) & (
        key_index[None, :, None] <= query_index[None, None, :]
    )
    bias = jnp.where(allowed, 0.0, -jnp.inf).astype(F32)

    attention_low = attention_weights.astype(BF16)
    if butterfly:
        orders = [
            jnp.array(block_order(path), jnp.int32) ^ owner_place
            for path in (stages, swap_dp(stages))
        ]
    else:
        orders = [straight, straight]
    if butterfly and paired:
        weights = attention_low.reshape(1, attention_length // LANES, LANES)
        window_inputs = own_inputs[None]
        for index, (axis, bit, unused_flat) in enumerate(stages):
            far = exchange(weights, axis, bit)
            if index < len(seq_stages):
                other_axis, other_bit, unused_flat = seq_stages[index]
                inputs_far = exchange(window_inputs, other_axis, other_bit)
                far, inputs_far = together(far, inputs_far)
                if index == 0:
                    far, cosines, sines, bias = together(far, cosines, sines, bias)
                if index < len(seq_stages) - 1:
                    window_inputs = jnp.concatenate([window_inputs, inputs_far], 0)
            if index < len(stages) - 1:
                weights = jnp.concatenate([weights, far], 0)
        weight_halves = (weights, far)
        input_halves = (window_inputs, inputs_far)
    else:
        weights = lax.all_gather(attention_low, both, axis=0, tiled=True)
        weights = weights.reshape(BLOCKS, -1, LANES)
        weight_halves = (weights[: BLOCKS // 2], weights[BLOCKS // 2 :])
        window_inputs = jnp.stack(
            [own_inputs]
            + [
                lax.ppermute(
                    own_inputs, "seq", [(p, p + step) for p in range(seq_count - step)]
                )
                for step in range(1, reach + 1)
            ],
            0,
        )
        middle = (reach + 1) // 2
        input_halves = (window_inputs[:middle], window_inputs[middle:])
        orders = [straight, straight]

    (
        w_project,
        w_output,
        normed_one,
        queries,
        keys_across,
        keys,
        values,
        log_totals,
        mixed_across,
        residual,
    ) = attention_forward(
        orders[0], weight_halves, input_halves, cosines, sines, bias, norm_gains
    )
    block_output, d_residual, part_one, part_two, part_three, gain_two = feedforward(
        (straight, *orders),
        feedforward_blocks,
        residual.reshape(-1, D),
        out_grad[:, 0].reshape(-1, D),
        norm_gains,
    )
    block_output = block_output.reshape(MICRO, DEVICE_TOKENS, D)
    d_residual = d_residual.reshape(MICRO, DEVICE_TOKENS, D)

    def operands_of(micro):
        return (
            w_output,
            normed_one[micro],
            queries[micro],
            keys_across[micro],
            keys[micro],
            values[micro],
            log_totals[micro],
            mixed_across[micro],
            d_residual[micro],
            cosines[micro],
            sines[micro],
            bias[micro],
        )

    attention_rows = D * (QKV_WIDTH + QUERY_WIDTH) // (LANES * BLOCKS)
    if butterfly and paired:
        paths = [stages[::-1], swap_dp(stages)[::-1]]
        halving_seq = seq_stages[::-1]
        owned_one = lax.psum_scatter(
            part_one.reshape(-1, LANES), both, scatter_dimension=0, tiled=True
        )
        received = [send_half(p, path[0]) for p, path in zip((part_two, part_three), paths)]
        first = attention_backward(operands_of(0), BLOCKS, attention_rows)
        received = together(*received, *first)
        first = received[2:]
        parts = [halve_step(part_two, received[0]), halve_step(part_three, received[1])]
        first_across, *parts = together(first[2], *parts)
        received = [send_half(p, path[1]) for p, path in zip(parts, paths)]
        second = attention_backward(
            operands_of(1),
            BLOCKS,
            attention_rows,
            (orders[0], w_project, first_across, first[3]),
        )
        received = together(*received, *second)
        attention_grads, d_queries_two, d_window_two, gain_one = received[2:]
        parts = [halve_step(p, r) for p, r in zip(parts, received)]
        d_queries = jnp.stack([first[0], d_queries_two], 0)
        d_window = jnp.stack([first[1], d_window_two], 1)
        gains_total = jnp.stack([gain_one[:, 0], gain_two[:, 0]], 0) / norm_gains
        for index, stage in enumerate(paths[0]):
            arrivals = {
                "attention": send_half(attention_grads, stage),
                "gains": exchange(gains_total, stage[0], stage[1]),
            }
            if index + 2 < len(paths[0]):
                arrivals["two"] = send_half(parts[0], paths[0][index + 2])
                arrivals["three"] = send_half(parts[1], paths[1][index + 2])
            if index < len(halving_seq):
                arrivals["window"] = send_half(d_window, halving_seq[index])
            arrivals = lax.optimization_barrier(arrivals)
            attention_grads = halve_step(attention_grads, arrivals["attention"])
            gains_total = gains_total + arrivals["gains"]
            if "two" in arrivals:
                parts = [
                    halve_step(parts[0], arrivals["two"]),
                    halve_step(parts[1], arrivals["three"]),
                ]
            if "window" in arrivals:
                d_window = halve_step(d_window, arrivals["window"])
        attention_owned = attention_grads.reshape(-1)
        d_own = d_window[0]
        feedforward_owned = jnp.concatenate(
            [owned_one, parts[0][0], parts[1][0]], 0
        ).reshape(-1)
    else:
        grads = jnp.concatenate([part_one, part_two, part_three], 1).reshape(-1)
        feedforward_owned = lax.psum_scatter(grads, both, scatter_dimension=0, tiled=True)
        first = attention_backward(operands_of(0), BLOCKS, attention_rows)
        attention_grads, d_queries_two, d_window_two, gain_one = attention_backward(
            operands_of(1), BLOCKS, attention_rows, (orders[0], w_project, first[2], first[3])
        )
        attention_owned = lax.psum_scatter(
            attention_grads.reshape(-1), both, scatter_dimension=0, tiled=True
        )
        d_queries = jnp.stack([first[0], d_queries_two], 0)
        d_window = jnp.stack([first[1], d_window_two], 1)
        d_own = d_window[0].astype(F32)
        for step in range(1, reach + 1):
            d_own = d_own + lax.ppermute(
                d_window[step], "seq", [(p, p - step) for p in range(step, seq_count)]
            ).astype(F32)
        d_own = d_own.astype(BF16)
        gains_total = jnp.stack([gain_one[:, 0], gain_two[:, 0]], 0) / norm_gains
        gains_total = lax.psum(gains_total, both)
    d_normed_one = matmul("met,de->mtd", jnp.concatenate([d_queries, d_own], 1), w_project)
    unit_one, inverse_one = unit_norm(own_inputs.astype(F32))
    input_grad = d_residual + norm_backward(d_normed_one, unit_one, inverse_one, norm_gains[0])

    attention_place = owner_place * attention_length + jnp.arange(attention_length, dtype=jnp.int32)
    attention_rate = jnp.where(
        attention_place < D * QKV_WIDTH, RATE_FACTOR * D ** (-0.5), RATE_FACTOR * OUT_FAN ** (-0.5)
    )
    feedforward_place = owner_place * feedforward_length + jnp.arange(
        feedforward_length, dtype=jnp.int32
    )
    feedforward_rate = jnp.where(
        feedforward_place < 2 * D * FF, RATE_FACTOR * D ** (-0.5), RATE_FACTOR * FF ** (-0.5)
    )
    new_attention = adam_update(
        attention_weights,
        attention_moment,
        attention_square,
        attention_owned.astype(F32),
        attention_rate,
        MATRIX_DECAY,
    )
    new_feedforward = adam_update(
        feedforward_weights,
        feedforward_moment,
        feedforward_square,
        feedforward_owned.astype(F32),
        feedforward_rate,
        MATRIX_DECAY,
    )
    new_gains = adam_update(norm_gains, gain_moment, gain_square, gains_total, GAIN_RATE, 0.0)
    return (
        block_output[:, None],
        input_grad[:, None],
        *new_attention,
        *new_feedforward,
        *new_gains,
    )


def solution(mesh):
    tokens = P(None, "dp", "seq", None)
    flat = P(("dp", "seq"))
    return jax.shard_map(
        on_device,
        mesh=mesh,
        in_specs=(
            tokens,
            tokens,
            P(None, "dp", None),
            flat,
            flat,
            P(),
            flat,
            flat,
            flat,
            flat,
            P(),
            P(),
        ),
        out_specs=(tokens, tokens, flat, flat, flat, flat, flat, flat, P(), P(), P()),
        check_vma=False,
    )
```

```python
import jax
import jax.numpy as jnp
from jax import lax
from jax.experimental import pallas as pl
from jax.experimental.pallas import tpu as pltpu
from jax.sharding import PartitionSpec as P

D = 576
QUERY_HEADS = 9
KEY_VALUE_HEADS = 3
GROUP = QUERY_HEADS // KEY_VALUE_HEADS
HEAD_SIZE = 64
FF = 1536
DEVICE_TOKENS = 128
MICRO = 2
DOC_MAX = 1000
STEP = 10
QKV_WIDTH = 960
QUERY_WIDTH = QUERY_HEADS * HEAD_SIZE
KV_WIDTH = KEY_VALUE_HEADS * HEAD_SIZE
OUT_FAN = 14
LANES = 128
HALF = LANES // 2
BLOCKS = 32
VMEM_LIMIT = 52 * 2**20

NORM_EPSILON = 1e-05
THETA = 100000.0
BETA_ONE = 0.9
BETA_TWO = 0.95
ADAM_EPSILON = 1e-08
MATRIX_DECAY = 0.1
RATE_FACTOR = 1.5
GAIN_RATE = 0.2
SCALE = HEAD_SIZE ** (-0.5)
BF16 = jnp.bfloat16
F32 = jnp.float32


def is_power_of_two(count):
    return count & (count - 1) == 0


def exchange(value, axis, bit):
    count = lax.axis_size(axis)
    return lax.ppermute(value, axis, [(place, place ^ bit) for place in range(count)])


def gather_stages():
    seq, dp = lax.axis_size("seq"), lax.axis_size("dp")
    stages = []
    bit = seq // 2
    while bit > 1:
        stages.append(("seq", bit, bit))
        bit //= 2
    bit = dp // 2
    while bit >= 1:
        stages.append(("dp", bit, bit * seq))
        bit //= 2
    if seq > 1:
        stages.append(("seq", 1, 1))
    return stages


def block_order(stages):
    order = [0]
    for unused_axis, unused_bit, flat_bit in stages:
        order = order + [place ^ flat_bit for place in order]
    return order


def swap_dp(stages):
    turned = iter([stage for stage in reversed(stages) if stage[0] == "dp"])
    return [next(turned) if stage[0] == "dp" else stage for stage in stages]


def halve_step(kept, received):
    half = kept.shape[0] // 2
    kept, received = kept.astype(F32), received.astype(F32)
    if half == 0:
        return (kept + received, None)
    return (
        (kept[:half] + received[:half]).astype(BF16),
        (kept[half:] + received[half:]).astype(BF16),
    )


def together(*values):
    return lax.optimization_barrier(values)


def unit_norm(inputs):
    inverse_rms = lax.rsqrt(jnp.mean(inputs * inputs, axis=-1, keepdims=True) + NORM_EPSILON)
    return (inputs * inverse_rms, inverse_rms)


def norm_backward(d_normed, unit_rows, inverse_rms, gain_row):
    scaled = d_normed * gain_row
    return inverse_rms * (
        scaled - unit_rows * jnp.mean(scaled * unit_rows, axis=-1, keepdims=True)
    )


def matmul(equation, left, right):
    return jnp.einsum(equation, left, right, preferred_element_type=F32)


def params():
    return pltpu.CompilerParams(vmem_limit_bytes=VMEM_LIMIT)


def vmem(count):
    return [pl.BlockSpec(memory_space=pltpu.VMEM)] * count


def smem():
    return pl.BlockSpec(memory_space=pltpu.SMEM)


def dot(left, right):
    return jnp.dot(left, right, preferred_element_type=F32)


def dot_nt(left, right):
    return lax.dot_general(left, right, (((1,), (1,)), ((), ())), preferred_element_type=F32)


def dot_tn(left, right):
    return lax.dot_general(left, right, (((0,), (0,)), ((), ())), preferred_element_type=F32)


def shift_half(low, high):
    lane = lax.broadcasted_iota(jnp.int32, low.shape, 1)
    return pltpu.roll(jnp.where(lane < HALF, low, high), HALF, 1)


def unflatten_odd(flat, base, pairs, whole, planes):
    step = 2 * whole + 1

    def piece(k):
        return flat[pl.ds(base + k, pairs, stride=step), :]

    for j in range(whole + 1):
        planes[j, pl.ds(0, pairs, stride=2), :] = piece(j)
        planes[j, pl.ds(1, pairs, stride=2), :] = shift_half(
            piece(min(whole + 1 + j, 2 * whole)), piece(whole + j)
        )


def flatten_odd(planes, pairs, whole, flat, base):
    step = 2 * whole + 1

    def even(j):
        return planes[j, pl.ds(0, pairs, stride=2), :]

    def odd(j):
        return planes[j, pl.ds(1, pairs, stride=2), :]

    for k in range(step):
        if k < whole:
            rows = even(k)
        elif k == whole:
            first = odd(0)
            lane = lax.broadcasted_iota(jnp.int32, first.shape, 1)
            rows = jnp.where(lane < HALF, even(whole), pltpu.roll(first, HALF, 1))
        else:
            rows = shift_half(odd(k - whole), odd(k - whole - 1))
        flat[pl.ds(base + k, pairs, stride=step), :] = rows


def load_blocks(order, halves, flat):
    first = 0
    for blocks in halves:
        count, rows, unused = blocks.shape

        def move(place, unused, blocks=blocks, rows=rows, first=first):
            start = pl.multiple_of(order[first + place] * rows, 8)
            flat[pl.ds(start, rows), :] = blocks[place].astype(F32)
            return unused

        lax.fori_loop(0, count, move, 0)
        first += count


def store_blocks(order, flat, blocks, owner_rows, first_row, first_index):
    count, rows, unused = blocks.shape

    def move(index, unused):
        start = pl.multiple_of(order[first_index + index] * owner_rows + first_row, 8)
        blocks[index] = flat[pl.ds(start, rows), :].astype(BF16)
        return unused

    lax.fori_loop(0, count, move, 0)


def planes_to_matrix(planes, whole, matrix):
    for j in range(whole):
        matrix[:, j * LANES : (j + 1) * LANES] = planes[j].astype(BF16)
    matrix[:, whole * LANES : whole * LANES + HALF] = planes[whole, :, :HALF].astype(BF16)


def rotated(rows, cosine, sine):
    half_width = HEAD_SIZE // 2
    first, second = rows[:half_width], rows[half_width:]
    return jnp.concatenate([first * cosine - second * sine, second * cosine + first * sine], 0)


def attention_forward_kernel(order, *refs):
    weight_pieces, input_pieces, refs = refs[:4], refs[4:8], refs[8:]
    cosines, sines, bias, gains, w_project, w_output, normed, queries = refs[:8]
    keys_across, keys, values, log_totals, mixed_across, residual = refs[8:14]
    flat, planes_one, planes_two, w_across, values_across = refs[14:]
    load_blocks(order, weight_pieces, flat)
    unflatten_odd(flat, 0, D // 2, 7, planes_one)
    planes_to_matrix(planes_one, 7, w_project)
    for j in range(7):
        w_across[j * LANES : (j + 1) * LANES, :] = jnp.transpose(planes_one[j]).astype(BF16)
    w_across[7 * LANES :, :] = jnp.transpose(planes_one[7])[:HALF].astype(BF16)
    unflatten_odd(flat, D * QKV_WIDTH // LANES, QUERY_WIDTH // 2, 4, planes_two)
    planes_to_matrix(planes_two, 4, w_output)
    blocks = [piece.at[place] for piece in input_pieces for place in range(piece.shape[0])]
    gain = gains[0:1, :]

    def one(micro, unused):
        for block, inputs in enumerate(blocks):
            rows = inputs[micro].astype(F32)
            inverse = lax.rsqrt(jnp.mean(rows * rows, axis=-1, keepdims=True) + NORM_EPSILON)
            normed[micro, block * DEVICE_TOKENS : (block + 1) * DEVICE_TOKENS, :] = (
                rows * inverse * gain
            ).astype(BF16)
        cosine, sine = cosines[micro], sines[micro]
        own_cosine, own_sine = cosine[:, :DEVICE_TOKENS], sine[:, :DEVICE_TOKENS]
        query = dot_nt(w_across[:QUERY_WIDTH, :], normed[micro, :DEVICE_TOKENS, :])
        for head in range(QUERY_HEADS):
            rows = slice(head * HEAD_SIZE, (head + 1) * HEAD_SIZE)
            queries[micro, rows, :] = rotated(query[rows], own_cosine, own_sine).astype(BF16)
        other = dot_nt(w_across[QUERY_WIDTH:, :], normed[micro])
        for head in range(KEY_VALUE_HEADS):
            rows = slice(head * HEAD_SIZE, (head + 1) * HEAD_SIZE)
            key = rotated(other[rows], cosine, sine)
            keys_across[micro, rows, :] = key.astype(BF16)
            keys[micro, head] = jnp.transpose(key).astype(BF16)
            value = other[KV_WIDTH + head * HEAD_SIZE : KV_WIDTH + (head + 1) * HEAD_SIZE]
            values_across[rows, :] = value.astype(BF16)
            values[micro, head] = jnp.transpose(value).astype(BF16)
        for head in range(QUERY_HEADS):
            group = head // GROUP
            rows = slice(head * HEAD_SIZE, (head + 1) * HEAD_SIZE)
            group_rows = slice(group * HEAD_SIZE, (group + 1) * HEAD_SIZE)
            scores = dot(keys[micro, group], queries[micro, rows, :] * SCALE) + bias[micro]
            top = jnp.max(scores, axis=0, keepdims=True)
            weights = jnp.exp(scores - top)
            total = jnp.sum(weights, axis=0, keepdims=True)
            low = (weights * (1.0 / total)).astype(BF16)
            mixed_across[micro, rows, :] = dot(values_across[group_rows, :], low)
            log_totals[micro, head : head + 1, :] = top + jnp.log(total)
        mixed = jnp.transpose(mixed_across[micro]).astype(BF16)
        residual[micro] = blocks[0][micro].astype(F32) + dot(mixed, w_output[...])
        return unused

    lax.fori_loop(0, MICRO, one, 0)


def attention_forward(order, weight_pieces, input_pieces, *tables):
    window = sum(piece.shape[0] for piece in input_pieces) * DEVICE_TOKENS
    shape = jax.ShapeDtypeStruct
    rows = sum(piece.shape[0] * piece.shape[1] for piece in weight_pieces)
    return pl.pallas_call(
        attention_forward_kernel,
        out_shape=(
            shape((D, QKV_WIDTH), BF16),
            shape((QUERY_WIDTH, D), BF16),
            shape((MICRO, window, D), BF16),
            shape((MICRO, QUERY_WIDTH, DEVICE_TOKENS), BF16),
            shape((MICRO, KV_WIDTH, window), BF16),
            shape((MICRO, KEY_VALUE_HEADS, window, HEAD_SIZE), BF16),
            shape((MICRO, KEY_VALUE_HEADS, window, HEAD_SIZE), BF16),
            shape((MICRO, QUERY_HEADS, DEVICE_TOKENS), F32),
            shape((MICRO, QUERY_WIDTH, DEVICE_TOKENS), F32),
            shape((MICRO, DEVICE_TOKENS, D), F32),
        ),
        in_specs=[smem()] + vmem(8 + len(tables)),
        out_specs=tuple(vmem(10)),
        scratch_shapes=[
            pltpu.VMEM((rows, LANES), F32),
            pltpu.VMEM((8, D, LANES), F32),
            pltpu.VMEM((5, QUERY_WIDTH, LANES), F32),
            pltpu.VMEM((QKV_WIDTH, D), BF16),
            pltpu.VMEM((KV_WIDTH, window), BF16),
        ],
        compiler_params=params(),
    )(order, *weight_pieces, *input_pieces, *tables)


def feedforward_kernel(
    straight,
    order_one,
    order_two,
    weight_blocks,
    residual,
    cotangent,
    gains,
    block_output,
    d_residual,
    one_kept,
    one_sent,
    two_kept,
    two_sent,
    gain_grad,
    flat,
    planes,
    w_gate_up,
    w_down,
    hidden,
    d_gate_up,
):
    columns = 2 * FF // LANES
    load_blocks(straight, (weight_blocks,), flat)
    for j in range(columns):
        w_gate_up[:, j * LANES : (j + 1) * LANES] = flat[
            pl.ds(j, D, stride=columns), :
        ].astype(BF16)
    unflatten_odd(flat, D * columns, FF // 2, 4, planes)
    planes_to_matrix(planes, 4, w_down)
    gain = gains[1:2, :]
    rows = jnp.concatenate([residual[micro] for micro in range(MICRO)], 0)
    inverse = lax.rsqrt(jnp.mean(rows * rows, axis=-1, keepdims=True) + NORM_EPSILON)
    unit = rows * inverse
    normed = (unit * gain).astype(BF16)
    cotangent_low = jnp.concatenate([cotangent[micro, 0] for micro in range(MICRO)], 0)
    part = 256
    for start in range(0, FF, part):
        gate = dot(normed, w_gate_up[:, start : start + part])
        up = dot(normed, w_gate_up[:, FF + start : FF + start + part])
        d_hidden = dot_nt(cotangent_low, w_down[start : start + part, :])
        sigmoid = 1.0 / (1.0 + jnp.exp(-gate))
        activated = gate * sigmoid
        hidden[:, start : start + part] = (activated * up).astype(BF16)
        d_gate_up[:, start : start + part] = (
            d_hidden * up * sigmoid * (1.0 + gate * (1.0 - sigmoid))
        ).astype(BF16)
        d_gate_up[:, FF + start : FF + start + part] = (d_hidden * activated).astype(BF16)
    block_output[...] = (rows + dot(hidden[...], w_down[...])).astype(BF16)
    d_normed = dot_nt(d_gate_up[...], w_gate_up[...])
    scaled = d_normed * gain
    d_residual[...] = cotangent_low.astype(F32) + inverse * (
        scaled - unit * jnp.mean(scaled * unit, axis=-1, keepdims=True)
    )
    normed_across = jnp.transpose(unit * gain).astype(BF16)
    total = jnp.zeros((D, LANES), F32)
    for start in range(0, 2 * FF, part):
        grad = dot(normed_across, d_gate_up[:, start : start + part])
        for offset in range(0, part, LANES):
            piece = grad[:, offset : offset + LANES]
            place = start + offset
            total = total + piece * w_gate_up[:, place : place + LANES].astype(F32)
            flat[pl.ds(place // LANES, D, stride=columns), :] = piece
    gain_grad[...] = jnp.sum(total, axis=1, keepdims=True)
    for start in range(0, FF, part):
        grad = dot_tn(hidden[:, start : start + part], cotangent_low)
        for j in range(4):
            planes[j, start : start + part, :] = grad[:, j * LANES : (j + 1) * LANES]
        planes[4, start : start + part, :HALF] = grad[:, 4 * LANES :]
    flatten_odd(planes, FF // 2, 4, flat, D * columns)
    owner_rows = weight_blocks.shape[1]
    half = one_kept.shape[0]
    middle = one_kept.shape[1]
    store_blocks(order_one, flat, one_sent, owner_rows, 0, half)
    store_blocks(order_two, flat, two_sent, owner_rows, middle, half)
    store_blocks(order_one, flat, one_kept, owner_rows, 0, 0)
    store_blocks(order_two, flat, two_kept, owner_rows, middle, 0)


def feedforward(orders, weight_blocks, residual, cotangent, gains):
    shape = jax.ShapeDtypeStruct
    count, owner_rows, unused = weight_blocks.shape
    middle = owner_rows // 32 * 16
    one = shape((count // 2, middle, LANES), BF16)
    two = shape((count // 2, owner_rows - middle, LANES), BF16)
    tokens = residual.shape[0] * residual.shape[1]
    rows = weight_blocks.shape[0] * weight_blocks.shape[1]
    return pl.pallas_call(
        feedforward_kernel,
        out_shape=(
            shape((tokens, D), BF16),
            shape((tokens, D), F32),
            one,
            one,
            two,
            two,
            shape((D, 1), F32),
        ),
        in_specs=[smem()] * 3 + vmem(4),
        out_specs=tuple(vmem(7)),
        scratch_shapes=[
            pltpu.VMEM((rows, LANES), F32),
            pltpu.VMEM((5, FF, LANES), F32),
            pltpu.VMEM((D, 2 * FF), BF16),
            pltpu.VMEM((FF, D), BF16),
            pltpu.VMEM((tokens, FF), BF16),
            pltpu.VMEM((tokens, 2 * FF), BF16),
        ],
        compiler_params=params(),
    )(*orders, weight_blocks, residual, cotangent, gains)


def attention_backward_body(
    w_output,
    normed,
    queries,
    keys_across,
    keys,
    values,
    log_totals,
    mixed_across,
    d_residual,
    cosines,
    sines,
    bias,
    d_queries,
    d_window,
    d_window_across,
    grad_across,
    grad_output,
    d_mixed,
):
    blocks = d_window.shape[0]
    cosine, sine = cosines[...], sines[...]
    own_cosine, own_sine = cosine[:, :DEVICE_TOKENS], sine[:, :DEVICE_TOKENS]
    d_branch = d_residual[...].astype(BF16)
    d_mixed[...] = dot_nt(w_output[...], d_branch).astype(BF16)

    def one(group, unused):
        group_rows = pl.ds(pl.multiple_of(group * HEAD_SIZE, HEAD_SIZE), HEAD_SIZE)
        value_rows = pl.ds(pl.multiple_of(KV_WIDTH + group * HEAD_SIZE, HEAD_SIZE), HEAD_SIZE)
        d_key = d_value = jnp.zeros((HEAD_SIZE, cosine.shape[1]), F32)
        for offset in range(GROUP):
            head = group * GROUP + offset
            rows = pl.ds(pl.multiple_of(head * HEAD_SIZE, HEAD_SIZE), HEAD_SIZE)
            query = queries[rows, :] * SCALE
            d_mixed_head = d_mixed[rows, :]
            delta = jnp.sum(
                d_mixed_head.astype(F32) * mixed_across[rows, :], axis=0, keepdims=True
            )
            scores = dot(keys[group], query) + bias[...]
            probability = jnp.exp(scores - log_totals[pl.ds(head, 1), :])
            d_probs = dot(values[group], d_mixed_head)
            d_scores = (probability * (d_probs - delta)).astype(BF16)
            d_query = dot(keys_across[group_rows, :], d_scores) * SCALE
            d_queries[rows, :] = rotated(d_query, own_cosine, -own_sine).astype(BF16)
            d_key = d_key + dot_nt(query, d_scores)
            d_value = d_value + dot_nt(d_mixed_head, probability.astype(BF16))
        d_window_across[group_rows, :] = rotated(d_key, cosine, -sine).astype(BF16)
        d_window_across[value_rows, :] = d_value.astype(BF16)
        return unused

    lax.fori_loop(0, KEY_VALUE_HEADS, one, 0)
    for block in range(blocks):
        d_window[block] = d_window_across[
            :, block * DEVICE_TOKENS : (block + 1) * DEVICE_TOKENS
        ]
    query_grad = dot(d_queries[...], normed[:DEVICE_TOKENS, :])
    window_grad = dot(d_window_across[...], normed[...])
    output_grad = dot(mixed_across[...].astype(BF16), d_branch)
    grad_across[:QUERY_WIDTH, :] = query_grad
    grad_across[QUERY_WIDTH:, :] = window_grad
    grad_output[...] = output_grad


def micro_views(micro, operands):
    w_output, *views = operands
    views = [view.at[micro] for view in views]
    views[7] = operands[8].at[micro * DEVICE_TOKENS : (micro + 1) * DEVICE_TOKENS, :]
    return (w_output, *views)


def attention_backward_first(*refs):
    operands, (d_queries, d_window, grad_across, grad_output, across, d_mixed) = (
        refs[:12],
        refs[12:],
    )
    attention_backward_body(
        *micro_views(0, operands), d_queries, d_window, across, grad_across, grad_output, d_mixed
    )


def attention_backward_second(order, w_project, *refs):
    first_queries, first_window, first_across, first_output = refs[:4]
    operands, refs = refs[4:16], refs[16:]
    kept, sent, d_queries, window_kept, window_sent, gain_grad, flat, planes = refs[:8]
    across, d_mixed, own_window, grad_across, grad_output = refs[8:]
    attention_backward_body(
        *micro_views(1, operands),
        d_queries.at[1],
        own_window,
        across,
        grad_across,
        grad_output,
        d_mixed,
    )
    d_queries[0] = first_queries[...]
    early = window_kept.shape[0]
    for block in range(own_window.shape[0]):
        target, place = (window_kept, block) if block < early else (window_sent, block - early)
        target[place, 0] = first_window[block]
        target[place, 1] = own_window[block]
    grad_across[...] += first_across[...]
    grad_output[...] += first_output[...]
    total = jnp.zeros((D, LANES), F32)
    for j in range(7):
        piece = jnp.transpose(grad_across[j * LANES : (j + 1) * LANES, :])
        planes[j] = piece
        total = total + piece * w_project[:, j * LANES : (j + 1) * LANES].astype(F32)
    last = jnp.transpose(grad_across[QKV_WIDTH - LANES :, :])
    last = pltpu.roll(last, HALF, 1)
    planes[7] = last
    last_sum = last[:, :HALF] * w_project[:, 7 * LANES :].astype(F32)
    gain_grad[...] = jnp.sum(total, axis=1, keepdims=True) + jnp.sum(
        last_sum, axis=1, keepdims=True
    )
    flatten_odd(planes, D // 2, 7, flat, 0)
    for j in range(4):
        planes[j] = grad_output[:, j * LANES : (j + 1) * LANES]
    planes[4, :, :HALF] = grad_output[:, 4 * LANES :]
    flatten_odd(planes, QUERY_WIDTH // 2, 4, flat, D * QKV_WIDTH // LANES)
    store_blocks(order, flat, sent, sent.shape[1], 0, sent.shape[0])
    store_blocks(order, flat, kept, kept.shape[1], 0, 0)


def attention_backward(operands, count, rows, final=()):
    shape = jax.ShapeDtypeStruct
    window = operands[1].shape[1]
    blocks = window // DEVICE_TOKENS
    sums = [(QKV_WIDTH, D), (QUERY_WIDTH, D)]
    scratch = [
        pltpu.VMEM((2 * KV_WIDTH, window), BF16),
        pltpu.VMEM((QUERY_WIDTH, DEVICE_TOKENS), BF16),
    ]
    if final:
        kernel = attention_backward_second
        half = shape((count // 2, rows, LANES), BF16)
        late = blocks // 2
        one_block = (MICRO, 2 * KV_WIDTH, DEVICE_TOKENS)
        outputs = (
            half,
            half,
            shape((MICRO, QUERY_WIDTH, DEVICE_TOKENS), BF16),
            shape((blocks - late, *one_block), BF16),
            shape((late, *one_block), BF16),
            shape((D, 1), F32),
        )
        scratch = [
            pltpu.VMEM((count * rows, LANES), F32),
            pltpu.VMEM((8, D, LANES), F32),
            *scratch,
            pltpu.VMEM((blocks, 2 * KV_WIDTH, DEVICE_TOKENS), BF16),
            *[pltpu.VMEM(dims, F32) for dims in sums],
        ]
        in_specs = [smem()] + vmem(len(final) - 1 + len(operands))
    else:
        kernel = attention_backward_first
        outputs = (
            shape((QUERY_WIDTH, DEVICE_TOKENS), BF16),
            shape((blocks, 2 * KV_WIDTH, DEVICE_TOKENS), BF16),
            *[shape(dims, F32) for dims in sums],
        )
        in_specs = vmem(len(operands))
    return pl.pallas_call(
        kernel,
        out_shape=outputs,
        in_specs=in_specs,
        out_specs=tuple(vmem(len(outputs))),
        scratch_shapes=scratch,
        compiler_params=params(),
    )(*final, *operands)


def adam_update(weights, moment, square, grad, rate, decay):
    new_moment = BETA_ONE * moment + (1.0 - BETA_ONE) * grad
    new_square = BETA_TWO * square + (1.0 - BETA_TWO) * grad * grad
    mean_hat = new_moment / (1.0 - BETA_ONE**STEP)
    square_hat = new_square / (1.0 - BETA_TWO**STEP)
    new_weights = weights - rate * (
        mean_hat / (jnp.sqrt(square_hat) + ADAM_EPSILON) + decay * weights
    )
    return (new_weights, new_moment, new_square)


def first_of(lengths, index):
    starts = jnp.cumsum(lengths, axis=-1) - lengths
    return jnp.max(
        jnp.where(starts[:, None, :] <= index[None, :, None], starts[:, None, :], 0), axis=-1
    )


def on_device(
    block_input,
    out_grad,
    doc_lengths,
    attention_weights,
    feedforward_weights,
    norm_gains,
    attention_moment,
    attention_square,
    feedforward_moment,
    feedforward_square,
    gain_moment,
    gain_square,
):
    both = ("dp", "seq")
    seq_count = lax.axis_size("seq")
    owner_count = lax.axis_size(both)
    seq_place = lax.axis_index("seq")
    owner_place = lax.axis_index(both)
    attention_length = attention_weights.shape[0]
    feedforward_length = feedforward_weights.shape[0]
    reach = min((DOC_MAX + DEVICE_TOKENS - 2) // DEVICE_TOKENS, seq_count - 1)
    paired = is_power_of_two(seq_count) and reach == seq_count - 1
    butterfly = is_power_of_two(owner_count) and attention_length % (8 * LANES) == 0
    stages = gather_stages()
    order = block_order(stages)
    seq_stages = [stage for stage in stages if stage[0] == "seq"]

    own_inputs = block_input[:, 0]
    straight = jnp.arange(BLOCKS, dtype=jnp.int32)
    tiled_rows = feedforward_length % (8 * LANES) == 0
    feedforward_low = feedforward_weights.astype(BF16)
    if tiled_rows:
        feedforward_low = feedforward_low.reshape(-1, LANES)
    feedforward_blocks = lax.all_gather(feedforward_low, both, axis=0, tiled=True)
    feedforward_blocks = feedforward_blocks.reshape(BLOCKS, -1, LANES)

    if paired:
        window_blocks = seq_place ^ jnp.array(block_order(seq_stages), jnp.int32)
    else:
        window_blocks = seq_place - jnp.arange(reach + 1, dtype=jnp.int32)
    token = jnp.arange(DEVICE_TOKENS, dtype=jnp.int32)
    query_index = seq_place * DEVICE_TOKENS + token
    key_index = (window_blocks[:, None] * DEVICE_TOKENS + token[None, :]).reshape(-1)
    lengths = doc_lengths[:, 0]
    first_query = first_of(lengths, query_index)
    first_key = first_of(lengths, key_index)
    half_width = HEAD_SIZE // 2
    inverse = THETA ** (-(jnp.arange(half_width, dtype=F32) * 2.0) / HEAD_SIZE)
    position = (key_index[None] - first_key).astype(F32)
    angles = position[:, None, :] * inverse[None, :, None]
    cosines, sines = jnp.cos(angles), jnp.sin(angles)
    allowed = (key_index[None, :, None] >= first_query[:, None, :]) & (
        key_index[None, :, None] <= query_index[None, None, :]
    )
    bias = jnp.where(allowed, 0.0, -jnp.inf).astype(F32)

    attention_low = attention_weights.astype(BF16)
    if butterfly:
        orders = [
            jnp.array(block_order(path), jnp.int32) ^ owner_place
            for path in (stages, swap_dp(stages))
        ]
    else:
        orders = [straight, straight]
    if butterfly and paired:
        weights = attention_low.reshape(1, attention_length // LANES, LANES)
        window_inputs = own_inputs[None]
        inputs_far = exchange(window_inputs, "seq", seq_stages[0][1])
        for index, (axis, bit, unused_flat) in enumerate(stages[:-1]):
            far = exchange(weights, axis, bit)
            if index == 0:
                far, cosines, sines, bias = together(far, cosines, sines, bias)
            if index < len(stages) - 2:
                weights = jnp.concatenate([weights, far], 0)
            if 0 < index < len(seq_stages) - 1:
                window_inputs = jnp.concatenate([window_inputs, inputs_far], 0)
                far_weights, window_inputs = together(weights, window_inputs)
                weights = far_weights
                inputs_far = exchange(window_inputs, "seq", seq_stages[index][1])
        axis, bit, unused_flat = stages[-1]
        weight_pieces = [weights, far]
        weight_pieces += [exchange(piece, axis, bit) for piece in weight_pieces]
        input_pieces = [window_inputs, inputs_far]
        input_pieces += [exchange(piece, axis, bit) for piece in input_pieces]
    else:
        weights = lax.all_gather(attention_low, both, axis=0, tiled=True)
        weights = weights.reshape(BLOCKS, -1, LANES)
        weight_pieces = jnp.split(weights, 4)
        window_inputs = jnp.stack(
            [own_inputs]
            + [
                lax.ppermute(
                    own_inputs, "seq", [(p, p + step) for p in range(seq_count - step)]
                )
                for step in range(1, reach + 1)
            ],
            0,
        )
        quarter = (reach + 1) // 4
        cuts = [0, quarter, 2 * quarter, 3 * quarter, reach + 1]
        input_pieces = [window_inputs[a:b] for a, b in zip(cuts, cuts[1:])]
        orders = [straight, straight]

    (
        w_project,
        w_output,
        normed_one,
        queries,
        keys_across,
        keys,
        values,
        log_totals,
        mixed_across,
        residual,
    ) = attention_forward(
        orders[0], weight_pieces, input_pieces, cosines, sines, bias, norm_gains
    )
    block_output, d_residual, *parts, gain_two = feedforward(
        (straight, *orders), feedforward_blocks, residual, out_grad, norm_gains
    )
    block_output = block_output.reshape(MICRO, DEVICE_TOKENS, D)
    operands = (
        w_output,
        normed_one,
        queries,
        keys_across,
        keys,
        values,
        log_totals,
        mixed_across,
        d_residual,
        cosines,
        sines,
        bias,
    )
    d_residual = d_residual.reshape(MICRO, DEVICE_TOKENS, D)
    attention_rows = D * (QKV_WIDTH + QUERY_WIDTH) // (LANES * BLOCKS)
    if butterfly and paired:
        paths = [stages[::-1], swap_dp(stages)[::-1]]
        halving_seq = seq_stages[::-1]

        def send(value, stage):
            return exchange(value, stage[0], stage[1])

        kept, sent = [parts[0], parts[2]], [parts[1], parts[3]]
        arrived = [send(part, path[0]) for part, path in zip(sent, paths)]
        first = attention_backward(operands, BLOCKS, attention_rows)
        arrived = together(*arrived, *first)
        first = arrived[2:]
        kept, sent = zip(*[halve_step(part, new) for part, new in zip(kept, arrived)])
        first_across, *sent = together(first[2], *sent)
        arrived = [send(part, path[1]) for part, path in zip(sent, paths)]
        second = attention_backward(
            operands,
            BLOCKS,
            attention_rows,
            (orders[0], w_project, first[0], first[1], first_across, first[3]),
        )
        arrived = together(*arrived, *second)
        attention_kept, attention_sent, d_queries, window_kept, window_sent, gain_one = arrived[2:]
        kept, sent = zip(*[halve_step(part, new) for part, new in zip(kept, arrived)])
        gains_total = jnp.stack([gain_one[:, 0], gain_two[:, 0]], 0) / norm_gains
        for index, stage in enumerate(paths[0]):
            arrivals = {}
            if index + 2 < len(stages):
                arrivals["one"] = send(sent[0], paths[0][index + 2])
                arrivals["two"] = send(sent[1], paths[1][index + 2])
            arrivals["attention"] = send(attention_sent, stage)
            if index < len(halving_seq):
                arrivals["window"] = send(window_sent, halving_seq[index])
            arrivals["gains"] = send(gains_total, stage)
            arrivals = lax.optimization_barrier(arrivals)
            if "one" in arrivals:
                news = [arrivals["one"], arrivals["two"]]
                kept, sent = zip(*[halve_step(part, new) for part, new in zip(kept, news)])
            attention_kept, attention_sent = halve_step(attention_kept, arrivals["attention"])
            if "window" in arrivals:
                window_kept, window_sent = halve_step(window_kept, arrivals["window"])
            gains_total = gains_total + arrivals["gains"]
        attention_owned = attention_kept.reshape(-1)
        d_own = window_kept[0].astype(BF16)
        feedforward_owned = jnp.concatenate([kept[0][0], kept[1][0]], 0).reshape(-1)
    else:
        halves = [jnp.concatenate(parts[index : index + 2], 0) for index in (0, 2)]
        grads = jnp.concatenate(halves, 1).reshape(-1)
        feedforward_owned = lax.psum_scatter(grads, both, scatter_dimension=0, tiled=True)
        first = attention_backward(operands, BLOCKS, attention_rows)
        kept, sent, d_queries, window_kept, window_sent, gain_one = attention_backward(
            operands, BLOCKS, attention_rows, (orders[0], w_project, *first)
        )
        attention_owned = lax.psum_scatter(
            jnp.concatenate([kept, sent], 0).reshape(-1), both, scatter_dimension=0, tiled=True
        )
        d_window = jnp.concatenate([window_kept, window_sent], 0)
        d_own = d_window[0].astype(F32)
        for step in range(1, reach + 1):
            d_own = d_own + lax.ppermute(
                d_window[step], "seq", [(p, p - step) for p in range(step, seq_count)]
            ).astype(F32)
        d_own = d_own.astype(BF16)
        gains_total = jnp.stack([gain_one[:, 0], gain_two[:, 0]], 0) / norm_gains
        gains_total = lax.psum(gains_total, both)
    d_normed_one = matmul("met,de->mtd", jnp.concatenate([d_queries, d_own], 1), w_project)
    unit_one, inverse_one = unit_norm(own_inputs.astype(F32))
    input_grad = d_residual + norm_backward(d_normed_one, unit_one, inverse_one, norm_gains[0])

    attention_place = owner_place * attention_length + jnp.arange(attention_length, dtype=jnp.int32)
    attention_rate = jnp.where(
        attention_place < D * QKV_WIDTH, RATE_FACTOR * D ** (-0.5), RATE_FACTOR * OUT_FAN ** (-0.5)
    )
    feedforward_place = owner_place * feedforward_length + jnp.arange(
        feedforward_length, dtype=jnp.int32
    )
    feedforward_rate = jnp.where(
        feedforward_place < 2 * D * FF, RATE_FACTOR * D ** (-0.5), RATE_FACTOR * FF ** (-0.5)
    )
    new_attention = adam_update(
        attention_weights,
        attention_moment,
        attention_square,
        attention_owned.astype(F32),
        attention_rate,
        MATRIX_DECAY,
    )
    new_feedforward = adam_update(
        feedforward_weights,
        feedforward_moment,
        feedforward_square,
        feedforward_owned.astype(F32),
        feedforward_rate,
        MATRIX_DECAY,
    )
    new_gains = adam_update(norm_gains, gain_moment, gain_square, gains_total, GAIN_RATE, 0.0)
    return (
        block_output[:, None],
        input_grad[:, None],
        *new_attention,
        *new_feedforward,
        *new_gains,
    )


def solution(mesh):
    tokens = P(None, "dp", "seq", None)
    flat = P(("dp", "seq"))
    return jax.shard_map(
        on_device,
        mesh=mesh,
        in_specs=(
            tokens,
            tokens,
            P(None, "dp", None),
            flat,
            flat,
            P(),
            flat,
            flat,
            flat,
            flat,
            P(),
            P(),
        ),
        out_specs=(tokens, tokens, flat, flat, flat, flat, flat, flat, P(), P(), P()),
        check_vma=False,
    )
```

```python
import functools

import jax
import jax.numpy as jnp
from jax import lax
from jax.experimental import pallas as pl
from jax.experimental.pallas import tpu as pltpu
from jax.sharding import PartitionSpec as P

D = 576
QUERY_HEADS = 9
KEY_VALUE_HEADS = 3
GROUP = QUERY_HEADS // KEY_VALUE_HEADS
HEAD_SIZE = 64
FF = 1536
DEVICE_TOKENS = 128
MICRO = 2
DOC_MAX = 1000
STEP = 10
QKV_WIDTH = 960
QUERY_WIDTH = QUERY_HEADS * HEAD_SIZE
KV_WIDTH = KEY_VALUE_HEADS * HEAD_SIZE
OUT_FAN = 14
LANES = 128
HALF = LANES // 2
BLOCKS = 32
VMEM_LIMIT = 52 * 2**20

NORM_EPSILON = 1e-05
THETA = 100000.0
BETA_ONE = 0.9
BETA_TWO = 0.95
ADAM_EPSILON = 1e-08
MATRIX_DECAY = 0.1
RATE_FACTOR = 1.5
GAIN_RATE = 0.2
SCALE = HEAD_SIZE ** (-0.5)
BF16 = jnp.bfloat16
F32 = jnp.float32


def is_power_of_two(count):
    return count & (count - 1) == 0


def exchange(value, axis, bit):
    count = lax.axis_size(axis)
    return lax.ppermute(value, axis, [(place, place ^ bit) for place in range(count)])


def add_up(kept, news, parts):
    size = kept.shape[0] // parts
    results = []
    for index in range(parts):
        rows = slice(index * size, (index + 1) * size)
        total = kept[rows].astype(F32)
        for new in news:
            total = total + new[rows].astype(F32)
        results.append(total.astype(BF16) if index else total)
    return results


def pair_sum(values):
    while len(values) > 1:
        values = [one + two for one, two in zip(values[::2], values[1::2])]
    return values[0]


def together(*values):
    return lax.optimization_barrier(values)


def unit_norm(inputs):
    inverse_rms = lax.rsqrt(jnp.mean(inputs * inputs, axis=1, keepdims=True) + NORM_EPSILON)
    return (inputs * inverse_rms, inverse_rms)


def norm_backward(d_normed, unit_rows, inverse_rms, gain_row):
    scaled = d_normed * gain_row
    return inverse_rms * (
        scaled - unit_rows * jnp.mean(scaled * unit_rows, axis=1, keepdims=True)
    )


def matmul(equation, left, right):
    return jnp.einsum(equation, left, right, preferred_element_type=F32)


def params():
    return pltpu.CompilerParams(vmem_limit_bytes=VMEM_LIMIT)


def vmem(count):
    return [pl.BlockSpec(memory_space=pltpu.VMEM)] * count


def smem():
    return pl.BlockSpec(memory_space=pltpu.SMEM)


def dot(left, right):
    return jnp.dot(left, right, preferred_element_type=F32)


def dot_nt(left, right):
    return lax.dot_general(left, right, (((1,), (1,)), ((), ())), preferred_element_type=F32)


def dot_tn(left, right):
    return lax.dot_general(left, right, (((0,), (0,)), ((), ())), preferred_element_type=F32)


def shift_half(low, high):
    lane = lax.broadcasted_iota(jnp.int32, low.shape, 1)
    return pltpu.roll(jnp.where(lane < HALF, low, high), HALF, 1)


def unflatten_odd(flat, base, pairs, whole, planes):
    step = 2 * whole + 1

    def piece(k):
        return flat[pl.ds(base + k, pairs, stride=step), :]

    for j in range(whole + 1):
        planes[j, pl.ds(0, pairs, stride=2), :] = piece(j)
        planes[j, pl.ds(1, pairs, stride=2), :] = shift_half(
            piece(min(whole + 1 + j, 2 * whole)), piece(whole + j)
        )


def flatten_odd(planes, pairs, whole, flat, base):
    step = 2 * whole + 1

    def even(j):
        return planes[j, pl.ds(0, pairs, stride=2), :]

    def odd(j):
        return planes[j, pl.ds(1, pairs, stride=2), :]

    for k in range(step):
        if k < whole:
            rows = even(k)
        elif k == whole:
            first = odd(0)
            lane = lax.broadcasted_iota(jnp.int32, first.shape, 1)
            rows = jnp.where(lane < HALF, even(whole), pltpu.roll(first, HALF, 1))
        else:
            rows = shift_half(odd(k - whole), odd(k - whole - 1))
        flat[pl.ds(base + k, pairs, stride=step), :] = rows


def load_blocks(order, halves, flat):
    first = 0
    for blocks in halves:
        count, rows, unused = blocks.shape

        def move(place, unused, blocks=blocks, rows=rows, first=first):
            start = pl.multiple_of(order[first + place] * rows, 8)
            flat[pl.ds(start, rows), :] = blocks[place].astype(F32)
            return unused

        lax.fori_loop(0, count, move, 0)
        first += count


def store_blocks(order, flat, blocks, owner_rows, first_row, first_index):
    count, rows, unused = blocks.shape

    def move(index, unused):
        start = pl.multiple_of(order[first_index + index] * owner_rows + first_row, 8)
        blocks[index] = flat[pl.ds(start, rows), :].astype(BF16)
        return unused

    lax.fori_loop(0, count, move, 0)


def planes_to_matrix(planes, whole, matrix):
    for j in range(whole):
        matrix[:, j * LANES : (j + 1) * LANES] = planes[j].astype(BF16)
    matrix[:, whole * LANES : whole * LANES + HALF] = planes[whole, :, :HALF].astype(BF16)


def rotated(rows, cosine, sine):
    half_width = HEAD_SIZE // 2
    first, second = rows[:half_width], rows[half_width:]
    return jnp.concatenate([first * cosine - second * sine, second * cosine + first * sine], 0)


def three(rows, group):
    pieces = []
    for offset in range(GROUP):
        start = pl.multiple_of((group * GROUP + offset) * HEAD_SIZE, HEAD_SIZE)
        pieces.append(rows[pl.ds(start, HEAD_SIZE), :])
    return jnp.concatenate(pieces, 1)


def attention_forward_kernel(weight_count, input_count, order, *refs):
    weight_pieces, refs = refs[:weight_count], refs[weight_count:]
    input_pieces, refs = refs[:input_count], refs[input_count:]
    cosines, sines, bias, gains, w_project, w_output, normed, queries = refs[:8]
    keys_across, keys, values, log_totals, mixed_across, residual = refs[8:14]
    flat, planes_one, planes_two, w_across, values_across = refs[14:]
    load_blocks(order, weight_pieces, flat)
    unflatten_odd(flat, 0, D // 2, 7, planes_one)
    planes_to_matrix(planes_one, 7, w_project)
    for j in range(7):
        w_across[j * LANES : (j + 1) * LANES, :] = jnp.transpose(planes_one[j]).astype(BF16)
    w_across[7 * LANES :, :] = jnp.transpose(planes_one[7])[:HALF].astype(BF16)
    unflatten_odd(flat, D * QKV_WIDTH // LANES, QUERY_WIDTH // 2, 4, planes_two)
    planes_to_matrix(planes_two, 4, w_output)
    blocks = [piece.at[place] for piece in input_pieces for place in range(piece.shape[0])]
    gain = jnp.broadcast_to(gains[...], (D, DEVICE_TOKENS))

    def one(micro, unused):
        for block, inputs in enumerate(blocks):
            rows = inputs[micro].astype(F32)
            inverse = lax.rsqrt(jnp.mean(rows * rows, axis=0, keepdims=True) + NORM_EPSILON)
            normed[micro, :, block * DEVICE_TOKENS : (block + 1) * DEVICE_TOKENS] = (
                rows * inverse * gain
            ).astype(BF16)
        cosine, sine = cosines[micro], sines[micro]
        own_cosine, own_sine = cosine[:, :DEVICE_TOKENS], sine[:, :DEVICE_TOKENS]
        query = dot(w_across[:QUERY_WIDTH, :], normed[micro, :, :DEVICE_TOKENS])
        for head in range(QUERY_HEADS):
            rows = slice(head * HEAD_SIZE, (head + 1) * HEAD_SIZE)
            queries[micro, rows, :] = rotated(query[rows], own_cosine, own_sine).astype(BF16)
        other = dot(w_across[QUERY_WIDTH:, :], normed[micro])
        for head in range(KEY_VALUE_HEADS):
            rows = slice(head * HEAD_SIZE, (head + 1) * HEAD_SIZE)
            key = rotated(other[rows], cosine, sine)
            keys_across[micro, rows, :] = key.astype(BF16)
            keys[micro, head] = jnp.transpose(key).astype(BF16)
            value = other[KV_WIDTH + head * HEAD_SIZE : KV_WIDTH + (head + 1) * HEAD_SIZE]
            values_across[rows, :] = value.astype(BF16)
            values[micro, head] = jnp.transpose(value).astype(BF16)
        bias_three = jnp.concatenate([bias[micro]] * GROUP, 1)
        for group in range(KEY_VALUE_HEADS):
            group_rows = slice(group * HEAD_SIZE, (group + 1) * HEAD_SIZE)
            scores = dot(keys[micro, group], three(queries.at[micro], group) * SCALE) + bias_three
            top = jnp.max(scores, axis=0, keepdims=True)
            weights = jnp.exp(scores - top)
            total = jnp.sum(weights, axis=0, keepdims=True)
            low = (weights * (1.0 / total)).astype(BF16)
            mixed = dot(values_across[group_rows, :], low)
            log_total = top + jnp.log(total)
            for offset in range(GROUP):
                head = group * GROUP + offset
                lanes = slice(offset * DEVICE_TOKENS, (offset + 1) * DEVICE_TOKENS)
                mixed_across[micro, head * HEAD_SIZE : (head + 1) * HEAD_SIZE, :] = mixed[:, lanes]
                log_totals[micro, head : head + 1, :] = log_total[:, lanes]
        mixed = jnp.transpose(mixed_across[micro]).astype(BF16)
        inputs = jnp.transpose(blocks[0][micro].astype(F32))
        residual[micro] = inputs + dot(mixed, w_output[...])
        return unused

    lax.fori_loop(0, MICRO, one, 0)


def attention_forward(order, weight_pieces, input_pieces, *tables):
    window = sum(piece.shape[0] for piece in input_pieces) * DEVICE_TOKENS
    shape = jax.ShapeDtypeStruct
    rows = sum(piece.shape[0] * piece.shape[1] for piece in weight_pieces)
    return pl.pallas_call(
        functools.partial(attention_forward_kernel, len(weight_pieces), len(input_pieces)),
        out_shape=(
            shape((D, QKV_WIDTH), BF16),
            shape((QUERY_WIDTH, D), BF16),
            shape((MICRO, D, window), BF16),
            shape((MICRO, QUERY_WIDTH, DEVICE_TOKENS), BF16),
            shape((MICRO, KV_WIDTH, window), BF16),
            shape((MICRO, KEY_VALUE_HEADS, window, HEAD_SIZE), BF16),
            shape((MICRO, KEY_VALUE_HEADS, window, HEAD_SIZE), BF16),
            shape((MICRO, QUERY_HEADS, DEVICE_TOKENS), F32),
            shape((MICRO, QUERY_WIDTH, DEVICE_TOKENS), F32),
            shape((MICRO, DEVICE_TOKENS, D), F32),
        ),
        in_specs=[smem()] + vmem(len(weight_pieces) + len(input_pieces) + len(tables)),
        out_specs=tuple(vmem(10)),
        scratch_shapes=[
            pltpu.VMEM((rows, LANES), F32),
            pltpu.VMEM((8, D, LANES), F32),
            pltpu.VMEM((5, QUERY_WIDTH, LANES), F32),
            pltpu.VMEM((QKV_WIDTH, D), BF16),
            pltpu.VMEM((KV_WIDTH, window), BF16),
        ],
        compiler_params=params(),
    )(order, *weight_pieces, *input_pieces, *tables)


def feedforward_kernel(
    straight,
    order_one,
    order_two,
    weight_blocks,
    residual,
    cotangent,
    gains,
    block_output,
    d_branch,
    d_residual,
    one_kept,
    one_sent,
    two_kept,
    two_sent,
    gain_grad,
    flat,
    planes,
    w_gate_up,
    w_down,
    hidden,
    d_gate_up,
):
    columns = 2 * FF // LANES
    load_blocks(straight, (weight_blocks,), flat)
    for j in range(columns):
        w_gate_up[:, j * LANES : (j + 1) * LANES] = flat[
            pl.ds(j, D, stride=columns), :
        ].astype(BF16)
    unflatten_odd(flat, D * columns, FF // 2, 4, planes)
    planes_to_matrix(planes, 4, w_down)
    gain = gains[...]
    rows = jnp.concatenate([residual[micro] for micro in range(MICRO)], 0)
    inverse = lax.rsqrt(jnp.mean(rows * rows, axis=-1, keepdims=True) + NORM_EPSILON)
    unit = rows * inverse
    normed = (unit * gain).astype(BF16)
    cotangent_low = jnp.concatenate(
        [jnp.transpose(cotangent[micro].astype(F32)) for micro in range(MICRO)], 0
    ).astype(BF16)
    part = 256
    for start in range(0, FF, part):
        gate = dot(normed, w_gate_up[:, start : start + part])
        up = dot(normed, w_gate_up[:, FF + start : FF + start + part])
        d_hidden = dot_nt(cotangent_low, w_down[start : start + part, :])
        sigmoid = 1.0 / (1.0 + jnp.exp(-gate))
        activated = gate * sigmoid
        hidden[:, start : start + part] = (activated * up).astype(BF16)
        d_gate_up[:, start : start + part] = (
            d_hidden * up * sigmoid * (1.0 + gate * (1.0 - sigmoid))
        ).astype(BF16)
        d_gate_up[:, FF + start : FF + start + part] = (d_hidden * activated).astype(BF16)
    result = rows + dot(hidden[...], w_down[...])
    d_normed = dot_nt(d_gate_up[...], w_gate_up[...])
    scaled = d_normed * gain
    d_rows = cotangent_low.astype(F32) + inverse * (
        scaled - unit * jnp.mean(scaled * unit, axis=-1, keepdims=True)
    )
    d_branch[...] = d_rows.astype(BF16)
    for micro in range(MICRO):
        own = slice(micro * DEVICE_TOKENS, (micro + 1) * DEVICE_TOKENS)
        block_output[micro] = jnp.transpose(result[own]).astype(BF16)
        d_residual[micro] = jnp.transpose(d_rows[own])
    normed_across = jnp.transpose(unit * gain).astype(BF16)
    total = jnp.zeros((D, LANES), F32)
    for start in range(0, 2 * FF, part):
        grad = dot(normed_across, d_gate_up[:, start : start + part])
        for offset in range(0, part, LANES):
            piece = grad[:, offset : offset + LANES]
            place = start + offset
            total = total + piece * w_gate_up[:, place : place + LANES].astype(F32)
            flat[pl.ds(place // LANES, D, stride=columns), :] = piece
    gain_grad[...] = jnp.sum(total, axis=1, keepdims=True)
    for start in range(0, FF, part):
        grad = dot_tn(hidden[:, start : start + part], cotangent_low)
        for j in range(4):
            planes[j, start : start + part, :] = grad[:, j * LANES : (j + 1) * LANES]
        planes[4, start : start + part, :HALF] = grad[:, 4 * LANES :]
    flatten_odd(planes, FF // 2, 4, flat, D * columns)
    owner_rows = weight_blocks.shape[1]
    half = one_kept.shape[0]
    middle = one_kept.shape[1]
    store_blocks(order_one, flat, one_sent, owner_rows, 0, half)
    store_blocks(order_two, flat, two_sent, owner_rows, middle, half)
    store_blocks(order_one, flat, one_kept, owner_rows, 0, 0)
    store_blocks(order_two, flat, two_kept, owner_rows, middle, 0)


def feedforward(orders, weight_blocks, residual, cotangent, gains):
    shape = jax.ShapeDtypeStruct
    count, owner_rows, unused = weight_blocks.shape
    middle = owner_rows // 32 * 16
    one = shape((count // 2, middle, LANES), BF16)
    two = shape((count // 2, owner_rows - middle, LANES), BF16)
    tokens = residual.shape[0] * residual.shape[1]
    rows = weight_blocks.shape[0] * weight_blocks.shape[1]
    return pl.pallas_call(
        feedforward_kernel,
        out_shape=(
            shape((MICRO, D, DEVICE_TOKENS), BF16),
            shape((tokens, D), BF16),
            shape((MICRO, D, DEVICE_TOKENS), F32),
            one,
            one,
            two,
            two,
            shape((D, 1), F32),
        ),
        in_specs=[smem()] * 3 + vmem(4),
        out_specs=tuple(vmem(8)),
        scratch_shapes=[
            pltpu.VMEM((rows, LANES), F32),
            pltpu.VMEM((5, FF, LANES), F32),
            pltpu.VMEM((D, 2 * FF), BF16),
            pltpu.VMEM((FF, D), BF16),
            pltpu.VMEM((tokens, FF), BF16),
            pltpu.VMEM((tokens, 2 * FF), BF16),
        ],
        compiler_params=params(),
    )(*orders, weight_blocks, residual, cotangent, gains)


def attention_backward_body(
    w_output,
    normed,
    queries,
    keys_across,
    keys,
    values,
    log_totals,
    mixed_across,
    d_branch,
    cosines,
    sines,
    bias,
    d_queries,
    d_window,
    query_grad,
    window_grad,
    output_grad,
    d_window_across,
    d_mixed,
):
    blocks = d_window.shape[0]
    cosine, sine = cosines[...], sines[...]
    own_cosine, own_sine = cosine[:, :DEVICE_TOKENS], sine[:, :DEVICE_TOKENS]
    d_mixed[...] = dot_nt(w_output[...], d_branch[...]).astype(BF16)

    def one(group, unused):
        group_rows = pl.ds(pl.multiple_of(group * HEAD_SIZE, HEAD_SIZE), HEAD_SIZE)
        value_rows = pl.ds(pl.multiple_of(KV_WIDTH + group * HEAD_SIZE, HEAD_SIZE), HEAD_SIZE)
        query = three(queries, group) * SCALE
        d_heads = three(d_mixed, group)
        delta = jnp.sum(d_heads.astype(F32) * three(mixed_across, group), axis=0, keepdims=True)
        log_total = jnp.concatenate(
            [log_totals[pl.ds(group * GROUP + offset, 1), :] for offset in range(GROUP)], 1
        )
        bias_three = jnp.concatenate([bias[...]] * GROUP, 1)
        probability = jnp.exp(dot(keys[group], query) + bias_three - log_total)
        d_probs = dot(values[group], d_heads)
        d_scores = (probability * (d_probs - delta)).astype(BF16)
        d_query = dot(keys_across[group_rows, :], d_scores) * SCALE
        for offset in range(GROUP):
            lanes = slice(offset * DEVICE_TOKENS, (offset + 1) * DEVICE_TOKENS)
            start = pl.multiple_of((group * GROUP + offset) * HEAD_SIZE, HEAD_SIZE)
            d_queries[pl.ds(start, HEAD_SIZE), :] = rotated(
                d_query[:, lanes], own_cosine, -own_sine
            ).astype(BF16)
        d_key = dot_nt(query, d_scores)
        d_value = dot_nt(d_heads, probability.astype(BF16))
        d_window_across[group_rows, :] = rotated(d_key, cosine, -sine).astype(BF16)
        d_window_across[value_rows, :] = d_value.astype(BF16)
        return unused

    lax.fori_loop(0, KEY_VALUE_HEADS, one, 0)
    for block in range(blocks):
        d_window[block] = d_window_across[
            :, block * DEVICE_TOKENS : (block + 1) * DEVICE_TOKENS
        ]
    query_grad[...] = dot_nt(normed[:, :DEVICE_TOKENS], d_queries[...])
    window_grad[...] = dot_nt(normed[...], d_window_across[...])
    output_grad[...] = dot(mixed_across[...].astype(BF16), d_branch[...])


def micro_views(micro, operands):
    w_output, *views = operands
    views = [view.at[micro] for view in views]
    views[7] = operands[8].at[micro * DEVICE_TOKENS : (micro + 1) * DEVICE_TOKENS, :]
    return (w_output, *views)


def attention_backward_first(*refs):
    attention_backward_body(*micro_views(0, refs[:12]), *refs[12:])


def attention_backward_second(order, w_project, *refs):
    first_queries, first_window, *first_grads = refs[:5]
    operands, refs = refs[5:17], refs[17:]
    kept, sent, d_queries, window_kept, window_sent, gain_grad, flat, planes = refs[:8]
    across, d_mixed, own_window, query_grad, window_grad, output_grad = refs[8:]
    attention_backward_body(
        *micro_views(1, operands),
        d_queries.at[1],
        own_window,
        query_grad,
        window_grad,
        output_grad,
        across,
        d_mixed,
    )
    d_queries[0] = first_queries[...]
    early = window_kept.shape[0]
    for block in range(own_window.shape[0]):
        target, place = (window_kept, block) if block < early else (window_sent, block - early)
        target[place, 0] = first_window[block]
        target[place, 1] = own_window[block]
    for sums, first in zip((query_grad, window_grad, output_grad), first_grads):
        sums[...] += first[...]
    total = jnp.zeros((D, LANES), F32)
    later = [window_grad[:, j * LANES : (j + 1) * LANES] for j in range(3)]
    for j in range(7):
        if j < 4:
            piece = query_grad[:, j * LANES : (j + 1) * LANES]
        elif j == 4:
            piece = jnp.concatenate([query_grad[:, j * LANES :], later[0][:, :HALF]], 1)
        else:
            piece = shift_half(later[j - 4], later[j - 5])
        planes[j] = piece
        total = total + piece * w_project[:, j * LANES : (j + 1) * LANES].astype(F32)
    planes[7] = pltpu.roll(later[2], HALF, 1)
    last_sum = planes[7, :, :HALF] * w_project[:, 7 * LANES :].astype(F32)
    gain_grad[...] = jnp.sum(total, axis=1, keepdims=True) + jnp.sum(
        last_sum, axis=1, keepdims=True
    )
    flatten_odd(planes, D // 2, 7, flat, 0)
    for j in range(4):
        planes[j] = output_grad[:, j * LANES : (j + 1) * LANES]
    planes[4, :, :HALF] = output_grad[:, 4 * LANES :]
    flatten_odd(planes, QUERY_WIDTH // 2, 4, flat, D * QKV_WIDTH // LANES)
    store_blocks(order, flat, sent, sent.shape[1], 0, sent.shape[0])
    store_blocks(order, flat, kept, kept.shape[1], 0, 0)


def attention_backward(operands, count, rows, final=()):
    shape = jax.ShapeDtypeStruct
    window = operands[1].shape[2]
    blocks = window // DEVICE_TOKENS
    sums = [(D, QUERY_WIDTH), (D, 2 * KV_WIDTH), (QUERY_WIDTH, D)]
    scratch = [
        pltpu.VMEM((2 * KV_WIDTH, window), BF16),
        pltpu.VMEM((QUERY_WIDTH, DEVICE_TOKENS), BF16),
    ]
    if final:
        kernel = attention_backward_second
        half = shape((count // 2, rows, LANES), BF16)
        late = blocks // 2
        one_block = (MICRO, 2 * KV_WIDTH, DEVICE_TOKENS)
        outputs = (
            half,
            half,
            shape((MICRO, QUERY_WIDTH, DEVICE_TOKENS), BF16),
            shape((blocks - late, *one_block), BF16),
            shape((late, *one_block), BF16),
            shape((D, 1), F32),
        )
        scratch = [
            pltpu.VMEM((count * rows, LANES), F32),
            pltpu.VMEM((8, D, LANES), F32),
            *scratch,
            pltpu.VMEM((blocks, 2 * KV_WIDTH, DEVICE_TOKENS), BF16),
            *[pltpu.VMEM(dims, F32) for dims in sums],
        ]
        in_specs = [smem()] + vmem(len(final) - 1 + len(operands))
    else:
        kernel = attention_backward_first
        outputs = (
            shape((QUERY_WIDTH, DEVICE_TOKENS), BF16),
            shape((blocks, 2 * KV_WIDTH, DEVICE_TOKENS), BF16),
            *[shape(dims, F32) for dims in sums],
        )
        in_specs = vmem(len(operands))
    return pl.pallas_call(
        kernel,
        out_shape=outputs,
        in_specs=in_specs,
        out_specs=tuple(vmem(len(outputs))),
        scratch_shapes=scratch,
        compiler_params=params(),
    )(*final, *operands)


def adam_update(weights, moment, square, grad, rate, decay):
    new_moment = BETA_ONE * moment + (1.0 - BETA_ONE) * grad
    new_square = BETA_TWO * square + (1.0 - BETA_TWO) * grad * grad
    mean_hat = new_moment / (1.0 - BETA_ONE**STEP)
    square_hat = new_square / (1.0 - BETA_TWO**STEP)
    new_weights = weights - rate * (
        mean_hat / (jnp.sqrt(square_hat) + ADAM_EPSILON) + decay * weights
    )
    return (new_weights, new_moment, new_square)


def first_of(lengths, index):
    starts = jnp.cumsum(lengths, axis=-1) - lengths
    return jnp.max(
        jnp.where(starts[:, None, :] <= index[None, :, None], starts[:, None, :], 0), axis=-1
    )


def on_device(
    block_input,
    out_grad,
    doc_lengths,
    attention_weights,
    feedforward_weights,
    norm_gains,
    attention_moment,
    attention_square,
    feedforward_moment,
    feedforward_square,
    gain_moment,
    gain_square,
):
    both = ("dp", "seq")
    seq_count = lax.axis_size("seq")
    owner_count = lax.axis_size(both)
    seq_place = lax.axis_index("seq")
    owner_place = lax.axis_index(both)
    attention_length = attention_weights.shape[0]
    feedforward_length = feedforward_weights.shape[0]
    reach = min((DOC_MAX + DEVICE_TOKENS - 2) // DEVICE_TOKENS, seq_count - 1)
    dp_count = lax.axis_size("dp")
    butterfly = (
        is_power_of_two(seq_count)
        and seq_count >= 4
        and reach == seq_count - 1
        and dp_count == 4
        and attention_length % (8 * LANES) == 0
    )
    pair = (0, 1)
    line = range(0, seq_count, 2)
    square = range(0, owner_count, seq_count)
    order = [c ^ r ^ s for c in pair for r in square for s in line]
    turned = [
        c ^ x ^ y ^ s
        for c in pair
        for x in (0, seq_count)
        for y in (0, 2 * seq_count)
        for s in line
    ]

    own_inputs = jnp.swapaxes(block_input[:, 0], 1, 2)
    straight = jnp.arange(BLOCKS, dtype=jnp.int32)
    tiled_rows = feedforward_length % (8 * LANES) == 0
    feedforward_low = feedforward_weights.astype(BF16)
    if tiled_rows:
        feedforward_low = feedforward_low.reshape(-1, LANES)
    feedforward_blocks = lax.all_gather(feedforward_low, both, axis=0, tiled=True)
    feedforward_blocks = feedforward_blocks.reshape(BLOCKS, -1, LANES)

    if butterfly:
        window_blocks = seq_place ^ jnp.array([c ^ s for c in pair for s in line], jnp.int32)
    else:
        window_blocks = seq_place - jnp.arange(reach + 1, dtype=jnp.int32)
    token = jnp.arange(DEVICE_TOKENS, dtype=jnp.int32)
    query_index = seq_place * DEVICE_TOKENS + token
    key_index = (window_blocks[:, None] * DEVICE_TOKENS + token[None, :]).reshape(-1)
    lengths = doc_lengths[:, 0]
    first_query = first_of(lengths, query_index)
    first_key = first_of(lengths, key_index)
    half_width = HEAD_SIZE // 2
    inverse = THETA ** (-(jnp.arange(half_width, dtype=F32) * 2.0) / HEAD_SIZE)
    position = (key_index[None] - first_key).astype(F32)
    angles = position[:, None, :] * inverse[None, :, None]
    cosines, sines = jnp.cos(angles), jnp.sin(angles)
    allowed = (key_index[None, :, None] >= first_query[:, None, :]) & (
        key_index[None, :, None] <= query_index[None, None, :]
    )
    bias = jnp.where(allowed, 0.0, -jnp.inf).astype(F32)

    attention_low = attention_weights.astype(BF16)
    if butterfly:
        orders = [jnp.array(path, jnp.int32) ^ owner_place for path in (turned, order)]
        weights = attention_low.reshape(1, attention_length // LANES, LANES)
        window_inputs = own_inputs[None]
        news = [exchange(weights, "seq", place) for place in line[1:]]
        inputs_near = [window_inputs]
        inputs_near += [exchange(window_inputs, "seq", place) for place in line[1:]]
        news = together(*news, cosines, sines, bias)
        *news, cosines, sines, bias = news
        weights = jnp.concatenate([weights, *news], 0)
        weight_pieces = [weights]
        weight_pieces += [exchange(weights, "dp", place) for place in range(1, dp_count)]
        weight_pieces += [exchange(piece, "seq", 1) for piece in weight_pieces]
        input_pieces = inputs_near + [exchange(piece, "seq", 1) for piece in inputs_near]
    else:
        weights = lax.all_gather(attention_low, both, axis=0, tiled=True)
        weights = weights.reshape(BLOCKS, -1, LANES)
        weight_pieces = jnp.split(weights, 4)
        window_inputs = jnp.stack(
            [own_inputs]
            + [
                lax.ppermute(
                    own_inputs, "seq", [(p, p + step) for p in range(seq_count - step)]
                )
                for step in range(1, reach + 1)
            ],
            0,
        )
        quarter = (reach + 1) // 4
        cuts = [0, quarter, 2 * quarter, 3 * quarter, reach + 1]
        input_pieces = [window_inputs[a:b] for a, b in zip(cuts, cuts[1:])]
        orders = [straight, straight]

    (
        w_project,
        w_output,
        normed_one,
        queries,
        keys_across,
        keys,
        values,
        log_totals,
        mixed_across,
        residual,
    ) = attention_forward(
        orders[1], weight_pieces, input_pieces, cosines, sines, bias, norm_gains[0][:, None]
    )
    block_output, d_branch, d_residual, *parts, gain_two = feedforward(
        (straight, *orders),
        feedforward_blocks,
        residual,
        jnp.swapaxes(out_grad[:, 0], 1, 2),
        norm_gains[1:2],
    )
    operands = (
        w_output,
        normed_one,
        queries,
        keys_across,
        keys,
        values,
        log_totals,
        mixed_across,
        d_branch,
        cosines,
        sines,
        bias,
    )
    attention_rows = D * (QKV_WIDTH + QUERY_WIDTH) // (LANES * BLOCKS)
    if butterfly:
        one_kept, one_sent, two_kept, two_sent = parts
        one_new, two_new = exchange(one_sent, "seq", 1), exchange(two_sent, "seq", 1)
        first = attention_backward(operands, BLOCKS, attention_rows)
        one_new, two_new, *first = together(one_new, two_new, *first)
        one_kept, one_sent = add_up(one_kept, [one_new], 2)
        two_kept, two_sent = add_up(two_kept, [two_new], 2)
        one_sent, two_sent, *first = together(one_sent, two_sent, *first)
        one_new, two_new = exchange(one_sent, "dp", 1), exchange(two_sent, "dp", 2)
        second = attention_backward(
            operands, BLOCKS, attention_rows, (orders[1], w_project, *first)
        )
        one_new, two_new, *second = together(one_new, two_new, *second)
        kept, sent, d_queries, window_kept, window_sent, gain_one = second
        one_kept, one_sent = add_up(one_kept, [one_new], 2)
        two_kept, two_sent = add_up(two_kept, [two_new], 2)
        gains_total = jnp.stack([gain_one[:, 0], gain_two[:, 0]], 0) / norm_gains

        new = exchange(sent, "seq", 1)
        one_new, two_new = exchange(one_sent, "dp", 2), exchange(two_sent, "dp", 1)
        window_new = exchange(window_sent, "seq", 1)
        gains_new = exchange(gains_total, "seq", 1)
        new, one_new, two_new, window_new, gains_new = together(
            new, one_new, two_new, window_new, gains_new
        )
        kept, *sent = add_up(kept, [new], dp_count)
        gains_total = gains_total + gains_new
        news = [exchange(part, "dp", place + 1) for place, part in enumerate(sent)]
        gains_news = [exchange(gains_total, "dp", place) for place in range(1, dp_count)]

        one_kept, *one_sent = add_up(one_kept, [one_new], len(line))
        two_kept, *two_sent = add_up(two_kept, [two_new], len(line))
        window_kept, *window_sent = add_up(window_kept, [window_new], len(line))

        def along_line(parts):
            return [exchange(part, "seq", place) for place, part in zip(line[1:], parts)]

        one_news, two_news = along_line(one_sent), along_line(two_sent)
        window_news = along_line(window_sent)

        arrived = together(*news, *gains_news)
        news, gains_news = arrived[: len(news)], arrived[len(news) :]
        kept, *sent = add_up(kept, news, len(line))
        gains_total = pair_sum([gains_total, *gains_news])
        news = along_line(sent)
        gains_news = along_line([gains_total] * len(sent))
        gains_total = pair_sum([gains_total, *gains_news])
        attention_owned = add_up(kept, news, 1)[0].reshape(-1)
        feedforward_owned = jnp.concatenate(
            [add_up(one_kept, one_news, 1)[0][0], add_up(two_kept, two_news, 1)[0][0]], 0
        ).reshape(-1)
        d_own = add_up(window_kept, window_news, 1)[0][0].astype(BF16)
    else:
        halves = [jnp.concatenate(parts[index : index + 2], 0) for index in (0, 2)]
        grads = jnp.concatenate(halves, 1).reshape(-1)
        feedforward_owned = lax.psum_scatter(grads, both, scatter_dimension=0, tiled=True)
        first = attention_backward(operands, BLOCKS, attention_rows)
        kept, sent, d_queries, window_kept, window_sent, gain_one = attention_backward(
            operands, BLOCKS, attention_rows, (orders[1], w_project, *first)
        )
        attention_owned = lax.psum_scatter(
            jnp.concatenate([kept, sent], 0).reshape(-1), both, scatter_dimension=0, tiled=True
        )
        d_window = jnp.concatenate([window_kept, window_sent], 0)
        d_own = d_window[0].astype(F32)
        for step in range(1, reach + 1):
            d_own = d_own + lax.ppermute(
                d_window[step], "seq", [(p, p - step) for p in range(step, seq_count)]
            ).astype(F32)
        d_own = d_own.astype(BF16)
        gains_total = jnp.stack([gain_one[:, 0], gain_two[:, 0]], 0) / norm_gains
        gains_total = lax.psum(gains_total, both)
    d_normed_one = matmul("de,met->mdt", w_project, jnp.concatenate([d_queries, d_own], 1))
    unit_one, inverse_one = unit_norm(own_inputs.astype(F32))
    input_grad = d_residual + norm_backward(
        d_normed_one, unit_one, inverse_one, norm_gains[0][None, :, None]
    )

    attention_place = owner_place * attention_length + jnp.arange(attention_length, dtype=jnp.int32)
    attention_rate = jnp.where(
        attention_place < D * QKV_WIDTH, RATE_FACTOR * D ** (-0.5), RATE_FACTOR * OUT_FAN ** (-0.5)
    )
    feedforward_place = owner_place * feedforward_length + jnp.arange(
        feedforward_length, dtype=jnp.int32
    )
    feedforward_rate = jnp.where(
        feedforward_place < 2 * D * FF, RATE_FACTOR * D ** (-0.5), RATE_FACTOR * FF ** (-0.5)
    )
    new_attention = adam_update(
        attention_weights,
        attention_moment,
        attention_square,
        attention_owned.astype(F32),
        attention_rate,
        MATRIX_DECAY,
    )
    new_feedforward = adam_update(
        feedforward_weights,
        feedforward_moment,
        feedforward_square,
        feedforward_owned.astype(F32),
        feedforward_rate,
        MATRIX_DECAY,
    )
    new_gains = adam_update(norm_gains, gain_moment, gain_square, gains_total, GAIN_RATE, 0.0)
    return (
        jnp.swapaxes(block_output, 1, 2)[:, None],
        jnp.swapaxes(input_grad, 1, 2)[:, None],
        *new_attention,
        *new_feedforward,
        *new_gains,
    )


def solution(mesh):
    tokens = P(None, "dp", "seq", None)
    flat = P(("dp", "seq"))
    return jax.shard_map(
        on_device,
        mesh=mesh,
        in_specs=(
            tokens,
            tokens,
            P(None, "dp", None),
            flat,
            flat,
            P(),
            flat,
            flat,
            flat,
            flat,
            P(),
            P(),
        ),
        out_specs=(tokens, tokens, flat, flat, flat, flat, flat, flat, P(), P(), P()),
        check_vma=False,
    )
```

```python
import functools

import jax
import jax.numpy as jnp
from jax import lax
from jax.experimental import pallas as pl
from jax.experimental.pallas import tpu as pltpu
from jax.sharding import PartitionSpec as P

D = 576
QUERY_HEADS = 9
KEY_VALUE_HEADS = 3
GROUP = QUERY_HEADS // KEY_VALUE_HEADS
HEAD_SIZE = 64
FF = 1536
DEVICE_TOKENS = 128
MICRO = 2
DOC_MAX = 1000
STEP = 10
QKV_WIDTH = 960
QUERY_WIDTH = QUERY_HEADS * HEAD_SIZE
KV_WIDTH = KEY_VALUE_HEADS * HEAD_SIZE
OUT_FAN = 14
LANES = 128
HALF = LANES // 2
BLOCKS = 32
VMEM_LIMIT = 52 * 2**20

NORM_EPSILON = 1e-05
THETA = 100000.0
BETA_ONE = 0.9
BETA_TWO = 0.95
ADAM_EPSILON = 1e-08
MATRIX_DECAY = 0.1
RATE_FACTOR = 1.5
GAIN_RATE = 0.2
SCALE = HEAD_SIZE ** (-0.5)
BF16 = jnp.bfloat16
F32 = jnp.float32


def exchange(value, axis, bit, way=0):
    count = lax.axis_size(axis)
    pairs = [(place, place ^ bit) for place in range(count)]
    if way:
        pairs = [(source, target) for source, target in pairs if (target - source) * way > 0]
    return lax.ppermute(value, axis, pairs)


def add_up(kept, news, parts):
    size = kept.shape[0] // parts
    results = []
    for index in range(parts):
        rows = slice(index * size, (index + 1) * size)
        total = kept[rows].astype(F32)
        for new in news:
            total = total + new[rows].astype(F32)
        results.append(total.astype(BF16) if index else total)
    return results


def both_bits(total, axis, one, two):
    total = total + exchange(total, axis, one)
    return total + exchange(total, axis, two)


def together(*values):
    return lax.optimization_barrier(values)


def unit_norm(inputs):
    inverse_rms = lax.rsqrt(jnp.mean(inputs * inputs, axis=1, keepdims=True) + NORM_EPSILON)
    return (inputs * inverse_rms, inverse_rms)


def norm_backward(d_normed, unit_rows, inverse_rms, gain_row):
    scaled = d_normed * gain_row
    return inverse_rms * (
        scaled - unit_rows * jnp.mean(scaled * unit_rows, axis=1, keepdims=True)
    )


def matmul(equation, left, right):
    return jnp.einsum(equation, left, right, preferred_element_type=F32)


def params():
    return pltpu.CompilerParams(vmem_limit_bytes=VMEM_LIMIT)


def vmem(count):
    return [pl.BlockSpec(memory_space=pltpu.VMEM)] * count


def smem():
    return pl.BlockSpec(memory_space=pltpu.SMEM)


def dot(left, right):
    return jnp.dot(left, right, preferred_element_type=F32)


def dot_nt(left, right):
    return lax.dot_general(left, right, (((1,), (1,)), ((), ())), preferred_element_type=F32)


def dot_tn(left, right):
    return lax.dot_general(left, right, (((0,), (0,)), ((), ())), preferred_element_type=F32)


def shift_half(low, high):
    lane = lax.broadcasted_iota(jnp.int32, low.shape, 1)
    return pltpu.roll(jnp.where(lane < HALF, low, high), HALF, 1)


def unflatten_odd(flat, base, pairs, whole, planes):
    step = 2 * whole + 1

    def piece(k):
        return flat[pl.ds(base + k, pairs, stride=step), :]

    for j in range(whole + 1):
        planes[j, pl.ds(0, pairs, stride=2), :] = piece(j)
        planes[j, pl.ds(1, pairs, stride=2), :] = shift_half(
            piece(min(whole + 1 + j, 2 * whole)), piece(whole + j)
        )


def flatten_odd(planes, pairs, whole, flat, base):
    step = 2 * whole + 1

    def even(j):
        return planes[j, pl.ds(0, pairs, stride=2), :]

    def odd(j):
        return planes[j, pl.ds(1, pairs, stride=2), :]

    for k in range(step):
        if k < whole:
            rows = even(k)
        elif k == whole:
            first = odd(0)
            lane = lax.broadcasted_iota(jnp.int32, first.shape, 1)
            rows = jnp.where(lane < HALF, even(whole), pltpu.roll(first, HALF, 1))
        else:
            rows = shift_half(odd(k - whole), odd(k - whole - 1))
        flat[pl.ds(base + k, pairs, stride=step), :] = rows


def load_blocks(order, halves, flat):
    first = 0
    for blocks in halves:
        count, rows, unused = blocks.shape

        def move(place, unused, blocks=blocks, rows=rows, first=first):
            start = pl.multiple_of(order[first + place] * rows, 8)
            flat[pl.ds(start, rows), :] = blocks[place].astype(F32)
            return unused

        lax.fori_loop(0, count, move, 0)
        first += count


def store_blocks(order, flat, blocks, owner_rows, first_row, first_index):
    count, rows, unused = blocks.shape

    def move(index, unused):
        start = pl.multiple_of(order[first_index + index] * owner_rows + first_row, 8)
        blocks[index] = flat[pl.ds(start, rows), :].astype(BF16)
        return unused

    lax.fori_loop(0, count, move, 0)


def planes_to_matrix(planes, whole, matrix):
    for j in range(whole):
        matrix[:, j * LANES : (j + 1) * LANES] = planes[j].astype(BF16)
    matrix[:, whole * LANES : whole * LANES + HALF] = planes[whole, :, :HALF].astype(BF16)


def rotated(rows, cosine, sine):
    half_width = HEAD_SIZE // 2
    first, second = rows[:half_width], rows[half_width:]
    return jnp.concatenate([first * cosine - second * sine, second * cosine + first * sine], 0)


def three(rows, group):
    pieces = []
    for offset in range(GROUP):
        start = pl.multiple_of((group * GROUP + offset) * HEAD_SIZE, HEAD_SIZE)
        pieces.append(rows[pl.ds(start, HEAD_SIZE), :])
    return jnp.concatenate(pieces, 1)


def attention_forward_kernel(weight_count, input_count, order, *refs):
    weight_pieces, refs = refs[:weight_count], refs[weight_count:]
    input_pieces, refs = refs[:input_count], refs[input_count:]
    cosines, sines, bias, gains, w_project, w_output, normed, queries = refs[:8]
    keys_across, keys, values, log_totals, mixed_across, residual = refs[8:14]
    flat, planes_one, planes_two, w_across, values_across = refs[14:]
    load_blocks(order, weight_pieces, flat)
    unflatten_odd(flat, 0, D // 2, 7, planes_one)
    planes_to_matrix(planes_one, 7, w_project)
    for j in range(7):
        w_across[j * LANES : (j + 1) * LANES, :] = jnp.transpose(planes_one[j]).astype(BF16)
    w_across[7 * LANES :, :] = jnp.transpose(planes_one[7])[:HALF].astype(BF16)
    unflatten_odd(flat, D * QKV_WIDTH // LANES, QUERY_WIDTH // 2, 4, planes_two)
    planes_to_matrix(planes_two, 4, w_output)
    blocks = [piece.at[place] for piece in input_pieces for place in range(piece.shape[0])]
    gain = jnp.broadcast_to(gains[...], (D, DEVICE_TOKENS))

    def one(micro, unused):
        for block, inputs in enumerate(blocks):
            rows = inputs[micro].astype(F32)
            inverse = lax.rsqrt(jnp.mean(rows * rows, axis=0, keepdims=True) + NORM_EPSILON)
            normed[micro, :, block * DEVICE_TOKENS : (block + 1) * DEVICE_TOKENS] = (
                rows * inverse * gain
            ).astype(BF16)
        cosine, sine = cosines[micro], sines[micro]
        own_cosine, own_sine = cosine[:, :DEVICE_TOKENS], sine[:, :DEVICE_TOKENS]
        query = dot(w_across[:QUERY_WIDTH, :], normed[micro, :, :DEVICE_TOKENS])
        for head in range(QUERY_HEADS):
            rows = slice(head * HEAD_SIZE, (head + 1) * HEAD_SIZE)
            queries[micro, rows, :] = rotated(query[rows], own_cosine, own_sine).astype(BF16)
        other = dot(w_across[QUERY_WIDTH:, :], normed[micro])
        for head in range(KEY_VALUE_HEADS):
            rows = slice(head * HEAD_SIZE, (head + 1) * HEAD_SIZE)
            key = rotated(other[rows], cosine, sine)
            keys_across[micro, rows, :] = key.astype(BF16)
            keys[micro, head] = jnp.transpose(key).astype(BF16)
            value = other[KV_WIDTH + head * HEAD_SIZE : KV_WIDTH + (head + 1) * HEAD_SIZE]
            values_across[rows, :] = value.astype(BF16)
            values[micro, head] = jnp.transpose(value).astype(BF16)
        bias_three = jnp.concatenate([bias[micro]] * GROUP, 1)
        for group in range(KEY_VALUE_HEADS):
            group_rows = slice(group * HEAD_SIZE, (group + 1) * HEAD_SIZE)
            scores = dot(keys[micro, group], three(queries.at[micro], group) * SCALE) + bias_three
            top = jnp.max(scores, axis=0, keepdims=True)
            weights = jnp.exp(scores - top)
            total = jnp.sum(weights, axis=0, keepdims=True)
            low = (weights * (1.0 / total)).astype(BF16)
            mixed = dot(values_across[group_rows, :], low)
            log_total = top + jnp.log(total)
            for offset in range(GROUP):
                head = group * GROUP + offset
                lanes = slice(offset * DEVICE_TOKENS, (offset + 1) * DEVICE_TOKENS)
                mixed_across[micro, head * HEAD_SIZE : (head + 1) * HEAD_SIZE, :] = mixed[:, lanes]
                log_totals[micro, head : head + 1, :] = log_total[:, lanes]
        mixed = jnp.transpose(mixed_across[micro]).astype(BF16)
        inputs = jnp.transpose(blocks[0][micro].astype(F32))
        residual[micro] = inputs + dot(mixed, w_output[...])
        return unused

    lax.fori_loop(0, MICRO, one, 0)


def attention_forward(order, weight_pieces, input_pieces, *tables):
    window = sum(piece.shape[0] for piece in input_pieces) * DEVICE_TOKENS
    shape = jax.ShapeDtypeStruct
    rows = sum(piece.shape[0] * piece.shape[1] for piece in weight_pieces)
    return pl.pallas_call(
        functools.partial(attention_forward_kernel, len(weight_pieces), len(input_pieces)),
        out_shape=(
            shape((D, QKV_WIDTH), BF16),
            shape((QUERY_WIDTH, D), BF16),
            shape((MICRO, D, window), BF16),
            shape((MICRO, QUERY_WIDTH, DEVICE_TOKENS), BF16),
            shape((MICRO, KV_WIDTH, window), BF16),
            shape((MICRO, KEY_VALUE_HEADS, window, HEAD_SIZE), BF16),
            shape((MICRO, KEY_VALUE_HEADS, window, HEAD_SIZE), BF16),
            shape((MICRO, QUERY_HEADS, DEVICE_TOKENS), F32),
            shape((MICRO, QUERY_WIDTH, DEVICE_TOKENS), F32),
            shape((MICRO, DEVICE_TOKENS, D), F32),
        ),
        in_specs=[smem()] + vmem(len(weight_pieces) + len(input_pieces) + len(tables)),
        out_specs=tuple(vmem(10)),
        scratch_shapes=[
            pltpu.VMEM((rows, LANES), F32),
            pltpu.VMEM((8, D, LANES), F32),
            pltpu.VMEM((5, QUERY_WIDTH, LANES), F32),
            pltpu.VMEM((QKV_WIDTH, D), BF16),
            pltpu.VMEM((KV_WIDTH, window), BF16),
        ],
        compiler_params=params(),
    )(order, *weight_pieces, *input_pieces, *tables)


def feedforward_kernel(
    straight,
    order_one,
    order_two,
    weight_blocks,
    residual,
    cotangent,
    gains,
    block_output,
    d_branch,
    d_residual,
    one_kept,
    one_sent,
    two_kept,
    two_sent,
    gain_grad,
    flat,
    planes,
    w_gate_up,
    w_down,
    hidden,
    d_gate_up,
):
    columns = 2 * FF // LANES
    load_blocks(straight, (weight_blocks,), flat)
    for j in range(columns):
        w_gate_up[:, j * LANES : (j + 1) * LANES] = flat[
            pl.ds(j, D, stride=columns), :
        ].astype(BF16)
    unflatten_odd(flat, D * columns, FF // 2, 4, planes)
    planes_to_matrix(planes, 4, w_down)
    gain = gains[...]
    rows = jnp.concatenate([residual[micro] for micro in range(MICRO)], 0)
    inverse = lax.rsqrt(jnp.mean(rows * rows, axis=-1, keepdims=True) + NORM_EPSILON)
    unit = rows * inverse
    normed = (unit * gain).astype(BF16)
    cotangent_low = jnp.concatenate(
        [jnp.transpose(cotangent[micro].astype(F32)) for micro in range(MICRO)], 0
    ).astype(BF16)
    part = 256
    for start in range(0, FF, part):
        gate = dot(normed, w_gate_up[:, start : start + part])
        up = dot(normed, w_gate_up[:, FF + start : FF + start + part])
        d_hidden = dot_nt(cotangent_low, w_down[start : start + part, :])
        sigmoid = 1.0 / (1.0 + jnp.exp(-gate))
        activated = gate * sigmoid
        hidden[:, start : start + part] = (activated * up).astype(BF16)
        d_gate_up[:, start : start + part] = (
            d_hidden * up * sigmoid * (1.0 + gate * (1.0 - sigmoid))
        ).astype(BF16)
        d_gate_up[:, FF + start : FF + start + part] = (d_hidden * activated).astype(BF16)
    result = rows + dot(hidden[...], w_down[...])
    d_normed = dot_nt(d_gate_up[...], w_gate_up[...])
    scaled = d_normed * gain
    d_rows = cotangent_low.astype(F32) + inverse * (
        scaled - unit * jnp.mean(scaled * unit, axis=-1, keepdims=True)
    )
    d_branch[...] = d_rows.astype(BF16)
    for micro in range(MICRO):
        own = slice(micro * DEVICE_TOKENS, (micro + 1) * DEVICE_TOKENS)
        block_output[micro] = jnp.transpose(result[own]).astype(BF16)
        d_residual[micro] = jnp.transpose(d_rows[own])
    normed_across = jnp.transpose(unit * gain).astype(BF16)
    total = jnp.zeros((D, LANES), F32)
    for start in range(0, 2 * FF, part):
        grad = dot(normed_across, d_gate_up[:, start : start + part])
        for offset in range(0, part, LANES):
            piece = grad[:, offset : offset + LANES]
            place = start + offset
            total = total + piece * w_gate_up[:, place : place + LANES].astype(F32)
            flat[pl.ds(place // LANES, D, stride=columns), :] = piece
    gain_grad[...] = jnp.sum(total, axis=1, keepdims=True)
    for start in range(0, FF, part):
        grad = dot_tn(hidden[:, start : start + part], cotangent_low)
        for j in range(4):
            planes[j, start : start + part, :] = grad[:, j * LANES : (j + 1) * LANES]
        planes[4, start : start + part, :HALF] = grad[:, 4 * LANES :]
    flatten_odd(planes, FF // 2, 4, flat, D * columns)
    owner_rows = weight_blocks.shape[1]
    half = one_kept.shape[0]
    middle = one_kept.shape[1]
    store_blocks(order_one, flat, one_sent, owner_rows, 0, half)
    store_blocks(order_two, flat, two_sent, owner_rows, middle, half)
    store_blocks(order_one, flat, one_kept, owner_rows, 0, 0)
    store_blocks(order_two, flat, two_kept, owner_rows, middle, 0)


def feedforward(orders, weight_blocks, residual, cotangent, gains):
    shape = jax.ShapeDtypeStruct
    count, owner_rows, unused = weight_blocks.shape
    middle = owner_rows // 32 * 16
    one = shape((count // 2, middle, LANES), BF16)
    two = shape((count // 2, owner_rows - middle, LANES), BF16)
    tokens = residual.shape[0] * residual.shape[1]
    rows = weight_blocks.shape[0] * weight_blocks.shape[1]
    return pl.pallas_call(
        feedforward_kernel,
        out_shape=(
            shape((MICRO, D, DEVICE_TOKENS), BF16),
            shape((tokens, D), BF16),
            shape((MICRO, D, DEVICE_TOKENS), F32),
            one,
            one,
            two,
            two,
            shape((D, 1), F32),
        ),
        in_specs=[smem()] * 3 + vmem(4),
        out_specs=tuple(vmem(8)),
        scratch_shapes=[
            pltpu.VMEM((rows, LANES), F32),
            pltpu.VMEM((5, FF, LANES), F32),
            pltpu.VMEM((D, 2 * FF), BF16),
            pltpu.VMEM((FF, D), BF16),
            pltpu.VMEM((tokens, FF), BF16),
            pltpu.VMEM((tokens, 2 * FF), BF16),
        ],
        compiler_params=params(),
    )(*orders, weight_blocks, residual, cotangent, gains)


def attention_backward_body(
    w_output,
    normed,
    queries,
    keys_across,
    keys,
    values,
    log_totals,
    mixed_across,
    d_branch,
    cosines,
    sines,
    bias,
    d_queries,
    d_window,
    query_grad,
    window_grad,
    output_grad,
    d_window_across,
    d_mixed,
):
    blocks = d_window.shape[0]
    cosine, sine = cosines[...], sines[...]
    own_cosine, own_sine = cosine[:, :DEVICE_TOKENS], sine[:, :DEVICE_TOKENS]
    d_mixed[...] = dot_nt(w_output[...], d_branch[...]).astype(BF16)

    def one(group, unused):
        group_rows = pl.ds(pl.multiple_of(group * HEAD_SIZE, HEAD_SIZE), HEAD_SIZE)
        value_rows = pl.ds(pl.multiple_of(KV_WIDTH + group * HEAD_SIZE, HEAD_SIZE), HEAD_SIZE)
        query = three(queries, group) * SCALE
        d_heads = three(d_mixed, group)
        delta = jnp.sum(d_heads.astype(F32) * three(mixed_across, group), axis=0, keepdims=True)
        log_total = jnp.concatenate(
            [log_totals[pl.ds(group * GROUP + offset, 1), :] for offset in range(GROUP)], 1
        )
        bias_three = jnp.concatenate([bias[...]] * GROUP, 1)
        probability = jnp.exp(dot(keys[group], query) + bias_three - log_total)
        d_probs = dot(values[group], d_heads)
        d_scores = (probability * (d_probs - delta)).astype(BF16)
        d_query = dot(keys_across[group_rows, :], d_scores) * SCALE
        for offset in range(GROUP):
            lanes = slice(offset * DEVICE_TOKENS, (offset + 1) * DEVICE_TOKENS)
            start = pl.multiple_of((group * GROUP + offset) * HEAD_SIZE, HEAD_SIZE)
            d_queries[pl.ds(start, HEAD_SIZE), :] = rotated(
                d_query[:, lanes], own_cosine, -own_sine
            ).astype(BF16)
        d_key = dot_nt(query, d_scores)
        d_value = dot_nt(d_heads, probability.astype(BF16))
        d_window_across[group_rows, :] = rotated(d_key, cosine, -sine).astype(BF16)
        d_window_across[value_rows, :] = d_value.astype(BF16)
        return unused

    lax.fori_loop(0, KEY_VALUE_HEADS, one, 0)
    for block in range(blocks):
        d_window[block] = d_window_across[
            :, block * DEVICE_TOKENS : (block + 1) * DEVICE_TOKENS
        ]
    query_grad[...] = dot_nt(normed[:, :DEVICE_TOKENS], d_queries[...])
    window_grad[...] = dot_nt(normed[...], d_window_across[...])
    output_grad[...] = dot(mixed_across[...].astype(BF16), d_branch[...])


def micro_views(micro, operands):
    w_output, *views = operands
    views = [view.at[micro] for view in views]
    views[7] = operands[8].at[micro * DEVICE_TOKENS : (micro + 1) * DEVICE_TOKENS, :]
    return (w_output, *views)


def attention_backward_first(*refs):
    attention_backward_body(*micro_views(0, refs[:12]), *refs[12:])


def attention_backward_second(order, w_project, *refs):
    first_queries, first_window, *first_grads = refs[:5]
    operands, refs = refs[5:17], refs[17:]
    kept, sent, d_queries, window_kept, window_sent, gain_grad, flat, planes = refs[:8]
    across, d_mixed, own_window, query_grad, window_grad, output_grad = refs[8:]
    attention_backward_body(
        *micro_views(1, operands),
        d_queries.at[1],
        own_window,
        query_grad,
        window_grad,
        output_grad,
        across,
        d_mixed,
    )
    d_queries[0] = first_queries[...]
    early = window_kept.shape[0]
    for block in range(own_window.shape[0]):
        target, place = (window_kept, block) if block < early else (window_sent, block - early)
        target[place, 0] = first_window[block]
        target[place, 1] = own_window[block]
    for sums, first in zip((query_grad, window_grad, output_grad), first_grads):
        sums[...] += first[...]
    total = jnp.zeros((D, LANES), F32)
    later = [window_grad[:, j * LANES : (j + 1) * LANES] for j in range(3)]
    for j in range(7):
        if j < 4:
            piece = query_grad[:, j * LANES : (j + 1) * LANES]
        elif j == 4:
            piece = jnp.concatenate([query_grad[:, j * LANES :], later[0][:, :HALF]], 1)
        else:
            piece = shift_half(later[j - 4], later[j - 5])
        planes[j] = piece
        total = total + piece * w_project[:, j * LANES : (j + 1) * LANES].astype(F32)
    planes[7] = pltpu.roll(later[2], HALF, 1)
    last_sum = planes[7, :, :HALF] * w_project[:, 7 * LANES :].astype(F32)
    gain_grad[...] = jnp.sum(total, axis=1, keepdims=True) + jnp.sum(
        last_sum, axis=1, keepdims=True
    )
    flatten_odd(planes, D // 2, 7, flat, 0)
    for j in range(4):
        planes[j] = output_grad[:, j * LANES : (j + 1) * LANES]
    planes[4, :, :HALF] = output_grad[:, 4 * LANES :]
    flatten_odd(planes, QUERY_WIDTH // 2, 4, flat, D * QKV_WIDTH // LANES)
    store_blocks(order, flat, sent, sent.shape[1], 0, sent.shape[0])
    store_blocks(order, flat, kept, kept.shape[1], 0, 0)


def attention_backward(operands, count, rows, final=()):
    shape = jax.ShapeDtypeStruct
    window = operands[1].shape[2]
    blocks = window // DEVICE_TOKENS
    sums = [(D, QUERY_WIDTH), (D, 2 * KV_WIDTH), (QUERY_WIDTH, D)]
    scratch = [
        pltpu.VMEM((2 * KV_WIDTH, window), BF16),
        pltpu.VMEM((QUERY_WIDTH, DEVICE_TOKENS), BF16),
    ]
    if final:
        kernel = attention_backward_second
        half = shape((count // 2, rows, LANES), BF16)
        late = blocks // 2
        one_block = (MICRO, 2 * KV_WIDTH, DEVICE_TOKENS)
        outputs = (
            half,
            half,
            shape((MICRO, QUERY_WIDTH, DEVICE_TOKENS), BF16),
            shape((blocks - late, *one_block), BF16),
            shape((late, *one_block), BF16),
            shape((D, 1), F32),
        )
        scratch = [
            pltpu.VMEM((count * rows, LANES), F32),
            pltpu.VMEM((8, D, LANES), F32),
            *scratch,
            pltpu.VMEM((blocks, 2 * KV_WIDTH, DEVICE_TOKENS), BF16),
            *[pltpu.VMEM(dims, F32) for dims in sums],
        ]
        in_specs = [smem()] + vmem(len(final) - 1 + len(operands))
    else:
        kernel = attention_backward_first
        outputs = (
            shape((QUERY_WIDTH, DEVICE_TOKENS), BF16),
            shape((blocks, 2 * KV_WIDTH, DEVICE_TOKENS), BF16),
            *[shape(dims, F32) for dims in sums],
        )
        in_specs = vmem(len(operands))
    return pl.pallas_call(
        kernel,
        out_shape=outputs,
        in_specs=in_specs,
        out_specs=tuple(vmem(len(outputs))),
        scratch_shapes=scratch,
        compiler_params=params(),
    )(*final, *operands)


def adam_update(weights, moment, square, grad, rate, decay):
    new_moment = BETA_ONE * moment + (1.0 - BETA_ONE) * grad
    new_square = BETA_TWO * square + (1.0 - BETA_TWO) * grad * grad
    mean_hat = new_moment / (1.0 - BETA_ONE**STEP)
    square_hat = new_square / (1.0 - BETA_TWO**STEP)
    new_weights = weights - rate * (
        mean_hat / (jnp.sqrt(square_hat) + ADAM_EPSILON) + decay * weights
    )
    return (new_weights, new_moment, new_square)


def first_of(lengths, index):
    starts = jnp.cumsum(lengths, axis=-1) - lengths
    return jnp.max(
        jnp.where(starts[:, None, :] <= index[None, :, None], starts[:, None, :], 0), axis=-1
    )


def on_device(
    block_input,
    out_grad,
    doc_lengths,
    attention_weights,
    feedforward_weights,
    norm_gains,
    attention_moment,
    attention_square,
    feedforward_moment,
    feedforward_square,
    gain_moment,
    gain_square,
):
    both = ("dp", "seq")
    seq_count = lax.axis_size("seq")
    owner_count = lax.axis_size(both)
    seq_place = lax.axis_index("seq")
    owner_place = lax.axis_index(both)
    attention_length = attention_weights.shape[0]
    feedforward_length = feedforward_weights.shape[0]
    reach = min((DOC_MAX + DEVICE_TOKENS - 2) // DEVICE_TOKENS, seq_count - 1)
    dp_count = lax.axis_size("dp")
    butterfly = (
        seq_count == 8
        and reach == seq_count - 1
        and dp_count == 4
        and attention_length % (8 * LANES) == 0
    )
    pair = (0, 1)
    line = range(0, seq_count, 2)
    square = range(0, owner_count, seq_count)
    order = [c ^ r ^ s for c in pair for r in square for s in line]
    window_line = (0, 4, 2, 6)
    across_x, across_y = (0, seq_count), (0, 2 * seq_count)
    paths = [
        [c ^ one ^ two ^ s for c in pair for one in first for two in second for s in window_line]
        for first, second in ((across_x, across_y), (across_y, across_x))
    ]

    own_inputs = jnp.swapaxes(block_input[:, 0], 1, 2)
    straight = jnp.arange(BLOCKS, dtype=jnp.int32)
    tiled_rows = feedforward_length % (8 * LANES) == 0
    feedforward_low = feedforward_weights.astype(BF16)
    if tiled_rows:
        feedforward_low = feedforward_low.reshape(-1, LANES)
    feedforward_blocks = lax.all_gather(feedforward_low, both, axis=0, tiled=True)
    feedforward_blocks = feedforward_blocks.reshape(BLOCKS, -1, LANES)

    if butterfly:
        window_blocks = seq_place ^ jnp.array([c ^ s for c in pair for s in window_line], jnp.int32)
    else:
        window_blocks = seq_place - jnp.arange(reach + 1, dtype=jnp.int32)
    token = jnp.arange(DEVICE_TOKENS, dtype=jnp.int32)
    query_index = seq_place * DEVICE_TOKENS + token
    key_index = (window_blocks[:, None] * DEVICE_TOKENS + token[None, :]).reshape(-1)
    lengths = doc_lengths[:, 0]
    first_query = first_of(lengths, query_index)
    first_key = first_of(lengths, key_index)
    half_width = HEAD_SIZE // 2
    inverse = THETA ** (-(jnp.arange(half_width, dtype=F32) * 2.0) / HEAD_SIZE)
    position = (key_index[None] - first_key).astype(F32)
    angles = position[:, None, :] * inverse[None, :, None]
    cosines, sines = jnp.cos(angles), jnp.sin(angles)
    allowed = (key_index[None, :, None] >= first_query[:, None, :]) & (
        key_index[None, :, None] <= query_index[None, None, :]
    )
    bias = jnp.where(allowed, 0.0, -jnp.inf).astype(F32)

    attention_low = attention_weights.astype(BF16)
    if butterfly:
        orders = [jnp.array(path, jnp.int32) ^ owner_place for path in (order, *paths)]
        weights = attention_low.reshape(1, attention_length // LANES, LANES)
        window_inputs = own_inputs[None]
        inputs_far = exchange(window_inputs, "seq", 4, 1)
        far, cosines, sines, bias = together(exchange(weights, "seq", 2), cosines, sines, bias)
        weights = jnp.concatenate([weights, far], 0)
        weights = jnp.concatenate([weights, exchange(weights, "seq", 4)], 0)
        window_inputs = jnp.concatenate([window_inputs, inputs_far], 0)
        weights, window_inputs = together(weights, window_inputs)
        inputs_far = exchange(window_inputs, "seq", 2)
        weights = jnp.concatenate([weights, exchange(weights, "dp", 1)], 0)
        weight_pieces = [weights, exchange(weights, "dp", 2)]
        weight_pieces += [exchange(piece, "seq", 1) for piece in weight_pieces]
        input_pieces = [window_inputs, inputs_far]
        input_pieces += [exchange(piece, "seq", 1) for piece in input_pieces]
    else:
        weights = lax.all_gather(attention_low, both, axis=0, tiled=True)
        weights = weights.reshape(BLOCKS, -1, LANES)
        weight_pieces = jnp.split(weights, 4)
        window_inputs = jnp.stack(
            [own_inputs]
            + [
                lax.ppermute(
                    own_inputs, "seq", [(p, p + step) for p in range(seq_count - step)]
                )
                for step in range(1, reach + 1)
            ],
            0,
        )
        quarter = (reach + 1) // 4
        cuts = [0, quarter, 2 * quarter, 3 * quarter, reach + 1]
        input_pieces = [window_inputs[a:b] for a, b in zip(cuts, cuts[1:])]
        orders = [straight] * 3

    (
        w_project,
        w_output,
        normed_one,
        queries,
        keys_across,
        keys,
        values,
        log_totals,
        mixed_across,
        residual,
    ) = attention_forward(
        orders[0], weight_pieces, input_pieces, cosines, sines, bias, norm_gains[0][:, None]
    )
    block_output, d_branch, d_residual, *parts, gain_two = feedforward(
        (straight, *orders[1:]),
        feedforward_blocks,
        residual,
        jnp.swapaxes(out_grad[:, 0], 1, 2),
        norm_gains[1:2],
    )
    operands = (
        w_output,
        normed_one,
        queries,
        keys_across,
        keys,
        values,
        log_totals,
        mixed_across,
        d_branch,
        cosines,
        sines,
        bias,
    )
    attention_rows = D * (QKV_WIDTH + QUERY_WIDTH) // (LANES * BLOCKS)
    if butterfly:
        one_kept, one_sent, two_kept, two_sent = parts
        one_new, two_new = exchange(one_sent, "seq", 1), exchange(two_sent, "seq", 1)
        first = attention_backward(operands, BLOCKS, attention_rows)
        one_new, two_new, *first = together(one_new, two_new, *first)
        one_kept, one_sent = add_up(one_kept, [one_new], 2)
        two_kept, two_sent = add_up(two_kept, [two_new], 2)
        one_sent, two_sent, *first = together(one_sent, two_sent, *first)
        one_new, two_new = exchange(one_sent, "dp", 1), exchange(two_sent, "dp", 2)
        second = attention_backward(
            operands, BLOCKS, attention_rows, (orders[0], w_project, *first)
        )
        one_new, two_new, *second = together(one_new, two_new, *second)
        kept, sent, d_queries, window_kept, window_sent, gain_one = second
        one_kept, one_sent = add_up(one_kept, [one_new], 2)
        two_kept, two_sent = add_up(two_kept, [two_new], 2)
        gains_total = jnp.stack([gain_one[:, 0], gain_two[:, 0]], 0) / norm_gains

        new, one_new, two_new, window_new, gains_new = together(
            exchange(sent, "seq", 1),
            exchange(one_sent, "dp", 2),
            exchange(two_sent, "dp", 1),
            exchange(window_sent, "seq", 1),
            exchange(gains_total, "seq", 1),
        )
        kept, *sent = add_up(kept, [new], dp_count)
        one_kept, one_sent = add_up(one_kept, [one_new], 2)
        two_kept, two_sent = add_up(two_kept, [two_new], 2)
        window_kept, window_sent = add_up(window_kept, [window_new], 2)
        gains_total = gains_total + gains_new

        arrived = together(
            *[exchange(part, "dp", place) for place, part in enumerate(sent, 1)],
            both_bits(gains_total, "dp", 1, 2),
            exchange(one_sent, "seq", 2),
            exchange(two_sent, "seq", 2),
            exchange(window_sent, "seq", 2),
        )
        kept, *sent = add_up(kept, arrived[:3], len(line))
        gains_total = arrived[3]
        one_kept, one_sent = add_up(one_kept, [arrived[4]], 2)
        two_kept, two_sent = add_up(two_kept, [arrived[5]], 2)
        window_kept, window_sent = add_up(window_kept, [arrived[6]], 2)

        arrived = together(
            *[exchange(part, "seq", place) for place, part in zip(line[1:], sent)],
            both_bits(gains_total, "seq", 2, 4),
            exchange(one_sent, "seq", 4),
            exchange(two_sent, "seq", 4),
            exchange(window_sent, "seq", 4),
        )
        attention_owned = add_up(kept, arrived[:3], 1)[0].reshape(-1)
        gains_total = arrived[3]
        feedforward_owned = jnp.concatenate(
            [add_up(one_kept, [arrived[4]], 1)[0][0], add_up(two_kept, [arrived[5]], 1)[0][0]], 0
        ).reshape(-1)
        d_own = add_up(window_kept, [arrived[6]], 1)[0][0].astype(BF16)
    else:
        halves = [jnp.concatenate(parts[index : index + 2], 0) for index in (0, 2)]
        grads = jnp.concatenate(halves, 1).reshape(-1)
        feedforward_owned = lax.psum_scatter(grads, both, scatter_dimension=0, tiled=True)
        first = attention_backward(operands, BLOCKS, attention_rows)
        kept, sent, d_queries, window_kept, window_sent, gain_one = attention_backward(
            operands, BLOCKS, attention_rows, (orders[0], w_project, *first)
        )
        attention_owned = lax.psum_scatter(
            jnp.concatenate([kept, sent], 0).reshape(-1), both, scatter_dimension=0, tiled=True
        )
        d_window = jnp.concatenate([window_kept, window_sent], 0)
        d_own = d_window[0].astype(F32)
        for step in range(1, reach + 1):
            d_own = d_own + lax.ppermute(
                d_window[step], "seq", [(p, p - step) for p in range(step, seq_count)]
            ).astype(F32)
        d_own = d_own.astype(BF16)
        gains_total = jnp.stack([gain_one[:, 0], gain_two[:, 0]], 0) / norm_gains
        gains_total = lax.psum(gains_total, both)
    d_normed_one = matmul("de,met->mdt", w_project, jnp.concatenate([d_queries, d_own], 1))
    unit_one, inverse_one = unit_norm(own_inputs.astype(F32))
    input_grad = d_residual + norm_backward(
        d_normed_one, unit_one, inverse_one, norm_gains[0][None, :, None]
    )

    attention_place = owner_place * attention_length + jnp.arange(attention_length, dtype=jnp.int32)
    attention_rate = jnp.where(
        attention_place < D * QKV_WIDTH, RATE_FACTOR * D ** (-0.5), RATE_FACTOR * OUT_FAN ** (-0.5)
    )
    feedforward_place = owner_place * feedforward_length + jnp.arange(
        feedforward_length, dtype=jnp.int32
    )
    feedforward_rate = jnp.where(
        feedforward_place < 2 * D * FF, RATE_FACTOR * D ** (-0.5), RATE_FACTOR * FF ** (-0.5)
    )
    new_attention = adam_update(
        attention_weights,
        attention_moment,
        attention_square,
        attention_owned.astype(F32),
        attention_rate,
        MATRIX_DECAY,
    )
    new_feedforward = adam_update(
        feedforward_weights,
        feedforward_moment,
        feedforward_square,
        feedforward_owned.astype(F32),
        feedforward_rate,
        MATRIX_DECAY,
    )
    new_gains = adam_update(norm_gains, gain_moment, gain_square, gains_total, GAIN_RATE, 0.0)
    return (
        jnp.swapaxes(block_output, 1, 2)[:, None],
        jnp.swapaxes(input_grad, 1, 2)[:, None],
        *new_attention,
        *new_feedforward,
        *new_gains,
    )


def solution(mesh):
    tokens = P(None, "dp", "seq", None)
    flat = P(("dp", "seq"))
    return jax.shard_map(
        on_device,
        mesh=mesh,
        in_specs=(
            tokens,
            tokens,
            P(None, "dp", None),
            flat,
            flat,
            P(),
            flat,
            flat,
            flat,
            flat,
            P(),
            P(),
        ),
        out_specs=(tokens, tokens, flat, flat, flat, flat, flat, flat, P(), P(), P()),
        check_vma=False,
    )
```

```python
import functools

import jax
import jax.numpy as jnp
from jax import lax
from jax.experimental import pallas as pl
from jax.experimental.pallas import tpu as pltpu
from jax.sharding import PartitionSpec as P

D = 576
QUERY_HEADS = 9
KEY_VALUE_HEADS = 3
GROUP = QUERY_HEADS // KEY_VALUE_HEADS
HEAD_SIZE = 64
FF = 1536
DEVICE_TOKENS = 128
MICRO = 2
DOC_MAX = 1000
STEP = 10
QKV_WIDTH = 960
QUERY_WIDTH = QUERY_HEADS * HEAD_SIZE
KV_WIDTH = KEY_VALUE_HEADS * HEAD_SIZE
OUT_FAN = 14
LANES = 128
HALF = LANES // 2
BLOCKS = 32
VMEM_LIMIT = 52 * 2**20

NORM_EPSILON = 1e-05
THETA = 100000.0
BETA_ONE = 0.9
BETA_TWO = 0.95
ADAM_EPSILON = 1e-08
MATRIX_DECAY = 0.1
RATE_FACTOR = 1.5
GAIN_RATE = 0.2
SCALE = HEAD_SIZE ** (-0.5)
BF16 = jnp.bfloat16
F32 = jnp.float32


def exchange(value, axis, bit, way=0):
    count = lax.axis_size(axis)
    pairs = [(place, place ^ bit) for place in range(count)]
    if way:
        pairs = [(source, target) for source, target in pairs if (target - source) * way > 0]
    return lax.ppermute(value, axis, pairs)


def add_up(kept, news, parts):
    size = kept.shape[0] // parts
    results = []
    for index in range(parts):
        rows = slice(index * size, (index + 1) * size)
        total = kept[rows].astype(F32)
        for new in news:
            total = total + new[rows].astype(F32)
        results.append(total.astype(BF16) if index else total)
    return results


def both_bits(total, axis, one, two):
    total = total + exchange(total, axis, one)
    return total + exchange(total, axis, two)


def together(*values):
    return lax.optimization_barrier(values)


def unit_norm(inputs):
    inverse_rms = lax.rsqrt(jnp.mean(inputs * inputs, axis=1, keepdims=True) + NORM_EPSILON)
    return (inputs * inverse_rms, inverse_rms)


def norm_backward(d_normed, unit_rows, inverse_rms, gain_row):
    scaled = d_normed * gain_row
    return inverse_rms * (
        scaled - unit_rows * jnp.mean(scaled * unit_rows, axis=1, keepdims=True)
    )


def matmul(equation, left, right):
    return jnp.einsum(equation, left, right, preferred_element_type=F32)


def params():
    return pltpu.CompilerParams(vmem_limit_bytes=VMEM_LIMIT)


def vmem(count):
    return [pl.BlockSpec(memory_space=pltpu.VMEM)] * count


def smem():
    return pl.BlockSpec(memory_space=pltpu.SMEM)


def dot(left, right):
    return jnp.dot(left, right, preferred_element_type=F32)


def dot_nt(left, right):
    return lax.dot_general(left, right, (((1,), (1,)), ((), ())), preferred_element_type=F32)


def dot_tn(left, right):
    return lax.dot_general(left, right, (((0,), (0,)), ((), ())), preferred_element_type=F32)


def shift_half(low, high):
    lane = lax.broadcasted_iota(jnp.int32, low.shape, 1)
    return pltpu.roll(jnp.where(lane < HALF, low, high), HALF, 1)


def unflatten_odd(flat, base, pairs, whole, planes):
    step = 2 * whole + 1

    def piece(k):
        return flat[pl.ds(base + k, pairs, stride=step), :]

    for j in range(whole + 1):
        planes[j, pl.ds(0, pairs, stride=2), :] = piece(j)
        planes[j, pl.ds(1, pairs, stride=2), :] = shift_half(
            piece(min(whole + 1 + j, 2 * whole)), piece(whole + j)
        )


def flatten_odd(planes, pairs, whole, flat, base):
    step = 2 * whole + 1

    def even(j):
        return planes[j, pl.ds(0, pairs, stride=2), :]

    def odd(j):
        return planes[j, pl.ds(1, pairs, stride=2), :]

    for k in range(step):
        if k < whole:
            rows = even(k)
        elif k == whole:
            first = odd(0)
            lane = lax.broadcasted_iota(jnp.int32, first.shape, 1)
            rows = jnp.where(lane < HALF, even(whole), pltpu.roll(first, HALF, 1))
        else:
            rows = shift_half(odd(k - whole), odd(k - whole - 1))
        flat[pl.ds(base + k, pairs, stride=step), :] = rows


def load_blocks(order, halves, flat):
    first = 0
    for blocks in halves:
        count, rows, unused = blocks.shape

        def move(place, unused, blocks=blocks, rows=rows, first=first):
            start = pl.multiple_of(order[first + place] * rows, 8)
            flat[pl.ds(start, rows), :] = blocks[place].astype(F32)
            return unused

        lax.fori_loop(0, count, move, 0)
        first += count


def store_blocks(order, flat, blocks, owner_rows, first_row, first_index):
    count, rows, unused = blocks.shape

    def move(index, unused):
        start = pl.multiple_of(order[first_index + index] * owner_rows + first_row, 8)
        blocks[index] = flat[pl.ds(start, rows), :].astype(BF16)
        return unused

    lax.fori_loop(0, count, move, 0)


def planes_to_matrix(planes, whole, matrix):
    for j in range(whole):
        matrix[:, j * LANES : (j + 1) * LANES] = planes[j].astype(BF16)
    matrix[:, whole * LANES : whole * LANES + HALF] = planes[whole, :, :HALF].astype(BF16)


def rotated(rows, cosine, sine):
    half_width = HEAD_SIZE // 2
    first, second = rows[:half_width], rows[half_width:]
    return jnp.concatenate([first * cosine - second * sine, second * cosine + first * sine], 0)


def three(rows, group):
    pieces = []
    for offset in range(GROUP):
        start = pl.multiple_of((group * GROUP + offset) * HEAD_SIZE, HEAD_SIZE)
        pieces.append(rows[pl.ds(start, HEAD_SIZE), :])
    return jnp.concatenate(pieces, 1)


def attention_forward_kernel(weight_count, input_count, order, *refs):
    weight_pieces, refs = refs[:weight_count], refs[weight_count:]
    input_pieces, refs = refs[:input_count], refs[input_count:]
    cosines, sines, bias, gains, w_project, w_output, normed, queries = refs[:8]
    keys_across, keys, values, log_totals, mixed_across, residual = refs[8:14]
    flat, planes_one, planes_two, w_across, values_across = refs[14:]
    load_blocks(order, weight_pieces, flat)
    unflatten_odd(flat, 0, D // 2, 7, planes_one)
    planes_to_matrix(planes_one, 7, w_project)
    for j in range(7):
        w_across[j * LANES : (j + 1) * LANES, :] = jnp.transpose(planes_one[j]).astype(BF16)
    w_across[7 * LANES :, :] = jnp.transpose(planes_one[7])[:HALF].astype(BF16)
    unflatten_odd(flat, D * QKV_WIDTH // LANES, QUERY_WIDTH // 2, 4, planes_two)
    planes_to_matrix(planes_two, 4, w_output)
    blocks = [piece.at[place] for piece in input_pieces for place in range(piece.shape[0])]
    gain = jnp.broadcast_to(gains[...], (D, DEVICE_TOKENS))

    def one(micro, unused):
        for block, inputs in enumerate(blocks):
            rows = inputs[micro].astype(F32)
            inverse = lax.rsqrt(jnp.mean(rows * rows, axis=0, keepdims=True) + NORM_EPSILON)
            normed[micro, :, block * DEVICE_TOKENS : (block + 1) * DEVICE_TOKENS] = (
                rows * inverse * gain
            ).astype(BF16)
        cosine, sine = cosines[micro], sines[micro]
        own_cosine, own_sine = cosine[:, :DEVICE_TOKENS], sine[:, :DEVICE_TOKENS]
        query = dot(w_across[:QUERY_WIDTH, :], normed[micro, :, :DEVICE_TOKENS])
        for head in range(QUERY_HEADS):
            rows = slice(head * HEAD_SIZE, (head + 1) * HEAD_SIZE)
            queries[micro, rows, :] = rotated(query[rows], own_cosine, own_sine).astype(BF16)
        other = dot(w_across[QUERY_WIDTH:, :], normed[micro])
        for head in range(KEY_VALUE_HEADS):
            rows = slice(head * HEAD_SIZE, (head + 1) * HEAD_SIZE)
            key = rotated(other[rows], cosine, sine)
            keys_across[micro, rows, :] = key.astype(BF16)
            keys[micro, head] = jnp.transpose(key).astype(BF16)
            value = other[KV_WIDTH + head * HEAD_SIZE : KV_WIDTH + (head + 1) * HEAD_SIZE]
            values_across[rows, :] = value.astype(BF16)
            values[micro, head] = jnp.transpose(value).astype(BF16)
        bias_three = jnp.concatenate([bias[micro]] * GROUP, 1)
        for group in range(KEY_VALUE_HEADS):
            group_rows = slice(group * HEAD_SIZE, (group + 1) * HEAD_SIZE)
            scores = dot(keys[micro, group], three(queries.at[micro], group) * SCALE) + bias_three
            top = jnp.max(scores, axis=0, keepdims=True)
            weights = jnp.exp(scores - top)
            total = jnp.sum(weights, axis=0, keepdims=True)
            low = (weights * (1.0 / total)).astype(BF16)
            mixed = dot(values_across[group_rows, :], low)
            log_total = top + jnp.log(total)
            for offset in range(GROUP):
                head = group * GROUP + offset
                lanes = slice(offset * DEVICE_TOKENS, (offset + 1) * DEVICE_TOKENS)
                mixed_across[micro, head * HEAD_SIZE : (head + 1) * HEAD_SIZE, :] = mixed[:, lanes]
                log_totals[micro, head : head + 1, :] = log_total[:, lanes]
        mixed = jnp.transpose(mixed_across[micro]).astype(BF16)
        inputs = jnp.transpose(blocks[0][micro].astype(F32))
        residual[micro] = inputs + dot(mixed, w_output[...])
        return unused

    lax.fori_loop(0, MICRO, one, 0)


def attention_forward(order, weight_pieces, input_pieces, *tables):
    window = sum(piece.shape[0] for piece in input_pieces) * DEVICE_TOKENS
    shape = jax.ShapeDtypeStruct
    rows = sum(piece.shape[0] * piece.shape[1] for piece in weight_pieces)
    return pl.pallas_call(
        functools.partial(attention_forward_kernel, len(weight_pieces), len(input_pieces)),
        out_shape=(
            shape((D, QKV_WIDTH), BF16),
            shape((QUERY_WIDTH, D), BF16),
            shape((MICRO, D, window), BF16),
            shape((MICRO, QUERY_WIDTH, DEVICE_TOKENS), BF16),
            shape((MICRO, KV_WIDTH, window), BF16),
            shape((MICRO, KEY_VALUE_HEADS, window, HEAD_SIZE), BF16),
            shape((MICRO, KEY_VALUE_HEADS, window, HEAD_SIZE), BF16),
            shape((MICRO, QUERY_HEADS, DEVICE_TOKENS), F32),
            shape((MICRO, QUERY_WIDTH, DEVICE_TOKENS), F32),
            shape((MICRO, DEVICE_TOKENS, D), F32),
        ),
        in_specs=[smem()] + vmem(len(weight_pieces) + len(input_pieces) + len(tables)),
        out_specs=tuple(vmem(10)),
        scratch_shapes=[
            pltpu.VMEM((rows, LANES), F32),
            pltpu.VMEM((8, D, LANES), F32),
            pltpu.VMEM((5, QUERY_WIDTH, LANES), F32),
            pltpu.VMEM((QKV_WIDTH, D), BF16),
            pltpu.VMEM((KV_WIDTH, window), BF16),
        ],
        compiler_params=params(),
    )(order, *weight_pieces, *input_pieces, *tables)


def feedforward_kernel(
    straight,
    order_one,
    order_two,
    weight_blocks,
    residual,
    cotangent,
    gains,
    block_output,
    d_branch,
    d_residual,
    one_kept,
    one_sent,
    two_kept,
    two_sent,
    gain_grad,
    flat,
    planes,
    w_gate_up,
    w_down,
    hidden,
    d_gate_up,
):
    columns = 2 * FF // LANES
    load_blocks(straight, (weight_blocks,), flat)
    for j in range(columns):
        w_gate_up[:, j * LANES : (j + 1) * LANES] = flat[
            pl.ds(j, D, stride=columns), :
        ].astype(BF16)
    unflatten_odd(flat, D * columns, FF // 2, 4, planes)
    planes_to_matrix(planes, 4, w_down)
    gain = gains[...]
    rows = jnp.concatenate([residual[micro] for micro in range(MICRO)], 0)
    inverse = lax.rsqrt(jnp.mean(rows * rows, axis=-1, keepdims=True) + NORM_EPSILON)
    unit = rows * inverse
    normed = (unit * gain).astype(BF16)
    cotangent_low = jnp.concatenate(
        [jnp.transpose(cotangent[micro].astype(F32)) for micro in range(MICRO)], 0
    ).astype(BF16)
    part = 256
    for start in range(0, FF, part):
        gate = dot(normed, w_gate_up[:, start : start + part])
        up = dot(normed, w_gate_up[:, FF + start : FF + start + part])
        d_hidden = dot_nt(cotangent_low, w_down[start : start + part, :])
        sigmoid = 1.0 / (1.0 + jnp.exp(-gate))
        activated = gate * sigmoid
        hidden[:, start : start + part] = (activated * up).astype(BF16)
        d_gate_up[:, start : start + part] = (
            d_hidden * up * sigmoid * (1.0 + gate * (1.0 - sigmoid))
        ).astype(BF16)
        d_gate_up[:, FF + start : FF + start + part] = (d_hidden * activated).astype(BF16)
    result = rows + dot(hidden[...], w_down[...])
    d_normed = dot_nt(d_gate_up[...], w_gate_up[...])
    scaled = d_normed * gain
    d_rows = cotangent_low.astype(F32) + inverse * (
        scaled - unit * jnp.mean(scaled * unit, axis=-1, keepdims=True)
    )
    d_branch[...] = d_rows.astype(BF16)
    for micro in range(MICRO):
        own = slice(micro * DEVICE_TOKENS, (micro + 1) * DEVICE_TOKENS)
        block_output[micro] = jnp.transpose(result[own]).astype(BF16)
        d_residual[micro] = jnp.transpose(d_rows[own])
    normed_across = jnp.transpose(unit * gain).astype(BF16)
    total = jnp.zeros((D, LANES), F32)
    for start in range(0, 2 * FF, part):
        grad = dot(normed_across, d_gate_up[:, start : start + part])
        for offset in range(0, part, LANES):
            piece = grad[:, offset : offset + LANES]
            place = start + offset
            total = total + piece * w_gate_up[:, place : place + LANES].astype(F32)
            flat[pl.ds(place // LANES, D, stride=columns), :] = piece
    gain_grad[...] = jnp.sum(total, axis=1, keepdims=True)
    for start in range(0, FF, part):
        grad = dot_tn(hidden[:, start : start + part], cotangent_low)
        for j in range(4):
            planes[j, start : start + part, :] = grad[:, j * LANES : (j + 1) * LANES]
        planes[4, start : start + part, :HALF] = grad[:, 4 * LANES :]
    flatten_odd(planes, FF // 2, 4, flat, D * columns)
    owner_rows = weight_blocks.shape[1]
    half = one_kept.shape[0]
    middle = one_kept.shape[1]
    store_blocks(order_one, flat, one_sent, owner_rows, 0, half)
    store_blocks(order_two, flat, two_sent, owner_rows, middle, half)
    store_blocks(order_one, flat, one_kept, owner_rows, 0, 0)
    store_blocks(order_two, flat, two_kept, owner_rows, middle, 0)


def feedforward(orders, weight_blocks, residual, cotangent, gains):
    shape = jax.ShapeDtypeStruct
    count, owner_rows, unused = weight_blocks.shape
    middle = owner_rows // 32 * 16
    one = shape((count // 2, middle, LANES), BF16)
    two = shape((count // 2, owner_rows - middle, LANES), BF16)
    tokens = residual.shape[0] * residual.shape[1]
    rows = weight_blocks.shape[0] * weight_blocks.shape[1]
    return pl.pallas_call(
        feedforward_kernel,
        out_shape=(
            shape((MICRO, D, DEVICE_TOKENS), BF16),
            shape((tokens, D), BF16),
            shape((MICRO, D, DEVICE_TOKENS), F32),
            one,
            one,
            two,
            two,
            shape((D, 1), F32),
        ),
        in_specs=[smem()] * 3 + vmem(4),
        out_specs=tuple(vmem(8)),
        scratch_shapes=[
            pltpu.VMEM((rows, LANES), F32),
            pltpu.VMEM((5, FF, LANES), F32),
            pltpu.VMEM((D, 2 * FF), BF16),
            pltpu.VMEM((FF, D), BF16),
            pltpu.VMEM((tokens, FF), BF16),
            pltpu.VMEM((tokens, 2 * FF), BF16),
        ],
        compiler_params=params(),
    )(*orders, weight_blocks, residual, cotangent, gains)


def attention_backward_body(
    w_output,
    normed,
    queries,
    keys_across,
    keys,
    values,
    log_totals,
    mixed_across,
    d_branch,
    cosines,
    sines,
    bias,
    d_queries,
    d_window,
    query_grad,
    window_grad,
    output_grad,
    d_window_across,
    d_mixed,
):
    blocks = d_window.shape[0]
    cosine, sine = cosines[...], sines[...]
    own_cosine, own_sine = cosine[:, :DEVICE_TOKENS], sine[:, :DEVICE_TOKENS]
    d_mixed[...] = dot_nt(w_output[...], d_branch[...]).astype(BF16)

    def one(group, unused):
        group_rows = pl.ds(pl.multiple_of(group * HEAD_SIZE, HEAD_SIZE), HEAD_SIZE)
        value_rows = pl.ds(pl.multiple_of(KV_WIDTH + group * HEAD_SIZE, HEAD_SIZE), HEAD_SIZE)
        query = three(queries, group) * SCALE
        d_heads = three(d_mixed, group)
        delta = jnp.sum(d_heads.astype(F32) * three(mixed_across, group), axis=0, keepdims=True)
        log_total = jnp.concatenate(
            [log_totals[pl.ds(group * GROUP + offset, 1), :] for offset in range(GROUP)], 1
        )
        bias_three = jnp.concatenate([bias[...]] * GROUP, 1)
        probability = jnp.exp(dot(keys[group], query) + bias_three - log_total)
        d_probs = dot(values[group], d_heads)
        d_scores = (probability * (d_probs - delta)).astype(BF16)
        d_query = dot(keys_across[group_rows, :], d_scores) * SCALE
        for offset in range(GROUP):
            lanes = slice(offset * DEVICE_TOKENS, (offset + 1) * DEVICE_TOKENS)
            start = pl.multiple_of((group * GROUP + offset) * HEAD_SIZE, HEAD_SIZE)
            d_queries[pl.ds(start, HEAD_SIZE), :] = rotated(
                d_query[:, lanes], own_cosine, -own_sine
            ).astype(BF16)
        d_key = dot_nt(query, d_scores)
        d_value = dot_nt(d_heads, probability.astype(BF16))
        d_window_across[group_rows, :] = rotated(d_key, cosine, -sine).astype(BF16)
        d_window_across[value_rows, :] = d_value.astype(BF16)
        return unused

    lax.fori_loop(0, KEY_VALUE_HEADS, one, 0)
    for block in range(blocks):
        d_window[block] = d_window_across[
            :, block * DEVICE_TOKENS : (block + 1) * DEVICE_TOKENS
        ]
    query_grad[...] = dot_nt(normed[:, :DEVICE_TOKENS], d_queries[...])
    window_grad[...] = dot_nt(normed[...], d_window_across[...])
    output_grad[...] = dot(mixed_across[...].astype(BF16), d_branch[...])


def micro_views(micro, operands):
    w_output, *views = operands
    views = [view.at[micro] for view in views]
    views[7] = operands[8].at[micro * DEVICE_TOKENS : (micro + 1) * DEVICE_TOKENS, :]
    return (w_output, *views)


def attention_backward_first(*refs):
    attention_backward_body(*micro_views(0, refs[:12]), *refs[12:])


def attention_backward_second(order, w_project, *refs):
    first_queries, first_window, *first_grads = refs[:5]
    operands, refs = refs[5:17], refs[17:]
    kept, sent, d_queries, window_kept, window_sent, gain_grad, flat, planes = refs[:8]
    across, d_mixed, own_window, query_grad, window_grad, output_grad = refs[8:]
    attention_backward_body(
        *micro_views(1, operands),
        d_queries.at[1],
        own_window,
        query_grad,
        window_grad,
        output_grad,
        across,
        d_mixed,
    )
    d_queries[0] = first_queries[...]
    early = window_kept.shape[0]
    for block in range(own_window.shape[0]):
        target, place = (window_kept, block) if block < early else (window_sent, block - early)
        target[place, 0] = first_window[block]
        target[place, 1] = own_window[block]
    for sums, first in zip((query_grad, window_grad, output_grad), first_grads):
        sums[...] += first[...]
    total = jnp.zeros((D, LANES), F32)
    later = [window_grad[:, j * LANES : (j + 1) * LANES] for j in range(3)]
    for j in range(7):
        if j < 4:
            piece = query_grad[:, j * LANES : (j + 1) * LANES]
        elif j == 4:
            piece = jnp.concatenate([query_grad[:, j * LANES :], later[0][:, :HALF]], 1)
        else:
            piece = shift_half(later[j - 4], later[j - 5])
        planes[j] = piece
        total = total + piece * w_project[:, j * LANES : (j + 1) * LANES].astype(F32)
    planes[7] = pltpu.roll(later[2], HALF, 1)
    last_sum = planes[7, :, :HALF] * w_project[:, 7 * LANES :].astype(F32)
    gain_grad[...] = jnp.sum(total, axis=1, keepdims=True) + jnp.sum(
        last_sum, axis=1, keepdims=True
    )
    flatten_odd(planes, D // 2, 7, flat, 0)
    for j in range(4):
        planes[j] = output_grad[:, j * LANES : (j + 1) * LANES]
    planes[4, :, :HALF] = output_grad[:, 4 * LANES :]
    flatten_odd(planes, QUERY_WIDTH // 2, 4, flat, D * QKV_WIDTH // LANES)
    store_blocks(order, flat, sent, sent.shape[1], 0, sent.shape[0])
    store_blocks(order, flat, kept, kept.shape[1], 0, 0)


def attention_backward(operands, count, rows, final=()):
    shape = jax.ShapeDtypeStruct
    window = operands[1].shape[2]
    blocks = window // DEVICE_TOKENS
    sums = [(D, QUERY_WIDTH), (D, 2 * KV_WIDTH), (QUERY_WIDTH, D)]
    scratch = [
        pltpu.VMEM((2 * KV_WIDTH, window), BF16),
        pltpu.VMEM((QUERY_WIDTH, DEVICE_TOKENS), BF16),
    ]
    if final:
        kernel = attention_backward_second
        half = shape((count // 2, rows, LANES), BF16)
        late = blocks // 2
        one_block = (MICRO, 2 * KV_WIDTH, DEVICE_TOKENS)
        outputs = (
            half,
            half,
            shape((MICRO, QUERY_WIDTH, DEVICE_TOKENS), BF16),
            shape((blocks - late, *one_block), BF16),
            shape((late, *one_block), BF16),
            shape((D, 1), F32),
        )
        scratch = [
            pltpu.VMEM((count * rows, LANES), F32),
            pltpu.VMEM((8, D, LANES), F32),
            *scratch,
            pltpu.VMEM((blocks, 2 * KV_WIDTH, DEVICE_TOKENS), BF16),
            *[pltpu.VMEM(dims, F32) for dims in sums],
        ]
        in_specs = [smem()] + vmem(len(final) - 1 + len(operands))
    else:
        kernel = attention_backward_first
        outputs = (
            shape((QUERY_WIDTH, DEVICE_TOKENS), BF16),
            shape((blocks, 2 * KV_WIDTH, DEVICE_TOKENS), BF16),
            *[shape(dims, F32) for dims in sums],
        )
        in_specs = vmem(len(operands))
    return pl.pallas_call(
        kernel,
        out_shape=outputs,
        in_specs=in_specs,
        out_specs=tuple(vmem(len(outputs))),
        scratch_shapes=scratch,
        compiler_params=params(),
    )(*final, *operands)


def adam_update(weights, moment, square, grad, rate, decay):
    new_moment = BETA_ONE * moment + (1.0 - BETA_ONE) * grad
    new_square = BETA_TWO * square + (1.0 - BETA_TWO) * grad * grad
    mean_hat = new_moment / (1.0 - BETA_ONE**STEP)
    square_hat = new_square / (1.0 - BETA_TWO**STEP)
    new_weights = weights - rate * (
        mean_hat / (jnp.sqrt(square_hat) + ADAM_EPSILON) + decay * weights
    )
    return (new_weights, new_moment, new_square)


def first_of(lengths, index):
    starts = jnp.cumsum(lengths, axis=-1) - lengths
    return jnp.max(
        jnp.where(starts[:, None, :] <= index[None, :, None], starts[:, None, :], 0), axis=-1
    )


def on_device(
    block_input,
    out_grad,
    doc_lengths,
    attention_weights,
    feedforward_weights,
    norm_gains,
    attention_moment,
    attention_square,
    feedforward_moment,
    feedforward_square,
    gain_moment,
    gain_square,
):
    both = ("dp", "seq")
    seq_count = lax.axis_size("seq")
    owner_count = lax.axis_size(both)
    seq_place = lax.axis_index("seq")
    owner_place = lax.axis_index(both)
    attention_length = attention_weights.shape[0]
    feedforward_length = feedforward_weights.shape[0]
    reach = min((DOC_MAX + DEVICE_TOKENS - 2) // DEVICE_TOKENS, seq_count - 1)
    dp_count = lax.axis_size("dp")
    butterfly = (
        seq_count == 8
        and reach == seq_count - 1
        and dp_count == 4
        and attention_length % (8 * LANES) == 0
    )
    pair = (0, 1)
    line = range(0, seq_count, 2)
    square = range(0, owner_count, seq_count)
    order = [c ^ r ^ s for c in pair for r in square for s in line]
    window_line = (0, 4, 2, 6)
    across_x, across_y = (0, seq_count), (0, 2 * seq_count)
    paths = [
        [c ^ one ^ two ^ s for c in pair for one in first for two in second for s in window_line]
        for first, second in ((across_x, across_y), (across_y, across_x))
    ]

    own_inputs = jnp.swapaxes(block_input[:, 0], 1, 2)
    straight = jnp.arange(BLOCKS, dtype=jnp.int32)
    tiled_rows = feedforward_length % (8 * LANES) == 0
    feedforward_low = feedforward_weights.astype(BF16)
    if tiled_rows:
        feedforward_low = feedforward_low.reshape(-1, LANES)
    feedforward_blocks = lax.all_gather(feedforward_low, both, axis=0, tiled=True)
    feedforward_blocks = feedforward_blocks.reshape(BLOCKS, -1, LANES)

    if butterfly:
        window_blocks = seq_place ^ jnp.array([c ^ s for c in pair for s in window_line], jnp.int32)
    else:
        window_blocks = seq_place - jnp.arange(reach + 1, dtype=jnp.int32)
    token = jnp.arange(DEVICE_TOKENS, dtype=jnp.int32)
    query_index = seq_place * DEVICE_TOKENS + token
    key_index = (window_blocks[:, None] * DEVICE_TOKENS + token[None, :]).reshape(-1)
    lengths = doc_lengths[:, 0]
    first_query = first_of(lengths, query_index)
    first_key = first_of(lengths, key_index)
    half_width = HEAD_SIZE // 2
    inverse = THETA ** (-(jnp.arange(half_width, dtype=F32) * 2.0) / HEAD_SIZE)
    position = (key_index[None] - first_key).astype(F32)
    angles = position[:, None, :] * inverse[None, :, None]
    cosines, sines = jnp.cos(angles), jnp.sin(angles)
    allowed = (key_index[None, :, None] >= first_query[:, None, :]) & (
        key_index[None, :, None] <= query_index[None, None, :]
    )
    bias = jnp.where(allowed, 0.0, -jnp.inf).astype(F32)

    attention_low = attention_weights.astype(BF16)
    if butterfly:
        orders = [jnp.array(path, jnp.int32) ^ owner_place for path in (order, *paths)]
        weights = attention_low.reshape(1, attention_length // LANES, LANES)
        window_inputs = own_inputs[None]
        inputs_far = exchange(window_inputs, "seq", 4, 1)
        far, cosines, sines, bias = together(exchange(weights, "seq", 2), cosines, sines, bias)
        weights = jnp.concatenate([weights, far], 0)
        weights = jnp.concatenate([weights, exchange(weights, "seq", 4)], 0)
        window_inputs = jnp.concatenate([window_inputs, inputs_far], 0)
        weights, window_inputs = together(weights, window_inputs)
        inputs_far = exchange(window_inputs, "seq", 2)
        weights = jnp.concatenate([weights, exchange(weights, "dp", 1)], 0)
        weight_pieces = [weights, exchange(weights, "dp", 2)]
        weight_pieces += [exchange(piece, "seq", 1) for piece in weight_pieces]
        input_pieces = [window_inputs, inputs_far]
        input_pieces += [exchange(piece, "seq", 1) for piece in input_pieces]
    else:
        weights = lax.all_gather(attention_low, both, axis=0, tiled=True)
        weights = weights.reshape(BLOCKS, -1, LANES)
        weight_pieces = jnp.split(weights, 4)
        window_inputs = jnp.stack(
            [own_inputs]
            + [
                lax.ppermute(
                    own_inputs, "seq", [(p, p + step) for p in range(seq_count - step)]
                )
                for step in range(1, reach + 1)
            ],
            0,
        )
        quarter = (reach + 1) // 4
        cuts = [0, quarter, 2 * quarter, 3 * quarter, reach + 1]
        input_pieces = [window_inputs[a:b] for a, b in zip(cuts, cuts[1:])]
        orders = [straight] * 3

    (
        w_project,
        w_output,
        normed_one,
        queries,
        keys_across,
        keys,
        values,
        log_totals,
        mixed_across,
        residual,
    ) = attention_forward(
        orders[0], weight_pieces, input_pieces, cosines, sines, bias, norm_gains[0][:, None]
    )
    block_output, d_branch, d_residual, *parts, gain_two = feedforward(
        (straight, *orders[1:]),
        feedforward_blocks,
        residual,
        jnp.swapaxes(out_grad[:, 0], 1, 2),
        norm_gains[1:2],
    )
    operands = (
        w_output,
        normed_one,
        queries,
        keys_across,
        keys,
        values,
        log_totals,
        mixed_across,
        d_branch,
        cosines,
        sines,
        bias,
    )
    attention_rows = D * (QKV_WIDTH + QUERY_WIDTH) // (LANES * BLOCKS)
    if butterfly:
        one_kept, one_sent, two_kept, two_sent = parts
        one_new, two_new = exchange(one_sent, "seq", 1), exchange(two_sent, "seq", 1)
        first = attention_backward(operands, BLOCKS, attention_rows)
        one_new, two_new, *first = together(one_new, two_new, *first)
        one_kept, one_sent = add_up(one_kept, [one_new], 2)
        two_kept, two_sent = add_up(two_kept, [two_new], 2)
        one_sent, two_sent, *first = together(one_sent, two_sent, *first)
        one_new, two_new = exchange(one_sent, "dp", 1), exchange(two_sent, "dp", 2)
        second = attention_backward(
            operands, BLOCKS, attention_rows, (orders[0], w_project, *first)
        )
        one_new, two_new, *second = together(one_new, two_new, *second)
        kept, sent, d_queries, window_kept, window_sent, gain_one = second
        one_kept, one_sent = add_up(one_kept, [one_new], 2)
        two_kept, two_sent = add_up(two_kept, [two_new], 2)
        gains_total = jnp.stack([gain_one[:, 0], gain_two[:, 0]], 0) / norm_gains

        new, one_new, two_new, window_new, gains_new = together(
            exchange(sent, "seq", 1),
            exchange(one_sent, "dp", 2),
            exchange(two_sent, "dp", 1),
            exchange(window_sent, "seq", 1),
            exchange(gains_total, "seq", 1),
        )
        kept, sent = add_up(kept, [new], 2)
        one_kept, one_sent = add_up(one_kept, [one_new], 2)
        two_kept, two_sent = add_up(two_kept, [two_new], 2)
        window_kept, window_sent = add_up(window_kept, [window_new], 2)
        gains_total = gains_total + gains_new

        new, one_new, two_new, window_new, gains_new = together(
            exchange(sent, "dp", 2),
            exchange(one_sent, "seq", 2),
            exchange(two_sent, "seq", 2),
            exchange(window_sent, "seq", 2),
            exchange(gains_total, "dp", 2),
        )
        kept, sent = add_up(kept, [new], 2)
        one_kept, one_sent = add_up(one_kept, [one_new], 2)
        two_kept, two_sent = add_up(two_kept, [two_new], 2)
        window_kept, window_sent = add_up(window_kept, [window_new], 2)
        gains_total = gains_total + gains_new

        new, one_new, two_new, window_new, gains_new = together(
            exchange(sent, "dp", 1),
            exchange(one_sent, "seq", 4),
            exchange(two_sent, "seq", 4),
            exchange(window_sent, "seq", 4),
            exchange(gains_total, "dp", 1),
        )
        kept, *sent = add_up(kept, [new], len(line))
        gains_total = gains_total + gains_new
        feedforward_owned = jnp.concatenate(
            [add_up(one_kept, [one_new], 1)[0][0], add_up(two_kept, [two_new], 1)[0][0]], 0
        ).reshape(-1)
        d_own = add_up(window_kept, [window_new], 1)[0][0].astype(BF16)

        news = [exchange(part, "seq", place) for place, part in zip(line[1:], sent)]
        gains_total = both_bits(gains_total, "seq", 2, 4)
        attention_owned = add_up(kept, news, 1)[0].reshape(-1)
    else:
        halves = [jnp.concatenate(parts[index : index + 2], 0) for index in (0, 2)]
        grads = jnp.concatenate(halves, 1).reshape(-1)
        feedforward_owned = lax.psum_scatter(grads, both, scatter_dimension=0, tiled=True)
        first = attention_backward(operands, BLOCKS, attention_rows)
        kept, sent, d_queries, window_kept, window_sent, gain_one = attention_backward(
            operands, BLOCKS, attention_rows, (orders[0], w_project, *first)
        )
        attention_owned = lax.psum_scatter(
            jnp.concatenate([kept, sent], 0).reshape(-1), both, scatter_dimension=0, tiled=True
        )
        d_window = jnp.concatenate([window_kept, window_sent], 0)
        d_own = d_window[0].astype(F32)
        for step in range(1, reach + 1):
            d_own = d_own + lax.ppermute(
                d_window[step], "seq", [(p, p - step) for p in range(step, seq_count)]
            ).astype(F32)
        d_own = d_own.astype(BF16)
        gains_total = jnp.stack([gain_one[:, 0], gain_two[:, 0]], 0) / norm_gains
        gains_total = lax.psum(gains_total, both)
    d_normed_one = matmul("de,met->mdt", w_project, jnp.concatenate([d_queries, d_own], 1))
    unit_one, inverse_one = unit_norm(own_inputs.astype(F32))
    input_grad = d_residual + norm_backward(
        d_normed_one, unit_one, inverse_one, norm_gains[0][None, :, None]
    )

    attention_place = owner_place * attention_length + jnp.arange(attention_length, dtype=jnp.int32)
    attention_rate = jnp.where(
        attention_place < D * QKV_WIDTH, RATE_FACTOR * D ** (-0.5), RATE_FACTOR * OUT_FAN ** (-0.5)
    )
    feedforward_place = owner_place * feedforward_length + jnp.arange(
        feedforward_length, dtype=jnp.int32
    )
    feedforward_rate = jnp.where(
        feedforward_place < 2 * D * FF, RATE_FACTOR * D ** (-0.5), RATE_FACTOR * FF ** (-0.5)
    )
    new_attention = adam_update(
        attention_weights,
        attention_moment,
        attention_square,
        attention_owned.astype(F32),
        attention_rate,
        MATRIX_DECAY,
    )
    new_feedforward = adam_update(
        feedforward_weights,
        feedforward_moment,
        feedforward_square,
        feedforward_owned.astype(F32),
        feedforward_rate,
        MATRIX_DECAY,
    )
    new_gains = adam_update(norm_gains, gain_moment, gain_square, gains_total, GAIN_RATE, 0.0)
    return (
        jnp.swapaxes(block_output, 1, 2)[:, None],
        jnp.swapaxes(input_grad, 1, 2)[:, None],
        *new_attention,
        *new_feedforward,
        *new_gains,
    )


def solution(mesh):
    tokens = P(None, "dp", "seq", None)
    flat = P(("dp", "seq"))
    return jax.shard_map(
        on_device,
        mesh=mesh,
        in_specs=(
            tokens,
            tokens,
            P(None, "dp", None),
            flat,
            flat,
            P(),
            flat,
            flat,
            flat,
            flat,
            P(),
            P(),
        ),
        out_specs=(tokens, tokens, flat, flat, flat, flat, flat, flat, P(), P(), P()),
        check_vma=False,
    )
```

```python
import functools

import jax
import jax.numpy as jnp
from jax import lax
from jax.experimental import pallas as pl
from jax.experimental.pallas import tpu as pltpu
from jax.sharding import PartitionSpec as P

D = 576
QUERY_HEADS = 9
KEY_VALUE_HEADS = 3
GROUP = QUERY_HEADS // KEY_VALUE_HEADS
HEAD_SIZE = 64
FF = 1536
DEVICE_TOKENS = 128
MICRO = 2
DOC_MAX = 1000
STEP = 10
QKV_WIDTH = 960
QUERY_WIDTH = QUERY_HEADS * HEAD_SIZE
KV_WIDTH = KEY_VALUE_HEADS * HEAD_SIZE
OUT_FAN = 14
LANES = 128
HALF = LANES // 2
BLOCKS = 32
VMEM_LIMIT = 52 * 2**20

NORM_EPSILON = 1e-05
THETA = 100000.0
BETA_ONE = 0.9
BETA_TWO = 0.95
ADAM_EPSILON = 1e-08
MATRIX_DECAY = 0.1
RATE_FACTOR = 1.5
GAIN_RATE = 0.2
SCALE = HEAD_SIZE ** (-0.5)
BF16 = jnp.bfloat16
F32 = jnp.float32


def exchange(value, axis, bit, way=0):
    count = lax.axis_size(axis)
    pairs = [(place, place ^ bit) for place in range(count)]
    if way:
        pairs = [(source, target) for source, target in pairs if (target - source) * way > 0]
    return lax.ppermute(value, axis, pairs)


def add_up(kept, news, parts):
    size = kept.shape[0] // parts
    results = []
    for index in range(parts):
        rows = slice(index * size, (index + 1) * size)
        total = kept[rows].astype(F32)
        for new in news:
            total = total + new[rows].astype(F32)
        results.append(total.astype(BF16) if index else total)
    return results


def together(*values):
    return lax.optimization_barrier(values)


def unit_norm(inputs):
    inverse_rms = lax.rsqrt(jnp.mean(inputs * inputs, axis=1, keepdims=True) + NORM_EPSILON)
    return (inputs * inverse_rms, inverse_rms)


def norm_backward(d_normed, unit_rows, inverse_rms, gain_row):
    scaled = d_normed * gain_row
    return inverse_rms * (
        scaled - unit_rows * jnp.mean(scaled * unit_rows, axis=1, keepdims=True)
    )


def matmul(equation, left, right):
    return jnp.einsum(equation, left, right, preferred_element_type=F32)


def params():
    return pltpu.CompilerParams(vmem_limit_bytes=VMEM_LIMIT)


def vmem(count):
    return [pl.BlockSpec(memory_space=pltpu.VMEM)] * count


def smem():
    return pl.BlockSpec(memory_space=pltpu.SMEM)


def dot(left, right):
    return jnp.dot(left, right, preferred_element_type=F32)


def dot_nt(left, right):
    return lax.dot_general(left, right, (((1,), (1,)), ((), ())), preferred_element_type=F32)


def dot_tn(left, right):
    return lax.dot_general(left, right, (((0,), (0,)), ((), ())), preferred_element_type=F32)


def shift_half(low, high):
    lane = lax.broadcasted_iota(jnp.int32, low.shape, 1)
    return pltpu.roll(jnp.where(lane < HALF, low, high), HALF, 1)


def unflatten_odd(flat, base, pairs, whole, planes):
    step = 2 * whole + 1

    def piece(k):
        return flat[pl.ds(base + k, pairs, stride=step), :]

    for j in range(whole + 1):
        planes[j, pl.ds(0, pairs, stride=2), :] = piece(j)
        planes[j, pl.ds(1, pairs, stride=2), :] = shift_half(
            piece(min(whole + 1 + j, 2 * whole)), piece(whole + j)
        )


def flatten_odd(planes, pairs, whole, flat, base):
    step = 2 * whole + 1

    def even(j):
        return planes[j, pl.ds(0, pairs, stride=2), :]

    def odd(j):
        return planes[j, pl.ds(1, pairs, stride=2), :]

    for k in range(step):
        if k < whole:
            rows = even(k)
        elif k == whole:
            first = odd(0)
            lane = lax.broadcasted_iota(jnp.int32, first.shape, 1)
            rows = jnp.where(lane < HALF, even(whole), pltpu.roll(first, HALF, 1))
        else:
            rows = shift_half(odd(k - whole), odd(k - whole - 1))
        flat[pl.ds(base + k, pairs, stride=step), :] = rows


def load_blocks(order, halves, flat):
    first = 0
    for blocks in halves:
        count, rows, unused = blocks.shape

        def move(place, unused, blocks=blocks, rows=rows, first=first):
            start = pl.multiple_of(order[first + place] * rows, 8)
            flat[pl.ds(start, rows), :] = blocks[place].astype(F32)
            return unused

        lax.fori_loop(0, count, move, 0)
        first += count


def store_blocks(order, flat, blocks, owner_rows, first_row, first_index):
    count, rows, unused = blocks.shape

    def move(index, unused):
        start = pl.multiple_of(order[first_index + index] * owner_rows + first_row, 8)
        blocks[index] = flat[pl.ds(start, rows), :].astype(BF16)
        return unused

    lax.fori_loop(0, count, move, 0)


def planes_to_matrix(planes, whole, matrix):
    for j in range(whole):
        matrix[:, j * LANES : (j + 1) * LANES] = planes[j].astype(BF16)
    matrix[:, whole * LANES : whole * LANES + HALF] = planes[whole, :, :HALF].astype(BF16)


def rotated(rows, cosine, sine):
    half_width = HEAD_SIZE // 2
    first, second = rows[:half_width], rows[half_width:]
    return jnp.concatenate([first * cosine - second * sine, second * cosine + first * sine], 0)


def three(rows, group):
    pieces = []
    for offset in range(GROUP):
        start = pl.multiple_of((group * GROUP + offset) * HEAD_SIZE, HEAD_SIZE)
        pieces.append(rows[pl.ds(start, HEAD_SIZE), :])
    return jnp.concatenate(pieces, 1)


def attention_forward_kernel(weight_count, input_count, order, *refs):
    weight_pieces, refs = refs[:weight_count], refs[weight_count:]
    input_pieces, refs = refs[:input_count], refs[input_count:]
    cosines, sines, bias, gains, w_project, w_output, normed, queries = refs[:8]
    keys_across, keys, values, log_totals, mixed_across, residual = refs[8:14]
    flat, planes_one, planes_two, w_across, values_across = refs[14:]
    load_blocks(order, weight_pieces, flat)
    unflatten_odd(flat, 0, D // 2, 7, planes_one)
    planes_to_matrix(planes_one, 7, w_project)
    for j in range(7):
        w_across[j * LANES : (j + 1) * LANES, :] = jnp.transpose(planes_one[j]).astype(BF16)
    w_across[7 * LANES :, :] = jnp.transpose(planes_one[7])[:HALF].astype(BF16)
    unflatten_odd(flat, D * QKV_WIDTH // LANES, QUERY_WIDTH // 2, 4, planes_two)
    planes_to_matrix(planes_two, 4, w_output)
    blocks = [piece.at[place] for piece in input_pieces for place in range(piece.shape[0])]
    gain = jnp.broadcast_to(gains[...], (D, DEVICE_TOKENS))

    def one(micro, unused):
        for block, inputs in enumerate(blocks):
            rows = inputs[micro].astype(F32)
            inverse = lax.rsqrt(jnp.mean(rows * rows, axis=0, keepdims=True) + NORM_EPSILON)
            normed[micro, :, block * DEVICE_TOKENS : (block + 1) * DEVICE_TOKENS] = (
                rows * inverse * gain
            ).astype(BF16)
        cosine, sine = cosines[micro], sines[micro]
        own_cosine, own_sine = cosine[:, :DEVICE_TOKENS], sine[:, :DEVICE_TOKENS]
        query = dot(w_across[:QUERY_WIDTH, :], normed[micro, :, :DEVICE_TOKENS])
        for head in range(QUERY_HEADS):
            rows = slice(head * HEAD_SIZE, (head + 1) * HEAD_SIZE)
            queries[micro, rows, :] = rotated(query[rows], own_cosine, own_sine).astype(BF16)
        other = dot(w_across[QUERY_WIDTH:, :], normed[micro])
        for head in range(KEY_VALUE_HEADS):
            rows = slice(head * HEAD_SIZE, (head + 1) * HEAD_SIZE)
            key = rotated(other[rows], cosine, sine)
            keys_across[micro, rows, :] = key.astype(BF16)
            keys[micro, head] = jnp.transpose(key).astype(BF16)
            value = other[KV_WIDTH + head * HEAD_SIZE : KV_WIDTH + (head + 1) * HEAD_SIZE]
            values_across[rows, :] = value.astype(BF16)
            values[micro, head] = jnp.transpose(value).astype(BF16)
        bias_three = jnp.concatenate([bias[micro]] * GROUP, 1)
        for group in range(KEY_VALUE_HEADS):
            group_rows = slice(group * HEAD_SIZE, (group + 1) * HEAD_SIZE)
            scores = dot(keys[micro, group], three(queries.at[micro], group) * SCALE) + bias_three
            top = jnp.max(scores, axis=0, keepdims=True)
            weights = jnp.exp(scores - top)
            total = jnp.sum(weights, axis=0, keepdims=True)
            low = (weights * (1.0 / total)).astype(BF16)
            mixed = dot(values_across[group_rows, :], low)
            log_total = top + jnp.log(total)
            for offset in range(GROUP):
                head = group * GROUP + offset
                lanes = slice(offset * DEVICE_TOKENS, (offset + 1) * DEVICE_TOKENS)
                mixed_across[micro, head * HEAD_SIZE : (head + 1) * HEAD_SIZE, :] = mixed[:, lanes]
                log_totals[micro, head : head + 1, :] = log_total[:, lanes]
        mixed = jnp.transpose(mixed_across[micro]).astype(BF16)
        inputs = jnp.transpose(blocks[0][micro].astype(F32))
        residual[micro] = inputs + dot(mixed, w_output[...])
        return unused

    lax.fori_loop(0, MICRO, one, 0)


def attention_forward(order, weight_pieces, input_pieces, *tables):
    window = sum(piece.shape[0] for piece in input_pieces) * DEVICE_TOKENS
    shape = jax.ShapeDtypeStruct
    rows = sum(piece.shape[0] * piece.shape[1] for piece in weight_pieces)
    return pl.pallas_call(
        functools.partial(attention_forward_kernel, len(weight_pieces), len(input_pieces)),
        out_shape=(
            shape((D, QKV_WIDTH), BF16),
            shape((QUERY_WIDTH, D), BF16),
            shape((MICRO, D, window), BF16),
            shape((MICRO, QUERY_WIDTH, DEVICE_TOKENS), BF16),
            shape((MICRO, KV_WIDTH, window), BF16),
            shape((MICRO, KEY_VALUE_HEADS, window, HEAD_SIZE), BF16),
            shape((MICRO, KEY_VALUE_HEADS, window, HEAD_SIZE), BF16),
            shape((MICRO, QUERY_HEADS, DEVICE_TOKENS), F32),
            shape((MICRO, QUERY_WIDTH, DEVICE_TOKENS), F32),
            shape((MICRO, DEVICE_TOKENS, D), F32),
        ),
        in_specs=[smem()] + vmem(len(weight_pieces) + len(input_pieces) + len(tables)),
        out_specs=tuple(vmem(10)),
        scratch_shapes=[
            pltpu.VMEM((rows, LANES), F32),
            pltpu.VMEM((8, D, LANES), F32),
            pltpu.VMEM((5, QUERY_WIDTH, LANES), F32),
            pltpu.VMEM((QKV_WIDTH, D), BF16),
            pltpu.VMEM((KV_WIDTH, window), BF16),
        ],
        compiler_params=params(),
    )(order, *weight_pieces, *input_pieces, *tables)


def feedforward_kernel(
    straight,
    order_one,
    order_two,
    weight_blocks,
    residual,
    cotangent,
    gains,
    block_output,
    d_branch,
    d_residual,
    one_kept,
    one_sent,
    two_kept,
    two_sent,
    gain_grad,
    flat,
    planes,
    w_gate_up,
    w_down,
    hidden,
    d_gate_up,
):
    columns = 2 * FF // LANES
    load_blocks(straight, (weight_blocks,), flat)
    for j in range(columns):
        w_gate_up[:, j * LANES : (j + 1) * LANES] = flat[
            pl.ds(j, D, stride=columns), :
        ].astype(BF16)
    unflatten_odd(flat, D * columns, FF // 2, 4, planes)
    planes_to_matrix(planes, 4, w_down)
    gain = gains[...]
    rows = jnp.concatenate([residual[micro] for micro in range(MICRO)], 0)
    inverse = lax.rsqrt(jnp.mean(rows * rows, axis=-1, keepdims=True) + NORM_EPSILON)
    unit = rows * inverse
    normed = (unit * gain).astype(BF16)
    cotangent_low = jnp.concatenate(
        [jnp.transpose(cotangent[micro].astype(F32)) for micro in range(MICRO)], 0
    ).astype(BF16)
    part = 256
    for start in range(0, FF, part):
        gate = dot(normed, w_gate_up[:, start : start + part])
        up = dot(normed, w_gate_up[:, FF + start : FF + start + part])
        d_hidden = dot_nt(cotangent_low, w_down[start : start + part, :])
        sigmoid = 1.0 / (1.0 + jnp.exp(-gate))
        activated = gate * sigmoid
        hidden[:, start : start + part] = (activated * up).astype(BF16)
        d_gate_up[:, start : start + part] = (
            d_hidden * up * sigmoid * (1.0 + gate * (1.0 - sigmoid))
        ).astype(BF16)
        d_gate_up[:, FF + start : FF + start + part] = (d_hidden * activated).astype(BF16)
    result = rows + dot(hidden[...], w_down[...])
    d_normed = dot_nt(d_gate_up[...], w_gate_up[...])
    scaled = d_normed * gain
    d_rows = cotangent_low.astype(F32) + inverse * (
        scaled - unit * jnp.mean(scaled * unit, axis=-1, keepdims=True)
    )
    d_branch[...] = d_rows.astype(BF16)
    for micro in range(MICRO):
        own = slice(micro * DEVICE_TOKENS, (micro + 1) * DEVICE_TOKENS)
        block_output[micro] = jnp.transpose(result[own]).astype(BF16)
        d_residual[micro] = jnp.transpose(d_rows[own])
    normed_across = jnp.transpose(unit * gain).astype(BF16)
    total = jnp.zeros((D, LANES), F32)
    for start in range(0, 2 * FF, part):
        grad = dot(normed_across, d_gate_up[:, start : start + part])
        for offset in range(0, part, LANES):
            piece = grad[:, offset : offset + LANES]
            place = start + offset
            total = total + piece * w_gate_up[:, place : place + LANES].astype(F32)
            flat[pl.ds(place // LANES, D, stride=columns), :] = piece
    gain_grad[...] = jnp.sum(total, axis=1, keepdims=True)
    for start in range(0, FF, part):
        grad = dot_tn(hidden[:, start : start + part], cotangent_low)
        for j in range(4):
            planes[j, start : start + part, :] = grad[:, j * LANES : (j + 1) * LANES]
        planes[4, start : start + part, :HALF] = grad[:, 4 * LANES :]
    flatten_odd(planes, FF // 2, 4, flat, D * columns)
    owner_rows = weight_blocks.shape[1]
    half = one_kept.shape[0]
    middle = one_kept.shape[1]
    store_blocks(order_one, flat, one_sent, owner_rows, 0, half)
    store_blocks(order_two, flat, two_sent, owner_rows, middle, half)
    store_blocks(order_one, flat, one_kept, owner_rows, 0, 0)
    store_blocks(order_two, flat, two_kept, owner_rows, middle, 0)


def feedforward(orders, weight_blocks, residual, cotangent, gains):
    shape = jax.ShapeDtypeStruct
    count, owner_rows, unused = weight_blocks.shape
    middle = owner_rows // 32 * 16
    one = shape((count // 2, middle, LANES), BF16)
    two = shape((count // 2, owner_rows - middle, LANES), BF16)
    tokens = residual.shape[0] * residual.shape[1]
    rows = weight_blocks.shape[0] * weight_blocks.shape[1]
    return pl.pallas_call(
        feedforward_kernel,
        out_shape=(
            shape((MICRO, D, DEVICE_TOKENS), BF16),
            shape((tokens, D), BF16),
            shape((MICRO, D, DEVICE_TOKENS), F32),
            one,
            one,
            two,
            two,
            shape((D, 1), F32),
        ),
        in_specs=[smem()] * 3 + vmem(4),
        out_specs=tuple(vmem(8)),
        scratch_shapes=[
            pltpu.VMEM((rows, LANES), F32),
            pltpu.VMEM((5, FF, LANES), F32),
            pltpu.VMEM((D, 2 * FF), BF16),
            pltpu.VMEM((FF, D), BF16),
            pltpu.VMEM((tokens, FF), BF16),
            pltpu.VMEM((tokens, 2 * FF), BF16),
        ],
        compiler_params=params(),
    )(*orders, weight_blocks, residual, cotangent, gains)


def attention_backward_body(
    w_output,
    normed,
    queries,
    keys_across,
    keys,
    values,
    log_totals,
    mixed_across,
    d_branch,
    cosines,
    sines,
    bias,
    d_queries,
    d_window,
    query_grad,
    window_grad,
    output_grad,
    d_window_across,
    d_mixed,
):
    blocks = d_window.shape[0]
    cosine, sine = cosines[...], sines[...]
    own_cosine, own_sine = cosine[:, :DEVICE_TOKENS], sine[:, :DEVICE_TOKENS]
    d_mixed[...] = dot_nt(w_output[...], d_branch[...]).astype(BF16)

    def one(group, unused):
        group_rows = pl.ds(pl.multiple_of(group * HEAD_SIZE, HEAD_SIZE), HEAD_SIZE)
        value_rows = pl.ds(pl.multiple_of(KV_WIDTH + group * HEAD_SIZE, HEAD_SIZE), HEAD_SIZE)
        query = three(queries, group) * SCALE
        d_heads = three(d_mixed, group)
        delta = jnp.sum(d_heads.astype(F32) * three(mixed_across, group), axis=0, keepdims=True)
        log_total = jnp.concatenate(
            [log_totals[pl.ds(group * GROUP + offset, 1), :] for offset in range(GROUP)], 1
        )
        bias_three = jnp.concatenate([bias[...]] * GROUP, 1)
        probability = jnp.exp(dot(keys[group], query) + bias_three - log_total)
        d_probs = dot(values[group], d_heads)
        d_scores = (probability * (d_probs - delta)).astype(BF16)
        d_query = dot(keys_across[group_rows, :], d_scores) * SCALE
        for offset in range(GROUP):
            lanes = slice(offset * DEVICE_TOKENS, (offset + 1) * DEVICE_TOKENS)
            start = pl.multiple_of((group * GROUP + offset) * HEAD_SIZE, HEAD_SIZE)
            d_queries[pl.ds(start, HEAD_SIZE), :] = rotated(
                d_query[:, lanes], own_cosine, -own_sine
            ).astype(BF16)
        d_key = dot_nt(query, d_scores)
        d_value = dot_nt(d_heads, probability.astype(BF16))
        d_window_across[group_rows, :] = rotated(d_key, cosine, -sine).astype(BF16)
        d_window_across[value_rows, :] = d_value.astype(BF16)
        return unused

    lax.fori_loop(0, KEY_VALUE_HEADS, one, 0)
    for block in range(blocks):
        d_window[block] = d_window_across[
            :, block * DEVICE_TOKENS : (block + 1) * DEVICE_TOKENS
        ]
    query_grad[...] = dot_nt(normed[:, :DEVICE_TOKENS], d_queries[...])
    window_grad[...] = dot_nt(normed[...], d_window_across[...])
    output_grad[...] = dot(mixed_across[...].astype(BF16), d_branch[...])


def micro_views(micro, operands):
    w_output, *views = operands
    views = [view.at[micro] for view in views]
    views[7] = operands[8].at[micro * DEVICE_TOKENS : (micro + 1) * DEVICE_TOKENS, :]
    return (w_output, *views)


def attention_backward_first(*refs):
    attention_backward_body(*micro_views(0, refs[:12]), *refs[12:])


def attention_backward_second(order, w_project, *refs):
    first_queries, first_window, *first_grads = refs[:5]
    operands, refs = refs[5:17], refs[17:]
    kept, sent, d_queries, window_kept, window_sent, gain_grad, flat, planes = refs[:8]
    across, d_mixed, own_window, query_grad, window_grad, output_grad = refs[8:]
    attention_backward_body(
        *micro_views(1, operands),
        d_queries.at[1],
        own_window,
        query_grad,
        window_grad,
        output_grad,
        across,
        d_mixed,
    )
    d_queries[0] = first_queries[...]
    early = window_kept.shape[0]
    for block in range(own_window.shape[0]):
        target, place = (window_kept, block) if block < early else (window_sent, block - early)
        target[place, 0] = first_window[block]
        target[place, 1] = own_window[block]
    for sums, first in zip((query_grad, window_grad, output_grad), first_grads):
        sums[...] += first[...]
    total = jnp.zeros((D, LANES), F32)
    later = [window_grad[:, j * LANES : (j + 1) * LANES] for j in range(3)]
    for j in range(7):
        if j < 4:
            piece = query_grad[:, j * LANES : (j + 1) * LANES]
        elif j == 4:
            piece = jnp.concatenate([query_grad[:, j * LANES :], later[0][:, :HALF]], 1)
        else:
            piece = shift_half(later[j - 4], later[j - 5])
        planes[j] = piece
        total = total + piece * w_project[:, j * LANES : (j + 1) * LANES].astype(F32)
    planes[7] = pltpu.roll(later[2], HALF, 1)
    last_sum = planes[7, :, :HALF] * w_project[:, 7 * LANES :].astype(F32)
    gain_grad[...] = jnp.sum(total, axis=1, keepdims=True) + jnp.sum(
        last_sum, axis=1, keepdims=True
    )
    flatten_odd(planes, D // 2, 7, flat, 0)
    for j in range(4):
        planes[j] = output_grad[:, j * LANES : (j + 1) * LANES]
    planes[4, :, :HALF] = output_grad[:, 4 * LANES :]
    flatten_odd(planes, QUERY_WIDTH // 2, 4, flat, D * QKV_WIDTH // LANES)
    store_blocks(order, flat, sent, sent.shape[1], 0, sent.shape[0])
    store_blocks(order, flat, kept, kept.shape[1], 0, 0)


def attention_backward(operands, count, rows, final=()):
    shape = jax.ShapeDtypeStruct
    window = operands[1].shape[2]
    blocks = window // DEVICE_TOKENS
    sums = [(D, QUERY_WIDTH), (D, 2 * KV_WIDTH), (QUERY_WIDTH, D)]
    scratch = [
        pltpu.VMEM((2 * KV_WIDTH, window), BF16),
        pltpu.VMEM((QUERY_WIDTH, DEVICE_TOKENS), BF16),
    ]
    if final:
        kernel = attention_backward_second
        half = shape((count // 2, rows, LANES), BF16)
        late = blocks // 2
        one_block = (MICRO, 2 * KV_WIDTH, DEVICE_TOKENS)
        outputs = (
            half,
            half,
            shape((MICRO, QUERY_WIDTH, DEVICE_TOKENS), BF16),
            shape((blocks - late, *one_block), BF16),
            shape((late, *one_block), BF16),
            shape((D, 1), F32),
        )
        scratch = [
            pltpu.VMEM((count * rows, LANES), F32),
            pltpu.VMEM((8, D, LANES), F32),
            *scratch,
            pltpu.VMEM((blocks, 2 * KV_WIDTH, DEVICE_TOKENS), BF16),
            *[pltpu.VMEM(dims, F32) for dims in sums],
        ]
        in_specs = [smem()] + vmem(len(final) - 1 + len(operands))
    else:
        kernel = attention_backward_first
        outputs = (
            shape((QUERY_WIDTH, DEVICE_TOKENS), BF16),
            shape((blocks, 2 * KV_WIDTH, DEVICE_TOKENS), BF16),
            *[shape(dims, F32) for dims in sums],
        )
        in_specs = vmem(len(operands))
    return pl.pallas_call(
        kernel,
        out_shape=outputs,
        in_specs=in_specs,
        out_specs=tuple(vmem(len(outputs))),
        scratch_shapes=scratch,
        compiler_params=params(),
    )(*final, *operands)


def adam_update(weights, moment, square, grad, rate, decay):
    new_moment = BETA_ONE * moment + (1.0 - BETA_ONE) * grad
    new_square = BETA_TWO * square + (1.0 - BETA_TWO) * grad * grad
    mean_hat = new_moment / (1.0 - BETA_ONE**STEP)
    square_hat = new_square / (1.0 - BETA_TWO**STEP)
    new_weights = weights - rate * (
        mean_hat / (jnp.sqrt(square_hat) + ADAM_EPSILON) + decay * weights
    )
    return (new_weights, new_moment, new_square)


def first_of(lengths, index):
    starts = jnp.cumsum(lengths, axis=-1) - lengths
    return jnp.max(
        jnp.where(starts[:, None, :] <= index[None, :, None], starts[:, None, :], 0), axis=-1
    )


def on_device(
    block_input,
    out_grad,
    doc_lengths,
    attention_weights,
    feedforward_weights,
    norm_gains,
    attention_moment,
    attention_square,
    feedforward_moment,
    feedforward_square,
    gain_moment,
    gain_square,
):
    both = ("dp", "seq")
    seq_count = lax.axis_size("seq")
    owner_count = lax.axis_size(both)
    seq_place = lax.axis_index("seq")
    owner_place = lax.axis_index(both)
    attention_length = attention_weights.shape[0]
    feedforward_length = feedforward_weights.shape[0]
    reach = min((DOC_MAX + DEVICE_TOKENS - 2) // DEVICE_TOKENS, seq_count - 1)
    dp_count = lax.axis_size("dp")
    butterfly = (
        seq_count == 8
        and reach == seq_count - 1
        and dp_count == 4
        and attention_length % (8 * LANES) == 0
    )
    pair = (0, 1)
    line = range(0, seq_count, 2)
    square = range(0, owner_count, seq_count)
    order = [c ^ r ^ s for c in pair for r in square for s in line]
    window_line = (0, 4, 2, 6)
    across_x, across_y = (0, seq_count), (0, 2 * seq_count)
    paths = [
        [c ^ one ^ two ^ s for c in pair for one in first for two in second for s in window_line]
        for first, second in ((across_x, across_y), (across_y, across_x))
    ]

    own_inputs = jnp.swapaxes(block_input[:, 0], 1, 2)
    straight = jnp.arange(BLOCKS, dtype=jnp.int32)
    tiled_rows = feedforward_length % (8 * LANES) == 0
    feedforward_low = feedforward_weights.astype(BF16)
    if tiled_rows:
        feedforward_low = feedforward_low.reshape(-1, LANES)
    feedforward_blocks = lax.all_gather(feedforward_low, both, axis=0, tiled=True)
    feedforward_blocks = feedforward_blocks.reshape(BLOCKS, -1, LANES)

    if butterfly:
        window_blocks = seq_place ^ jnp.array([c ^ s for c in pair for s in window_line], jnp.int32)
    else:
        window_blocks = seq_place - jnp.arange(reach + 1, dtype=jnp.int32)
    token = jnp.arange(DEVICE_TOKENS, dtype=jnp.int32)
    query_index = seq_place * DEVICE_TOKENS + token
    key_index = (window_blocks[:, None] * DEVICE_TOKENS + token[None, :]).reshape(-1)
    lengths = doc_lengths[:, 0]
    first_query = first_of(lengths, query_index)
    first_key = first_of(lengths, key_index)
    half_width = HEAD_SIZE // 2
    inverse = THETA ** (-(jnp.arange(half_width, dtype=F32) * 2.0) / HEAD_SIZE)
    position = (key_index[None] - first_key).astype(F32)
    angles = position[:, None, :] * inverse[None, :, None]
    cosines, sines = jnp.cos(angles), jnp.sin(angles)
    allowed = (key_index[None, :, None] >= first_query[:, None, :]) & (
        key_index[None, :, None] <= query_index[None, None, :]
    )
    bias = jnp.where(allowed, 0.0, -jnp.inf).astype(F32)

    attention_low = attention_weights.astype(BF16)
    if butterfly:
        orders = [jnp.array(path, jnp.int32) ^ owner_place for path in (order, *paths)]
        weights = attention_low.reshape(1, attention_length // LANES, LANES)
        window_inputs = own_inputs[None]
        inputs_far = exchange(window_inputs, "seq", 4, 1)
        far, cosines, sines, bias = together(exchange(weights, "seq", 2), cosines, sines, bias)
        weights = jnp.concatenate([weights, far], 0)
        weights = jnp.concatenate([weights, exchange(weights, "seq", 4)], 0)
        window_inputs = jnp.concatenate([window_inputs, inputs_far], 0)
        weights, window_inputs = together(weights, window_inputs)
        inputs_far = exchange(window_inputs, "seq", 2)
        weights = jnp.concatenate([weights, exchange(weights, "dp", 1)], 0)
        weight_pieces = [weights, exchange(weights, "dp", 2)]
        weight_pieces += [exchange(piece, "seq", 1) for piece in weight_pieces]
        input_pieces = [window_inputs, inputs_far]
        input_pieces += [exchange(piece, "seq", 1) for piece in input_pieces]
    else:
        weights = lax.all_gather(attention_low, both, axis=0, tiled=True)
        weights = weights.reshape(BLOCKS, -1, LANES)
        weight_pieces = jnp.split(weights, 4)
        window_inputs = jnp.stack(
            [own_inputs]
            + [
                lax.ppermute(
                    own_inputs, "seq", [(p, p + step) for p in range(seq_count - step)]
                )
                for step in range(1, reach + 1)
            ],
            0,
        )
        quarter = (reach + 1) // 4
        cuts = [0, quarter, 2 * quarter, 3 * quarter, reach + 1]
        input_pieces = [window_inputs[a:b] for a, b in zip(cuts, cuts[1:])]
        orders = [straight] * 3

    (
        w_project,
        w_output,
        normed_one,
        queries,
        keys_across,
        keys,
        values,
        log_totals,
        mixed_across,
        residual,
    ) = attention_forward(
        orders[0], weight_pieces, input_pieces, cosines, sines, bias, norm_gains[0][:, None]
    )
    block_output, d_branch, d_residual, *parts, gain_two = feedforward(
        (straight, *orders[1:]),
        feedforward_blocks,
        residual,
        jnp.swapaxes(out_grad[:, 0], 1, 2),
        norm_gains[1:2],
    )
    operands = (
        w_output,
        normed_one,
        queries,
        keys_across,
        keys,
        values,
        log_totals,
        mixed_across,
        d_branch,
        cosines,
        sines,
        bias,
    )
    attention_rows = D * (QKV_WIDTH + QUERY_WIDTH) // (LANES * BLOCKS)
    if butterfly:
        one_kept, one_sent, two_kept, two_sent = parts
        one_new, two_new = exchange(one_sent, "seq", 1), exchange(two_sent, "seq", 1)
        first = attention_backward(operands, BLOCKS, attention_rows)
        one_new, two_new, *first = together(one_new, two_new, *first)
        one_kept, one_sent = add_up(one_kept, [one_new], 2)
        two_kept, two_sent = add_up(two_kept, [two_new], 2)
        one_sent, two_sent, *first = together(one_sent, two_sent, *first)
        one_new, two_new = exchange(one_sent, "dp", 1), exchange(two_sent, "dp", 2)
        second = attention_backward(
            operands, BLOCKS, attention_rows, (orders[0], w_project, *first)
        )
        one_new, two_new, *second = together(one_new, two_new, *second)
        kept, sent, d_queries, window_kept, window_sent, gain_one = second
        one_kept, one_sent = add_up(one_kept, [one_new], 2)
        two_kept, two_sent = add_up(two_kept, [two_new], 2)
        gains_total = jnp.stack([gain_one[:, 0], gain_two[:, 0]], 0) / norm_gains

        new, one_new, two_new, window_new, gains_new = together(
            exchange(sent, "seq", 1),
            exchange(one_sent, "dp", 2),
            exchange(two_sent, "dp", 1),
            exchange(window_sent, "seq", 1),
            exchange(gains_total, "seq", 1),
        )
        kept, sent = add_up(kept, [new], 2)
        one_kept, one_sent = add_up(one_kept, [one_new], 2)
        two_kept, two_sent = add_up(two_kept, [two_new], 2)
        window_kept, window_sent = add_up(window_kept, [window_new], 2)
        gains_total = gains_total + gains_new

        new, one_new, two_new, window_new, gains_new = together(
            exchange(sent, "dp", 2),
            exchange(one_sent, "seq", 2),
            exchange(two_sent, "seq", 2),
            exchange(window_sent, "seq", 2),
            exchange(gains_total, "dp", 2),
        )
        kept, sent = add_up(kept, [new], 2)
        one_kept, one_sent = add_up(one_kept, [one_new], 2)
        two_kept, two_sent = add_up(two_kept, [two_new], 2)
        window_kept, window_sent = add_up(window_kept, [window_new], 2)
        gains_total = gains_total + gains_new

        new, one_new, two_new, window_new, gains_new = together(
            exchange(sent, "dp", 1),
            exchange(one_sent, "seq", 4),
            exchange(two_sent, "seq", 4),
            exchange(window_sent, "seq", 4),
            exchange(gains_total, "dp", 1),
        )
        kept, *sent = add_up(kept, [new], len(line))
        gains_total = gains_total + gains_new

        news = [exchange(part, "seq", place) for place, part in zip(line[1:], sent)]
        gains_new = exchange(gains_total, "seq", 2)
        gains_new, one_new, two_new, window_new = together(
            gains_new, one_new, two_new, window_new
        )
        gains_total = gains_total + gains_new
        gains_total = gains_total + exchange(gains_total, "seq", 4)
        feedforward_owned = jnp.concatenate(
            [add_up(one_kept, [one_new], 1)[0][0], add_up(two_kept, [two_new], 1)[0][0]], 0
        ).reshape(-1)
        d_own = add_up(window_kept, [window_new], 1)[0][0].astype(BF16)
        attention_owned = add_up(kept, news, 1)[0].reshape(-1)
    else:
        halves = [jnp.concatenate(parts[index : index + 2], 0) for index in (0, 2)]
        grads = jnp.concatenate(halves, 1).reshape(-1)
        feedforward_owned = lax.psum_scatter(grads, both, scatter_dimension=0, tiled=True)
        first = attention_backward(operands, BLOCKS, attention_rows)
        kept, sent, d_queries, window_kept, window_sent, gain_one = attention_backward(
            operands, BLOCKS, attention_rows, (orders[0], w_project, *first)
        )
        attention_owned = lax.psum_scatter(
            jnp.concatenate([kept, sent], 0).reshape(-1), both, scatter_dimension=0, tiled=True
        )
        d_window = jnp.concatenate([window_kept, window_sent], 0)
        d_own = d_window[0].astype(F32)
        for step in range(1, reach + 1):
            d_own = d_own + lax.ppermute(
                d_window[step], "seq", [(p, p - step) for p in range(step, seq_count)]
            ).astype(F32)
        d_own = d_own.astype(BF16)
        gains_total = jnp.stack([gain_one[:, 0], gain_two[:, 0]], 0) / norm_gains
        gains_total = lax.psum(gains_total, both)
    d_normed_one = matmul("de,met->mdt", w_project, jnp.concatenate([d_queries, d_own], 1))
    unit_one, inverse_one = unit_norm(own_inputs.astype(F32))
    input_grad = d_residual + norm_backward(
        d_normed_one, unit_one, inverse_one, norm_gains[0][None, :, None]
    )

    attention_place = owner_place * attention_length + jnp.arange(attention_length, dtype=jnp.int32)
    attention_rate = jnp.where(
        attention_place < D * QKV_WIDTH, RATE_FACTOR * D ** (-0.5), RATE_FACTOR * OUT_FAN ** (-0.5)
    )
    feedforward_place = owner_place * feedforward_length + jnp.arange(
        feedforward_length, dtype=jnp.int32
    )
    feedforward_rate = jnp.where(
        feedforward_place < 2 * D * FF, RATE_FACTOR * D ** (-0.5), RATE_FACTOR * FF ** (-0.5)
    )
    new_attention = adam_update(
        attention_weights,
        attention_moment,
        attention_square,
        attention_owned.astype(F32),
        attention_rate,
        MATRIX_DECAY,
    )
    new_feedforward = adam_update(
        feedforward_weights,
        feedforward_moment,
        feedforward_square,
        feedforward_owned.astype(F32),
        feedforward_rate,
        MATRIX_DECAY,
    )
    new_gains = adam_update(norm_gains, gain_moment, gain_square, gains_total, GAIN_RATE, 0.0)
    return (
        jnp.swapaxes(block_output, 1, 2)[:, None],
        jnp.swapaxes(input_grad, 1, 2)[:, None],
        *new_attention,
        *new_feedforward,
        *new_gains,
    )


def solution(mesh):
    tokens = P(None, "dp", "seq", None)
    flat = P(("dp", "seq"))
    return jax.shard_map(
        on_device,
        mesh=mesh,
        in_specs=(
            tokens,
            tokens,
            P(None, "dp", None),
            flat,
            flat,
            P(),
            flat,
            flat,
            flat,
            flat,
            P(),
            P(),
        ),
        out_specs=(tokens, tokens, flat, flat, flat, flat, flat, flat, P(), P(), P()),
        check_vma=False,
    )
```
